32 devices in a mesh: dp: 2 (over x), expert: 16 (over z, y, core).
Axes of the slice: x: 2, y: 2, z: 4, core: 2. Of those that a mesh axis runs over, the one named last changes fastest.
Arguments:
- tokens: bfloat16 [4096, 1536], P(('dp', 'expert')), may hold values from -6 to 6
- cotangent: bfloat16 [4096, 1536], P(('dp', 'expert')), may hold values from -6 to 6
- lengths: int32 [32, 5], P(('dp', 'expert')), may hold values from 1 to 64, 128 in all within a row
- routes: int32 [4096, 8], P(('dp', 'expert')), may hold values from 0 to 15, all different within a row; in each aligned block of 128 rows (0 to 127, 128 to 255, ...) at most 80 rows name the same one
- gain_attn: float32 [1536], P('dp'), may hold values from 0.5 to 1.5
- w_query: float32 [1536, 1536], P('dp'), may hold values from -0.5 to 0.5
- key_weight: float32 [1536, 512], P('dp'), may hold values from -0.5 to 0.5
- value_weight: float32 [1536, 512], P('dp'), may hold values from -0.15625 to 0.15625
- w_out: float32 [1536, 1536], P('dp'), may hold values from -0.75 to 0.75
- gain_moe: float32 [1536], P('dp'), may hold values from 0.5 to 1.5
- w_router: float32 [1536, 16], P('dp'), may hold values from -0.078125 to 0.078125
- w_gate: float32 [16, 1536, 512], P('expert', 'dp'), may hold values from -0.15625 to 0.15625
- w_up: float32 [16, 1536, 512], P('expert', 'dp'), may hold values from -0.15625 to 0.15625
- w_down: float32 [16, 512, 1536], P('expert', 'dp'), may hold values from -1 to 1
Outputs:
- mixed: bfloat16 [4096, 1536], P(('dp', 'expert'))
- d_tokens: float32 [4096, 1536], P(('dp', 'expert'))
- d_gain_attn: float32 [1536], P('dp')
- d_w_query: float32 [1536, 1536], P('dp')
- d_w_key: float32 [1536, 512], P('dp')
- d_w_value: float32 [1536, 512], P('dp')
- d_w_out: float32 [1536, 1536], P('dp')
- d_gain_moe: float32 [1536], P('dp')
- d_w_router: float32 [1536, 16], P('dp')
- d_w_gate: float32 [16, 1536, 512], P('expert', 'dp')
- d_w_up: float32 [16, 1536, 512], P('expert', 'dp')
- d_w_down: float32 [16, 512, 1536], P('expert', 'dp')
The draws below stay inside these ranges and needn't reach their ends.
Inputs may be any that keep to these rules, and one draw needn't show every extreme that they name: In each row the first 4 entries are the lengths of a sequence's documents in order and the last is the padding at its end; each row sums to 128 and its largest entry is 64. `routes`: each row names 8 different experts. In each aligned block of 128 rows (one sequence) no expert is named more than 80 times, and in some blocks an expert is named exactly 80 times.
All inputs are finite; a program needn't handle non-finite values.
Results may differ from the reference program's by a relative error of at most 0.02.
The reference program's roundings to bfloat16 on the way count: a program that leaves them out, or rounds other values in their place, can miss the bound.
Values may be sent and summed in bfloat16 or wider, within the bound.
No kernel may reach another device: no remote copies, remote signals or barrier semaphores. Data moves between devices by JAX's collectives and lax.ppermute only.
A program may use at most 192 MiB of HBM per device.

```python
import math
import jax
import jax.numpy as jnp
import numpy as np
from jax import lax

MODEL_DIMENSION = 1536
QUERY_HEADS = 24
KEY_VALUE_HEADS = 8
HEAD_DIMENSION = 64
FFE = 512
TOP = 8
TOKENS_PER_PART = 128
PIECES = 5
EXPERTS = 16
CAP = 80
SEQS = 32
TOKENS = 4096


def shard_levels(rng, dims, shards, smallest, top_value):
    def one(position, blocks):
        steps = jax.random.uniform(jax.random.fold_in(jax.random.fold_in(rng, 6), position), (blocks,), jnp.float32, smallest / len(shards), top_value / len(shards))
        return jnp.repeat(jnp.exp(steps), dims[position] // blocks).reshape((-1,) + (1,) * (len(dims) - position - 1))

    factor_of = one(*shards[0])
    for cut in shards[1:]:
        factor_of = factor_of * one(*cut)
    return factor_of


def profile(number_of, total, reach, slope):
    weights = [(1 << 20) // math.isqrt(standing ** slope) + 1 for standing in range(2, number_of + 1)]
    rest, counts = total - reach - (number_of - 1), [1] * (number_of - 1)
    while rest > 0:
        free = [i for i in range(number_of - 1) if counts[i] < reach]
        whole, remaining = sum([weights[i] for i in free]), rest
        for i in free:
            more = min(reach - counts[i], max(1, remaining * weights[i] // whole), rest)
            counts[i] = counts[i] + more
            rest = rest - more
    return np.array([reach] + counts)


def uneven(rng, number_of, total, bound, skew):
    if number_of == 2:
        one = jax.random.randint(rng, (), max(1, total - bound), min(bound, total - 1) + 1)
        return jnp.stack([one, total - one])
    sizes = jnp.asarray(profile(number_of, total, bound, skew), jnp.int32)
    twos = (number_of - 1) // 2
    giver, taker = sizes[1:1 + 2 * twos:2], sizes[2:2 + 2 * twos:2]
    margin = jnp.minimum(giver - 1, bound - taker)
    shifted = jax.random.randint(jax.random.fold_in(rng, 1), (twos,), 0, 1 << 20) % (margin + 1)
    sizes = sizes.at[1:1 + 2 * twos:2].set(giver - shifted).at[2:2 + 2 * twos:2].set(taker + shifted)
    return sizes[jax.random.permutation(jax.random.fold_in(rng, 2), number_of)]


def deal_out(key, own, number, rows, number_of, top, bound, slope):
    order = jax.random.permutation(key, number_of)
    heavy_load, common = shares(number_of, rows * top, bound, slope, True), shares(number_of, rows * top, bound, slope, False)
    places = jnp.arange(number_of)

    def named(tallies, rotation):
        used = int((tallies > 0).sum())
        fixed = max(1, used // 4)
        shifted = fixed + (places - fixed + rotation * (used - fixed)) % max(1, number_of - fixed)
        return jnp.zeros((number_of,), jnp.int32).at[order[jnp.where(places < fixed, places, shifted)]].set(jnp.asarray(tallies, jnp.int32))

    tallies = jnp.where(number % 4 == 0, named(heavy_load, number // 4), named(common, number - number // 4 - 1))
    mixed = jax.random.permutation(jax.random.fold_in(own, 3), number_of)
    giver, sink = mixed[0:number_of // 2 * 2:2], mixed[1:number_of // 2 * 2:2]
    slack = jnp.minimum(tallies[giver] - 1, bound - tallies[sink]) // 2
    slack = jnp.where((giver == order[0]) | (sink == order[0]) | (tallies[sink] == 0), 0, jnp.maximum(slack, 0))
    shifted = jax.random.randint(jax.random.fold_in(own, 4), (number_of // 2,), 0, 1 << 20) % (slack + 1)
    tallies = tallies.at[giver].add(-shifted).at[sink].add(shifted)
    items = jnp.searchsorted(jnp.cumsum(tallies), jnp.arange(rows * top), side="right").astype(jnp.int32)
    listing = items.reshape(top, rows).T
    listing = listing[jax.random.permutation(jax.random.fold_in(own, 1), rows)]
    rotation = jax.random.randint(jax.random.fold_in(own, 2), (rows, 1), 0, top)
    return jnp.take_along_axis(listing, (jnp.arange(top)[None, :] + rotation) % top, axis=1)


def shares(count, total, reach, slope, full):
    portions = [(1 << 20) // math.isqrt(grade ** slope) + 1 for grade in range(1, count + 1)]
    largest = reach if full else min(reach, max(-(-total // count), total * portions[0] // sum(portions)))
    least = 1 if total - largest >= count - 1 else 0
    counts, spare = [largest] + [least] * (count - 1), total - largest - least * (count - 1)
    while spare > 0:
        candidates = [i for i in range(1, count) if counts[i] < largest] or [i for i in range(1, count) if counts[i] < reach]
        pool, remaining = sum([portions[i] for i in candidates]), spare
        for i in candidates:
            addition = min(reach - counts[i], max(1, remaining * portions[i] // pool), spare)
            counts[i] = counts[i] + addition
            spare = spare - addition
    return np.array(counts)


def scatter_about(key, dims, spread, most, shards=(), held_as=jnp.bfloat16):
    factor_of = shard_levels(key, dims, shards, -0.22, 0.18) if shards else 1.0
    array = jax.random.normal(key, dims, jnp.float32) * spread * factor_of
    return jnp.minimum(jnp.maximum(array, -most), most).astype(held_as)


def setup_inputs(seed: int = 0) -> dict:
    key_list = jax.random.split(jax.random.key(seed), 15)
    tokens = scatter_about(key_list[0], (TOKENS, MODEL_DIMENSION), 1.0, 6.0, ((0, 32),))
    cotangent = scatter_about(key_list[1], (TOKENS, MODEL_DIMENSION), 1.0, 6.0, ((0, 32),))
    lengths = jax.vmap(lambda own: uneven(own, PIECES, TOKENS_PER_PART, TOKENS_PER_PART // 2, 1))(jax.random.split(key_list[2], SEQS)).reshape((SEQS, PIECES)).astype(jnp.int32)
    routes_keys = jax.random.split(jax.random.fold_in(key_list[3], 1), TOKENS // TOKENS_PER_PART)
    routes_turns = jax.random.permutation(jax.random.fold_in(key_list[3], 3), TOKENS // TOKENS_PER_PART)
    routes = jax.vmap(lambda own, number: deal_out(jax.random.fold_in(key_list[3], 2), own, number, TOKENS_PER_PART, EXPERTS, TOP, CAP, 1))(routes_keys, routes_turns).reshape((TOKENS, TOP))
    gain_attn = jnp.clip(1.0 + 0.1 * jax.random.normal(key_list[4], (MODEL_DIMENSION,), jnp.float32), 0.5, 1.5)
    w_query = scatter_about(key_list[5], (MODEL_DIMENSION, QUERY_HEADS * HEAD_DIMENSION), (MODEL_DIMENSION // 12) ** -0.5, 0.5, ((0, 2),), jnp.float32)
    key_weight = scatter_about(key_list[6], (MODEL_DIMENSION, KEY_VALUE_HEADS * HEAD_DIMENSION), (MODEL_DIMENSION // 12) ** -0.5, 0.5, ((0, 2),), jnp.float32)
    value_weight = scatter_about(key_list[7], (MODEL_DIMENSION, KEY_VALUE_HEADS * HEAD_DIMENSION), MODEL_DIMENSION ** -0.5, 0.15625, ((0, 2),), jnp.float32)
    w_out = scatter_about(key_list[8], (QUERY_HEADS * HEAD_DIMENSION, MODEL_DIMENSION), (QUERY_HEADS * HEAD_DIMENSION // 24) ** -0.5, 0.75, ((0, 2),), jnp.float32)
    gain_moe = jnp.clip(1.0 + 0.1 * jax.random.normal(key_list[9], (MODEL_DIMENSION,), jnp.float32), 0.5, 1.5)
    w_router = scatter_about(key_list[10], (MODEL_DIMENSION, EXPERTS), (4 * MODEL_DIMENSION) ** -0.5, 0.078125, ((0, 2),), jnp.float32)
    w_gate = scatter_about(key_list[11], (EXPERTS, MODEL_DIMENSION, FFE), MODEL_DIMENSION ** -0.5, 0.15625, ((0, 16), (1, 2)), jnp.float32)
    w_up = scatter_about(key_list[12], (EXPERTS, MODEL_DIMENSION, FFE), MODEL_DIMENSION ** -0.5, 0.15625, ((0, 16), (1, 2)), jnp.float32)
    w_down = scatter_about(key_list[13], (EXPERTS, FFE, MODEL_DIMENSION), (FFE // 16) ** -0.5, 1.0, ((0, 16), (1, 2)), jnp.float32)
    return {"tokens": tokens, "cotangent": cotangent, "lengths": lengths, "routes": routes, "gain_attn": gain_attn, "w_query": w_query, "key_weight": key_weight, "value_weight": value_weight, "w_out": w_out, "gain_moe": gain_moe, "w_router": w_router, "w_gate": w_gate, "w_up": w_up, "w_down": w_down}


@jax.custom_vjp
def reduced_precision(v):
    return lax.optimization_barrier(v.astype(jnp.bfloat16)).astype(jnp.float32)

@jax.custom_vjp
def low_back(v):
    return v

def low_keep(v):
    return (reduced_precision(v), None)

def low_pass(kept, grad):
    return (grad,)

def back_keep(v):
    return (v, None)

def back_low(kept, grad):
    return (reduced_precision(grad),)
reduced_precision.defvjp(low_keep, low_pass)
low_back.defvjp(back_keep, back_low)
norm_eps = 1e-06
score_scale = 0.015625
rope_base = 10000.0
mask_fill = -1e+30

def highest(form, left, right):
    return jnp.einsum(form, left, right, precision=lax.Precision.HIGHEST)

def apply_rotary(field_in, places, head_count):
    half_dim = HEAD_DIMENSION // 2
    inverse = rope_base ** (-jnp.arange(half_dim, dtype=jnp.float32) * 2.0 / HEAD_DIMENSION)
    angles = places.astype(jnp.float32)[:, None] * inverse[None, :]
    cosine = jnp.cos(angles)[:, None, :]
    sine_t = jnp.sin(angles)[:, None, :]
    shaped = field_in.reshape(field_in.shape[0], head_count, HEAD_DIMENSION)
    first_half = shaped[..., :half_dim]
    second = shaped[..., half_dim:]
    turned = jnp.concatenate([first_half * cosine - second * sine_t, second * cosine + first_half * sine_t], -1)
    return turned.reshape(field_in.shape)

def layout(doc_lengths, length):
    pieces = doc_lengths.shape[0]
    doc_ends = jnp.cumsum(doc_lengths).astype(jnp.int32)
    starts = (doc_ends - doc_lengths).astype(jnp.int32)
    places = jnp.arange(length, dtype=jnp.int32)
    segment = lax.optimization_barrier(jnp.sum((places[:, None] >= doc_ends[None, :]).astype(jnp.int32), 1)).astype(jnp.int32)
    owned_by = segment[:, None] == jnp.arange(pieces, dtype=jnp.int32)[None, :]
    incoming_placement = (places - lax.optimization_barrier(jnp.sum(jnp.where(owned_by, starts[None, :], 0), 1))).astype(jnp.int32)
    live_rows = segment < pieces - 1
    allowed = (segment[:, None] == segment[None, :]) & (places[None, :] <= places[:, None]) & (live_rows[None, :] | (places[:, None] == places[None, :]))
    return (incoming_placement, live_rows, allowed)

def slot_table(route_ids, experts, capacity):
    flat_ids = route_ids.reshape(-1)
    hit_table = (flat_ids[:, None] == jnp.arange(experts, dtype=jnp.int32)[None, :]).astype(jnp.int32)
    rank_in = lax.optimization_barrier(jnp.sum((jnp.cumsum(hit_table, 0).astype(jnp.int32) - 1) * hit_table, 1)).astype(jnp.int32)
    return (flat_ids * capacity + rank_in).astype(jnp.int32).reshape(route_ids.shape)

def device_layer(params, stream, doc_lengths, route_ids):
    gain_one, query_w, key_w, value_w, out_w, gain_two, router_w, gate_w, up_w, down_w = [reduced_precision(master) for master in params]
    incoming_placement, live_rows, allowed = layout(doc_lengths, TOKENS_PER_PART)
    normed_one = reduced_precision(stream * lax.rsqrt(lax.optimization_barrier(jnp.mean(stream * stream, -1, keepdims=True)) + norm_eps) * gain_one)
    query_unrotated = low_back(highest('sd,df->sf', normed_one, query_w))
    key_unrotated = low_back(highest('sd,df->sf', normed_one, key_w))
    value_projected = low_back(highest('sd,df->sf', normed_one, value_w))
    query_matrix = reduced_precision(apply_rotary(query_unrotated, incoming_placement, QUERY_HEADS)).reshape(TOKENS_PER_PART, KEY_VALUE_HEADS, QUERY_HEADS // KEY_VALUE_HEADS, HEAD_DIMENSION)
    key_matrix = reduced_precision(apply_rotary(key_unrotated, incoming_placement, KEY_VALUE_HEADS)).reshape(TOKENS_PER_PART, KEY_VALUE_HEADS, HEAD_DIMENSION)
    value_matrix = reduced_precision(value_projected).reshape(TOKENS_PER_PART, KEY_VALUE_HEADS, HEAD_DIMENSION)
    scores = low_back(score_scale * highest('sngh,tnh->ngst', query_matrix, key_matrix))
    attention = jax.nn.softmax(jnp.where(allowed, scores, mask_fill), -1)
    context = highest('ngst,tnh->sngh', reduced_precision(attention), value_matrix).reshape(TOKENS_PER_PART, QUERY_HEADS * HEAD_DIMENSION)
    attended = reduced_precision(low_back(jnp.where(live_rows[:, None], context, 0.0)))
    stream_mid = stream + low_back(highest('sf,fd->sd', attended, out_w))
    normed_two = reduced_precision(stream_mid * lax.rsqrt(lax.optimization_barrier(jnp.mean(stream_mid * stream_mid, -1, keepdims=True)) + norm_eps) * gain_two)
    logits = low_back(highest('sd,de->se', normed_two, router_w))
    gate_weights = reduced_precision(jax.nn.softmax(jnp.take_along_axis(logits, route_ids, 1), -1))
    slot_ids = slot_table(route_ids, EXPERTS, CAP).reshape(-1)
    holder = jnp.full((EXPERTS * CAP,), -1, jnp.int32).at[slot_ids].set(jnp.arange(TOKENS_PER_PART * TOP, dtype=jnp.int32))
    expert_rows = jnp.where((holder >= 0)[:, None], normed_two[jnp.maximum(holder, 0) // TOP], 0.0)
    expert_rows = low_back(expert_rows).reshape(EXPERTS, CAP, MODEL_DIMENSION)
    gate_pre = low_back(highest('ecd,edf->ecf', expert_rows, gate_w))
    up_pre = low_back(highest('ecd,edf->ecf', expert_rows, up_w))
    hidden = reduced_precision(jax.nn.silu(gate_pre) * up_pre)
    result = reduced_precision(low_back(highest('ecf,efd->ecd', hidden, down_w))).reshape(EXPERTS * CAP, MODEL_DIMENSION)
    picked = result[slot_ids].reshape(TOKENS_PER_PART, TOP, MODEL_DIMENSION)
    return stream_mid + low_back(lax.optimization_barrier(jnp.sum(gate_weights[:, :, None] * picked, 1)))

def reference(tokens, cotangent, lengths, routes, gain_attn, w_query, key_weight, value_weight, w_out, gain_moe, w_router, w_gate, w_up, w_down):
    bundle = math.gcd(SEQS, max(1, 2048 // TOKENS_PER_PART))
    step_count = SEQS // bundle
    streams = tokens.astype(jnp.float32).reshape(step_count, bundle, TOKENS_PER_PART, MODEL_DIMENSION)
    doc_table = lengths.reshape(step_count, bundle, PIECES)
    route_table = routes.reshape(step_count, bundle, TOKENS_PER_PART, TOP)
    params = (gain_attn, w_query, key_weight, value_weight, w_out, gain_moe, w_router, w_gate, w_up, w_down)
    device_step = jax.checkpoint(jax.vmap(device_layer, in_axes=(None, 0, 0, 0)))

    def forward(params_in, streams_in):

        def advance(carry_in, item_in):
            return (carry_in, device_step(params_in, item_in[0], item_in[1], item_in[2]))
        return lax.scan(advance, jnp.zeros((), jnp.float32), (streams_in, doc_table, route_table))[1]
    layer_out, pullback = jax.vjp(forward, params, streams)
    weight_grads, input_grads = pullback(cotangent.astype(jnp.float32).reshape(layer_out.shape))
    return (layer_out.reshape(TOKENS, MODEL_DIMENSION).astype(jnp.bfloat16), input_grads.reshape(TOKENS, MODEL_DIMENSION), weight_grads[0], weight_grads[1], weight_grads[2], weight_grads[3], weight_grads[4], weight_grads[5], weight_grads[6], weight_grads[7], weight_grads[8], weight_grads[9])
```

```python
import jax
import jax.numpy as jnp
import numpy as np
from jax import lax
from jax.experimental import pallas as pl
from jax.experimental.pallas import tpu as pltpu
from jax.sharding import PartitionSpec as P

HEAD = 64
norm_eps = 1e-06
score_scale = 0.015625
rope_base = 10000.0
mask_fill = -1e30
BF = jnp.bfloat16
F32 = jnp.float32


def narrow(v):
    return v.astype(BF)


def wide(v):
    return v.astype(F32)


def mm(a, b):
    return jnp.dot(a, b, preferred_element_type=F32)


def mm_tn(a, b):
    return lax.dot_general(a, b, (((0,), (0,)), ((), ())), preferred_element_type=F32)


def mm_nt(a, b):
    return lax.dot_general(a, b, (((1,), (1,)), ((), ())), preferred_element_type=F32)


def add_low(a, b):
    return narrow(wide(a) + wide(b))


def rotary(v, places, heads, sign):
    half = HEAD // 2
    inverse = rope_base ** (-jnp.arange(half, dtype=F32) * 2.0 / HEAD)
    angles = places.astype(F32)[:, None] * inverse[None, :]
    cosine = jnp.cos(angles)[:, None, :]
    sine = sign * jnp.sin(angles)[:, None, :]
    s = v.reshape(v.shape[0], heads, HEAD)
    a, b = s[..., :half], s[..., half:]
    return jnp.concatenate([a * cosine - b * sine, b * cosine + a * sine], -1).reshape(v.shape)


def layout(lengths, length):
    pieces = lengths.shape[0]
    order = jnp.arange(pieces, dtype=jnp.int32)
    ends = jnp.sum(jnp.where(order[None, :] <= order[:, None], lengths[None, :], 0), 1)
    starts = ends - lengths
    at = jnp.arange(length, dtype=jnp.int32)
    segment = jnp.sum((at[:, None] >= ends[None, :]).astype(jnp.int32), 1)
    owned = segment[:, None] == order[None, :]
    places = at - jnp.sum(jnp.where(owned, starts[None, :], 0), 1)
    live = segment < pieces - 1
    allowed = (
        (segment[:, None] == segment[None, :])
        & (at[None, :] <= at[:, None])
        & (live[None, :] | (at[:, None] == at[None, :]))
    )
    return places, live, allowed


def put_rows(pair, at, widths):
    rows, per = pair[0].shape[0] * 2, pair[0].shape[0] * 2 // at.shape[0]
    c = at.shape[0] // 2
    total = sum(widths)
    cuts = [sum(widths[:i]) for i in range(len(widths) + 1)]
    if per % 16:
        out = jnp.zeros((rows, total), F32)
        for i in range(2 * c):
            blk = wide(pair[i // c][i % c * per : (i % c + 1) * per])
            out = lax.dynamic_update_slice_in_dim(out, blk, at[i] * per, 0)
        return [out[:, a:b] for a, b in zip(cuts, cuts[1:])]

    def body(at_ref, own, sib, *outs):
        def write(src):
            for ref, a, b in zip(outs, cuts, cuts[1:]):
                ref[...] = wide(src[:, a:b])

        @pl.when(pl.program_id(0) < c)
        def _():
            write(own)

        @pl.when(pl.program_id(0) >= c)
        def _():
            write(sib)

    return pl.pallas_call(
        body,
        grid_spec=pltpu.PrefetchScalarGridSpec(
            num_scalar_prefetch=1,
            grid=(2 * c,),
            in_specs=[
                pl.BlockSpec((per, total), lambda i, at: (jnp.minimum(i, c - 1), 0)),
                pl.BlockSpec((per, total), lambda i, at: (jnp.maximum(i - c, 0), 0)),
            ],
            out_specs=[pl.BlockSpec((per, w), lambda i, at: (at[i], 0)) for w in widths],
        ),
        out_shape=[jax.ShapeDtypeStruct((rows, w), F32) for w in widths],
        cost_estimate=pl.CostEstimate(
            flops=rows * total, bytes_accessed=rows * total * 6, transcendentals=0
        ),
        name="put_rows",
    )(at, *pair)


def expert_step(spots, rows, cots, weights, kept, start, total):
    gate_w, up_w, down_w, router = weights
    n, width = rows[0].shape
    ffe = gate_w.shape[1]
    tail = router.shape[0]
    block = cots.shape[0] // spots[1]
    steps = n // block
    two = 2 * block

    def body(spot, xa, xb, ca, cb, gw, uw, dw, rt, *refs):
        mix_a, mix_b, row_a, row_b, x_o, hid_o, gpg_o, upg_o, rg_o = refs[-9:]
        x = jnp.concatenate([xa[...], xb[...]])
        cm = jnp.concatenate([ca[...], cb[...]])
        cot, chosen = wide(cm[:, :width]), cm[:, width:] > 0
        x_o[...] = x
        logits = jnp.where(chosen, mm_nt(x, rt[...]), mask_fill)
        top = jnp.max(logits, -1, keepdims=True)
        raised = jnp.where(chosen, jnp.exp(logits - top), 0.0)
        mine = lax.broadcasted_iota(jnp.int32, raised.shape, 1)
        gate = jnp.sum(jnp.where(mine == spot[0], raised, 0.0), -1, keepdims=True)
        gate = wide(narrow(gate / jnp.sum(raised, -1, keepdims=True)))
        gate_pre, up_pre = mm(x, gw[...]), mm(x, uw[...])
        sg = jax.nn.sigmoid(gate_pre)
        silu = gate_pre * sg
        hidden = narrow(silu * up_pre)
        hid_o[...] = hidden
        result_grad = narrow(gate * cot)
        rg_o[...] = result_grad
        result = wide(narrow(mm(hidden, dw[...])))
        mix = narrow(gate * result)
        mix_a[...], mix_b[...] = mix[:block], mix[block:]
        gate_grad = jnp.sum(result * cot, -1, keepdims=True)
        hidden_grad = mm_nt(result_grad, dw[...])
        gpg = narrow(hidden_grad * up_pre * sg * (1.0 + gate_pre * (1.0 - sg)))
        upg = narrow(hidden_grad * silu)
        gpg_o[...], upg_o[...] = gpg, upg
        row = narrow(mm_nt(gpg, gw[...]) + mm_nt(upg, uw[...]))
        row_a[:, :width], row_b[:, :width] = row[:block], row[block:]
        high = wide(narrow(gate_grad))
        ends = jnp.where(mine == spot[0], high, 0.0)
        ends = narrow(jnp.where(mine == spot[0] + tail // 2, gate_grad - high, ends))
        row_a[:, width:], row_b[:, width:] = ends[:block], ends[block:]

    whole = lambda a: pl.BlockSpec(a.shape, lambda i, s: (0, 0))
    step = lambda w: pl.BlockSpec((block, w), lambda i, s: (i, 0))
    keep = lambda w: pl.BlockSpec((two, w), lambda i, s: (start + i, 0))
    widths = [width, ffe, ffe, ffe, width]
    out_shape = [jax.ShapeDtypeStruct((n, w), BF) for w in (width, width, width + tail, width + tail)]
    out_shape += [jax.ShapeDtypeStruct((total, w), BF) for w in widths]
    given = list(kept or ())
    return pl.pallas_call(
        body,
        grid_spec=pltpu.PrefetchScalarGridSpec(
            num_scalar_prefetch=1,
            grid=(steps,),
            in_specs=[
                step(width),
                step(width),
                pl.BlockSpec((block, width + tail), lambda i, s: (s[1 + i], 0)),
                pl.BlockSpec((block, width + tail), lambda i, s: (s[1 + steps + i], 0)),
                whole(gate_w),
                whole(up_w),
                whole(down_w),
                whole(router),
            ]
            + [pl.BlockSpec(memory_space=pl.ANY)] * len(given),
            out_specs=[step(width), step(width), step(width + tail), step(width + tail)]
            + [keep(w) for w in widths],
        ),
        out_shape=out_shape,
        input_output_aliases={9 + i: 4 + i for i in range(len(given))},
        compiler_params=pltpu.CompilerParams(vmem_limit_bytes=48 << 20),
        cost_estimate=pl.CostEstimate(
            flops=12 * 2 * n * width * ffe,
            bytes_accessed=6 * width * ffe + 2 * n * width * 16,
            transcendentals=2 * n * ffe,
        ),
        name="expert_step",
    )(jnp.asarray(spots[0]), *rows, cots, cots, *weights, *given)


class Links:
    def __init__(self):
        self.n = lax.axis_size("dp")
        self.e = lax.axis_size("expert")
        self.chips = self.e // 2
        order = list(range(self.chips))
        if self.n == 2 and self.chips == 8:
            order = [0, 2, 4, 6, 7, 5, 3, 1]
        self.order = order
        where = np.argsort(np.array(order)).astype(np.int32)
        self.x = lax.axis_index("dp")
        self.me = lax.axis_index("expert")
        self.core = self.me % 2
        chip = self.me // 2
        self.place = jnp.sum(
            jnp.where(jnp.arange(self.chips, dtype=jnp.int32) == chip, jnp.asarray(where), 0)
        )

    def at(self, r, lane):
        place = (self.place + r) % self.chips
        order = jnp.asarray(np.array(self.order, np.int32))
        chip = jnp.sum(jnp.where(jnp.arange(self.chips, dtype=jnp.int32) == place, order, 0))
        return chip * 2 + (self.core ^ lane)

    def sibling(self, v):
        return lax.ppermute(v, "expert", [(i, i ^ 1) for i in range(self.e)])

    def flip(self, v, bit):
        return lax.ppermute(v, "expert", [(i, i ^ bit) for i in range(self.e)])

    def ring(self, v, step):
        c, o = self.chips, self.order
        pairs = [(o[k] * 2 + l, o[(k + step) % c] * 2 + l) for k in range(c) for l in (0, 1)]
        return lax.ppermute(v, "expert", pairs)

    def gather(self, block):
        c = self.chips
        half = block.shape[0] // 2
        got = {0: block}
        up = down = block
        for s in range(1, c // 2):
            up, down = self.ring(up, 1), self.ring(down, -1)
            got[c - s], got[s] = up, down
        far = (self.ring(up[:half], 1), self.ring(down[half:], -1))
        return got, far

    def scatter(self, s, far):
        c = self.chips
        half = far[0].shape[0]
        up, down = self.ring(far[0], 1), self.ring(far[1], -1)
        r = c // 2 - 1
        up = jnp.concatenate([add_low(up, s[r][:half]), s[r][half:]])
        down = jnp.concatenate([s[c - r][:half], add_low(down, s[c - r][half:])])
        up, down = self.ring(up, 1), self.ring(down, -1)
        for r in range(c // 2 - 2, 0, -1):
            up, down = self.ring(add_low(up, s[r]), 1), self.ring(add_low(down, s[c - r]), -1)
        return wide(s[0]) + wide(up) + wide(down)

    def swap(self, v):
        return lax.ppermute(v, "dp", [(0, 1), (1, 0)])

    def pick(self, v, other, axis):
        size = v.shape[axis] // self.n
        at = (1 - self.x if other else self.x) * size
        return lax.dynamic_slice_in_dim(v, at, size, axis)

    def both(self, own, got, axis):
        return jnp.where(
            self.x == 0,
            jnp.concatenate([own, got], axis),
            jnp.concatenate([got, own], axis),
        )

    def columns(self, v):
        if self.n == 2:
            return jnp.concatenate([self.pick(v, False, 1), self.swap(self.pick(v, True, 1))])
        return lax.all_to_all(v, "dp", split_axis=1, concat_axis=0, tiled=True)

    def columns_back(self, v):
        if self.n == 2:
            t = v.shape[0] // 2
            return self.both(v[:t], wide(self.swap(narrow(v[t:]))), 1)
        return wide(lax.all_to_all(narrow(v), "dp", split_axis=0, concat_axis=1, tiled=True))

    def rows(self, v):
        if self.n == 2:
            return jnp.concatenate([v, self.swap(v)])
        return lax.all_gather(v, "dp", axis=0, tiled=True)

    def sum_back(self, v):
        if self.n == 2:
            t = v.shape[0] // 2
            return v[:t] + wide(self.swap(narrow(v[t:])))
        return wide(lax.psum_scatter(narrow(v), "dp", scatter_dimension=0, tiled=True))

    def whole(self, v, axis):
        if self.n == 2:
            return self.both(v, self.swap(v), axis)
        return lax.all_gather(v, "dp", axis=axis, tiled=True)

    def shard_sum(self, v, axis):
        if self.n == 2:
            return self.pick(v, False, axis) + wide(self.swap(narrow(self.pick(v, True, axis))))
        return wide(lax.psum_scatter(narrow(v), "dp", scatter_dimension=axis, tiled=True))

    def whole_out(self, w):
        if self.n != 2 or self.e % 4:
            return lax.all_gather(w, "dp", axis=0, tiled=True)
        rows = w.shape[0]
        part = rows // 4
        q = self.me % 4
        a = self.swap(lax.dynamic_slice_in_dim(w, q * part, part, 0))
        b = self.flip(a, 2)
        c, d = self.flip(a, 1), self.flip(b, 1)
        full = jnp.zeros((rows * 2, w.shape[1]), w.dtype)
        full = lax.dynamic_update_slice_in_dim(full, w, self.x * rows, 0)
        for piece, at in ((a, q), (b, q ^ 2), (c, q ^ 1), (d, q ^ 3)):
            full = lax.dynamic_update_slice_in_dim(full, piece, (1 - self.x) * rows + at * part, 0)
        return full


def shards(
    tokens, cotangent, lengths, routes, gain_attn, w_query, key_weight, value_weight,
    w_out, gain_moe, w_router, w_gate, w_up, w_down,
):
    net = Links()
    c = net.chips
    length, width = tokens.shape
    dh = gain_attn.shape[0]
    heads = w_query.shape[1] // HEAD
    kv_heads = key_weight.shape[1] // HEAD
    group = heads // kv_heads
    fq, fk = w_query.shape[1], key_weight.shape[1]
    experts = w_router.shape[1]
    places, live, allowed = layout(lengths[0], length)

    stream = wide(tokens)
    inv_one = lax.rsqrt(jnp.mean(stream * stream, -1, keepdims=True) + norm_eps)
    token_cols = wide(net.columns(tokens))
    inv_all = net.rows(inv_one.reshape(1, length)).reshape(-1, 1)
    scaled_cols = token_cols * inv_all
    gain_one_low = wide(narrow(gain_attn))[None, :]
    normed_cols = narrow(scaled_cols * gain_one_low)
    w_qkv = jnp.concatenate([narrow(w_query), narrow(key_weight), narrow(value_weight)], 1)
    qkv = net.sum_back(mm(normed_cols, w_qkv))

    small = jnp.concatenate(
        [narrow(w_router).T, narrow(gain_attn)[None], narrow(gain_moe)[None]], 0
    )
    small = net.whole(small, 1)
    router_t, gain_one, gain_two = small[:experts], wide(small[experts]), wide(small[experts + 1])
    out_full = net.whole_out(narrow(w_out))
    mask = jnp.sum(
        (routes[:, :, None] == jnp.arange(experts, dtype=jnp.int32)[None, None, :]).astype(F32), 1
    )
    tail = 128
    cot_mask = jnp.concatenate(
        [cotangent, narrow(jnp.pad(mask, ((0, 0), (0, tail - experts))))], 1
    )
    cot_all = lax.all_gather(cot_mask, "expert", axis=0, tiled=True)
    router_pad = jnp.pad(router_t, ((0, tail - experts), (0, 0)))

    qkv_d, wg, wu, wd = lax.optimization_barrier(
        (qkv, narrow(w_gate[0]), narrow(w_up[0]), narrow(w_down[0]))
    )
    qkv = qkv_d
    gate_full, up_full = net.whole(wg, 0), net.whole(wu, 0)
    down_full = net.whole(wd, 0)

    q = narrow(rotary(qkv[:, :fq], places, heads, 1.0)).reshape(length, kv_heads, group, HEAD)
    k = narrow(rotary(qkv[:, fq : fq + fk], places, kv_heads, 1.0)).reshape(length, kv_heads, HEAD)
    v = narrow(qkv[:, fq + fk :]).reshape(length, kv_heads, HEAD)
    scores = score_scale * jnp.einsum("sngh,tnh->ngst", q, k, preferred_element_type=F32)
    masked = jnp.where(allowed, scores, mask_fill)
    peak = jnp.max(masked, -1, keepdims=True)
    raised = jnp.exp(masked - peak)
    attention = raised / jnp.sum(raised, -1, keepdims=True)
    attention_low = narrow(attention)
    context = jnp.einsum("ngst,tnh->sngh", attention_low, v, preferred_element_type=F32)
    context = context.reshape(length, fq)
    attended = narrow(jnp.where(live[:, None], context, 0.0))
    stream_mid = stream + mm(attended, out_full)
    inv_two = lax.rsqrt(jnp.mean(stream_mid * stream_mid, -1, keepdims=True) + norm_eps)
    scaled_two = stream_mid * inv_two
    normed_two = narrow(scaled_two * gain_two)

    def gates(rows, chosen):
        logits = jnp.where(chosen > 0, mm_nt(rows, router_t), mask_fill)
        top = jnp.max(logits, -1, keepdims=True)
        up = jnp.where(chosen > 0, jnp.exp(logits - top), 0.0)
        return up / jnp.sum(up, -1, keepdims=True)

    gate_own = gates(normed_two, mask)

    rows_got, rows_far = net.gather(normed_two)
    half = length // 2
    groups = [[0]] + [[s, c - s] for s in range(1, c // 2)] + [[c // 2]]
    kept, start, mixes, backs = None, 0, {}, {}
    weights = (gate_full, up_full, down_full, router_pad)
    for g in groups:
        if g == [c // 2]:
            x0 = jnp.concatenate(rows_far)
        else:
            x0 = jnp.concatenate([rows_got[r] for r in g])
        spots = [net.me] + [net.at(r, l) for l in (0, 1) for r in g]
        spots = (jnp.stack(spots).astype(jnp.int32), net.e)
        out = expert_step(
            spots, (x0, net.sibling(x0)), cot_all, weights, kept, start, net.e * length
        )
        kept, start = out[4:], start + len(g)
        for store, a, b in ((mixes, out[0], out[1]), (backs, out[2], out[3])):
            s = add_low(a, net.sibling(b))
            for i, r in enumerate(g):
                store[r] = s[i * length : (i + 1) * length]
    far = c // 2
    back = net.scatter(backs, (backs[far][:half], backs[far][half:]))
    mixed = narrow(stream_mid + net.scatter(mixes, (mixes[far][:half], mixes[far][half:])))

    rows_all, hid_all, gpg_all, upg_all, rg_all = kept
    d_down = net.shard_sum(mm_tn(hid_all, rg_all), 0)[None]
    d_gate = net.shard_sum(mm_tn(rows_all, gpg_all), 0)[None]
    d_up = net.shard_sum(mm_tn(rows_all, upg_all), 0)[None]

    ends = back[:, width:]
    gate_grad = ends[:, :experts] + ends[:, tail // 2 : tail // 2 + experts]
    chosen = gate_own * (gate_grad - jnp.sum(gate_own * gate_grad, -1, keepdims=True))
    logit_grad = narrow(chosen)
    n2g = back[:, :width] + mm(logit_grad, router_t)
    du = n2g * gain_two
    mid_grad = wide(cotangent) + inv_two * (
        du - scaled_two * jnp.mean(du * scaled_two, -1, keepdims=True)
    )
    d_small = jnp.concatenate(
        [mm_tn(logit_grad, normed_two), jnp.sum(n2g * scaled_two, 0)[None]], 0
    )
    d_small = net.shard_sum(d_small, 1)
    branch = narrow(mid_grad)

    per = dh // net.e
    slot = jnp.arange(dh, dtype=jnp.int32)
    lane, dist, inner = slot // (c * per), (slot // per) % c, slot % per
    source = (((net.place + dist) % c) * 2 + (net.core ^ lane)) * per + inner
    perm = (slot[:, None] == source[None, :]).astype(BF)

    seats = jnp.stack(
        [((net.place + r) % c) * 2 + (net.core ^ l) for l in (0, 1) for r in range(c)]
    ).astype(jnp.int32)

    def all_sum(d, widths):
        n = c * per
        s = add_low(d[:n], net.sibling(d[n:]))
        s = {r: s[r * per : (r + 1) * per] for r in range(c)}
        far = c // 2
        cut = per // 2
        total = net.scatter(s, (s[far][:cut], s[far][cut:]))
        got, ends = net.gather(narrow(total))
        got[far] = jnp.concatenate(ends)
        own = jnp.concatenate([got[r] for r in range(c)])
        return put_rows((own, net.sibling(own)), seats, widths)

    attended_cols = narrow(mm(net.columns(attended), perm))
    branch_all = net.rows(branch)
    [d_out] = all_sum(narrow(mm_tn(attended_cols, branch_all)), [width])

    zero = jnp.zeros((), BF)
    cg = jnp.where(live[:, None], narrow(mm_nt(branch, out_full)), zero)
    cg = cg.reshape(length, kv_heads, group, HEAD)
    ag = jnp.einsum("sngh,tnh->ngst", cg, v, preferred_element_type=F32)
    vg = narrow(jnp.einsum("ngst,sngh->tnh", attention_low, cg, preferred_element_type=F32))
    sgr = narrow(attention * (ag - jnp.sum(attention * ag, -1, keepdims=True)))
    qg = score_scale * jnp.einsum("ngst,tnh->sngh", sgr, k, preferred_element_type=F32)
    kg = score_scale * jnp.einsum("ngst,sngh->tnh", sgr, q, preferred_element_type=F32)
    qpg = narrow(rotary(qg.reshape(length, fq), places, heads, -1.0))
    kpg = narrow(rotary(kg.reshape(length, fk), places, kv_heads, -1.0))
    grads = jnp.concatenate([qpg, kpg, vg.reshape(length, fk)], 1)
    grads_all = net.rows(grads)
    normed_ring = narrow(mm(normed_cols, perm))
    d_qkv = mm_tn(normed_ring, grads_all)
    n1g_cols = mm_nt(grads_all, w_qkv)
    d_gain_one = jnp.sum(n1g_cols * scaled_cols, 0)[None]
    d_small = mm(narrow(jnp.concatenate([d_small, d_gain_one], 0)), perm)
    d_small = jnp.pad(d_small.T, ((0, 0), (0, 128 - experts - 2)))
    d_query, d_key, d_value, d_small = all_sum(
        narrow(jnp.concatenate([d_qkv, d_small], 1)), [fq, fk, fk, 128]
    )
    n1g = net.columns_back(n1g_cols)
    scaled_one = stream * inv_one
    du = n1g * gain_one
    d_tokens = mid_grad + inv_one * (
        du - scaled_one * jnp.mean(du * scaled_one, -1, keepdims=True)
    )
    return (
        mixed,
        d_tokens,
        d_small[:, experts + 1],
        d_query,
        d_key,
        d_value,
        d_out,
        d_small[:, experts],
        d_small[:, :experts],
        d_gate,
        d_up,
        d_down,
    )


def solution(mesh):
    rows = P(("dp", "expert"), None)
    flat, dense, routed = P("dp"), P("dp", None), P("expert", "dp", None)
    return jax.shard_map(
        shards,
        mesh=mesh,
        in_specs=(
            rows, rows, rows, rows, flat, dense, dense, dense, dense, flat, dense,
            routed, routed, routed,
        ),
        out_specs=(
            rows, rows, flat, dense, dense, dense, dense, flat, dense, routed, routed, routed,
        ),
        check_vma=False,
    )
```

```python
import jax
import jax.numpy as jnp
import numpy as np
from jax import lax
from jax.experimental import pallas as pl
from jax.experimental.pallas import tpu as pltpu
from jax.sharding import PartitionSpec as P

HEAD = 64
norm_eps = 1e-06
score_scale = 0.015625
rope_base = 10000.0
mask_fill = -1e30
BF = jnp.bfloat16
F32 = jnp.float32


def narrow(v):
    return v.astype(BF)


def wide(v):
    return v.astype(F32)


def mm(a, b):
    return jnp.dot(a, b, preferred_element_type=F32)


def mm_tn(a, b):
    return lax.dot_general(a, b, (((0,), (0,)), ((), ())), preferred_element_type=F32)


def mm_nt(a, b):
    return lax.dot_general(a, b, (((1,), (1,)), ((), ())), preferred_element_type=F32)


def add_low(a, b):
    return narrow(wide(a) + wide(b))


def layout(lengths, length):
    pieces = lengths.shape[0]
    order = jnp.arange(pieces, dtype=jnp.int32)
    ends = jnp.sum(jnp.where(order[None, :] <= order[:, None], lengths[None, :], 0), 1)
    starts = ends - lengths
    at = jnp.arange(length, dtype=jnp.int32)
    segment = jnp.sum((at[:, None] >= ends[None, :]).astype(jnp.int32), 1)
    owned = segment[:, None] == order[None, :]
    places = at - jnp.sum(jnp.where(owned, starts[None, :], 0), 1)
    live = segment < pieces - 1
    allowed = (
        (segment[:, None] == segment[None, :])
        & (at[None, :] <= at[:, None])
        & (live[None, :] | (at[:, None] == at[None, :]))
    )
    return places, live, allowed


def tie(v, *after):
    return lax.optimization_barrier((v, *after))[0]


ANY = pl.BlockSpec(memory_space=pl.ANY)
BIG = pltpu.CompilerParams(vmem_limit_bytes=56 << 20)


def cost(flops, moved, hard=0):
    return pl.CostEstimate(flops=int(flops), bytes_accessed=int(moved), transcendentals=int(hard))


def like(*shape, dtype=BF):
    return jax.ShapeDtypeStruct(shape, dtype)


def load_parts(parts, spots, whole, sems):
    return [
        pltpu.make_async_copy(
            ref, whole.at[pl.ds(pl.multiple_of(spots[i], 16), ref.shape[0])], sems.at[i]
        )
        for i, ref in enumerate(parts)
    ]


def turn(v, cosine, sine):
    lane = lax.broadcasted_iota(jnp.int32, v.shape, 1) % HEAD
    other = jnp.where(lane < HEAD // 2, pltpu.roll(v, 96, 1), pltpu.roll(v, 32, 1))
    return v * cosine + other * sine


def twice(v, odd):
    low = lax.broadcasted_iota(jnp.int32, v.shape, 1) < HEAD
    return jnp.where(low != odd, v, pltpu.roll(v, HEAD, 1))


def softmax_rows(q3, keys, allowed3):
    s = jnp.where(allowed3, mm_nt(q3, keys) * score_scale, mask_fill)
    e = jnp.exp(s - jnp.max(s, -1, keepdims=True))
    return e / jnp.sum(e, -1, keepdims=True)


def project_columns(cols, inverses, gain, weights):
    length, dh = cols[0].shape
    widths = [w.shape[1] for w in weights]
    tile = 256
    counts = [w // tile for w in widths]
    first = [sum(counts[:i]) for i in range(len(counts))]
    total = sum(widths)

    def body(ca, cb, ia, ib, g, wq, wk, wv, own, other, normed, low):
        i = pl.program_id(0)

        @pl.when(i == 0)
        def _():
            gain_row = wide(narrow(g[...]))
            normed[:length] = narrow(wide(ca[...]) * ia[...] * gain_row)
            normed[length:] = narrow(wide(cb[...]) * ib[...] * gain_row)

        def go(w):
            low[...] = narrow(w[...])
            out = mm(normed[...], low[...])
            own[...], other[...] = out[:length], narrow(out[length:])

        for ref, a, n in zip((wq, wk, wv), first, counts):
            pl.when((i >= a) & (i < a + n))(lambda ref=ref: go(ref))

    whole = lambda a: pl.BlockSpec(a.shape, lambda i: (0, 0))
    column = lambda a, n: pl.BlockSpec((dh, tile), lambda i: (0, jnp.clip(i - a, 0, n - 1)))
    return pl.pallas_call(
        body,
        grid=(sum(counts),),
        in_specs=[whole(v) for v in (*cols, *inverses, gain)]
        + [column(a, n) for a, n in zip(first, counts)],
        out_specs=[
            pl.BlockSpec((length, tile), lambda i: (0, i)),
            pl.BlockSpec((length, tile), lambda i: (0, i)),
            pl.BlockSpec((2 * length, dh), lambda i: (0, 0)),
            pl.BlockSpec((dh, tile), lambda i: (0, i)),
        ],
        out_shape=[
            like(length, total, dtype=F32), like(length, total), like(2 * length, dh), like(dh, total),
        ],
        cost_estimate=cost(4 * length * dh * total, 6 * dh * total),
        name="project_columns",
    )(*cols, *inverses, gain, *weights)


def attend(sums, tables, tokens, gain_two, router, chosen, out_parts, out_spots, heads, kv_heads):
    length, width = tokens.shape
    group = heads // kv_heads
    fq, fk = heads * HEAD, kv_heads * HEAD
    total = fq + 2 * fk
    n_sum, n_out = len(sums), len(out_parts)

    def body(spots, *refs):
        parts, refs = refs[:n_sum], refs[n_sum:]
        cosine, sine, allowed, live, tok, gain, rt, pick = refs[:8]
        outs = refs[8 : 8 + n_out]
        qkv_o, att_o, mid_o, norm_o, gate_o, w_out, sems = refs[8 + n_out :]
        copies = load_parts(outs, spots, w_out, sems)
        for copy in copies:
            copy.start()
        cos, sin = cosine[...], sine[...]

        def block(j):
            at = slice(j * 128, j * 128 + 128)
            v = wide(parts[0][:, at])
            for p in parts[1:]:
                v = v + wide(p[:, at])
            return at, v

        keys, values, q = [], [], []
        for j in range(fq // 128):
            at, v = block(j)
            v = narrow(turn(v, cos, sin))
            qkv_o[:, at] = v
            q.append(v)
        for j in range(fk // 128):
            at, v = block(fq // 128 + j)
            v = turn(v, cos, sin)
            qkv_o[:, at] = narrow(v)
            keys += [narrow(twice(v, False)), narrow(twice(v, True))]
        for j in range(fk // 128):
            at, v = block((fq + fk) // 128 + j)
            qkv_o[:, at] = narrow(v)
            values += [narrow(twice(v, False)), narrow(twice(v, True))]
        low = lax.broadcasted_iota(jnp.int32, (length, 128), 1) < HEAD
        ok = jnp.concatenate([allowed[...] > 0] * group)
        alive = live[...] > 0
        done = {}
        zero = jnp.zeros((length, 128), BF)
        for g in range(kv_heads):
            hs = range(g * group, (g + 1) * group)
            q3 = jnp.concatenate([jnp.where(low != bool(h % 2), q[h // 2], zero) for h in hs])
            a = narrow(softmax_rows(q3, keys[g], ok))
            ctx = mm(a, values[g])
            for n, h in enumerate(hs):
                done[h] = ctx[n * length : (n + 1) * length]
                if h % 2:
                    both = jnp.where(low, done.pop(h - 1), done.pop(h))
                    att_o[:, h // 2 * 128 : h // 2 * 128 + 128] = narrow(
                        jnp.where(alive, both, 0.0)
                    )
        for copy in copies:
            copy.wait()
        mid = wide(tok[...]) + mm(att_o[...], w_out[...])
        mid_o[...] = mid
        inverse = lax.rsqrt(jnp.mean(mid * mid, -1, keepdims=True) + norm_eps)
        normed = narrow(mid * inverse * gain[...])
        norm_o[...] = normed
        yes = pick[...] > 0
        logits = jnp.where(yes, mm_nt(normed, rt[...]), mask_fill)
        up = jnp.where(yes, jnp.exp(logits - jnp.max(logits, -1, keepdims=True)), 0.0)
        gate_o[...] = up / jnp.sum(up, -1, keepdims=True)

    given = (*sums, *tables, tokens, gain_two, router, chosen)
    whole = [pl.BlockSpec(memory_space=pltpu.VMEM)] * len(given)
    return pl.pallas_call(
        body,
        in_specs=[pl.BlockSpec(memory_space=pltpu.SMEM)] + whole + [ANY] * n_out,
        out_shape=[
            like(length, total),
            like(length, fq),
            like(length, width, dtype=F32),
            like(length, width),
            like(length, router.shape[0], dtype=F32),
        ],
        scratch_shapes=[
            pltpu.VMEM((fq, width), BF),
            pltpu.SemaphoreType.DMA((n_out,)),
        ],
        compiler_params=BIG,
        cost_estimate=cost(
            2 * length * fq * width + 4 * heads * length * length * 128,
            2 * fq * width + 12 * length * total,
            heads * length * length,
        ),
        name="attend",
    )(out_spots, *given, *out_parts)


def second_norm_back(sums, gates, router, mid, gain_two, cotangent, normed, experts):
    length, width = mid.shape
    tail = router.shape[0]

    def body(a, b, c, gate_r, rt, mid_r, gain, cot, norm, mid_o, branch_o, small_o):
        ends = wide(a[:, width:]) + wide(b[:, width:]) + wide(c[:, width:])
        grad = ends + pltpu.roll(ends, tail // 2, 1)
        gate = gate_r[...]
        chosen = gate * (grad - jnp.sum(gate * grad, -1, keepdims=True))
        logit = narrow(chosen)
        n2g = wide(a[:, :width]) + wide(b[:, :width]) + wide(c[:, :width]) + mm(logit, rt[...])
        m = mid_r[...]
        inverse = lax.rsqrt(jnp.mean(m * m, -1, keepdims=True) + norm_eps)
        scaled = m * inverse
        du = n2g * gain[...]
        out = wide(cot[...]) + inverse * (
            du - scaled * jnp.mean(du * scaled, -1, keepdims=True)
        )
        mid_o[...] = out
        branch_o[...] = narrow(out)
        small_o[:experts] = narrow(mm_tn(logit, norm[...])[:experts])
        gain_row = jnp.sum(n2g * scaled, 0, keepdims=True)
        small_o[experts:] = narrow(jnp.broadcast_to(gain_row, (16, width)))

    return pl.pallas_call(
        body,
        out_shape=[like(length, width, dtype=F32), like(length, width), like(experts + 16, width)],
        compiler_params=BIG,
        cost_estimate=cost(6 * length * width * tail, 20 * length * width),
        name="second_norm_back",
    )(*sums, gates, router, mid, gain_two, cotangent, normed)


def attend_back(qkv, tables, branch, out_parts, out_spots, heads, kv_heads):
    length, width = branch.shape
    group = heads // kv_heads
    fq, fk = heads * HEAD, kv_heads * HEAD
    total = fq + 2 * fk
    n_out = len(out_parts)

    def body(spots, qkv_r, cosine, sine, allowed, live, br, *refs):
        outs = refs[:n_out]
        grads, w_out, sems = refs[n_out:]
        copies = load_parts(outs, spots, w_out, sems)
        for copy in copies:
            copy.start()
        cos, sin = cosine[...], -sine[...]
        low = lax.broadcasted_iota(jnp.int32, (length, 128), 1) < HEAD
        ok = jnp.concatenate([allowed[...] > 0] * group)
        zero = jnp.zeros((length, 128), BF)
        q = [qkv_r[:, j * 128 : j * 128 + 128] for j in range(fq // 128)]
        keys, values = [], []
        for store, base in ((keys, fq), (values, fq + fk)):
            for j in range(fk // 128):
                v = wide(qkv_r[:, base + j * 128 : base + j * 128 + 128])
                store += [narrow(twice(v, False)), narrow(twice(v, True))]
        for copy in copies:
            copy.wait()
        cg = narrow(jnp.where(live[...] > 0, mm_nt(br[...], w_out[...]), 0.0))
        done, fold = {}, {}

        def put(at, v, rotate):
            v = turn(v, cos, sin) if rotate else v
            grads[:, at * 128 : at * 128 + 128] = narrow(v)

        for g in range(kv_heads):
            hs = range(g * group, (g + 1) * group)
            pick = lambda src: jnp.concatenate(
                [jnp.where(low != bool(h % 2), src(h // 2), zero) for h in hs]
            )
            q3 = pick(lambda j: q[j])
            c3 = pick(lambda j: cg[:, j * 128 : j * 128 + 128])
            a = softmax_rows(q3, keys[g], ok)
            ag = mm_nt(c3, values[g])
            sg = narrow(a * (ag - jnp.sum(a * ag, -1, keepdims=True)))
            vg = mm_tn(narrow(a), c3)
            kg = score_scale * mm_tn(sg, q3)
            qg = score_scale * mm(sg, keys[g])
            fold[g] = (kg + pltpu.roll(kg, HEAD, 1), vg + pltpu.roll(vg, HEAD, 1))
            for n, h in enumerate(hs):
                done[h] = qg[n * length : (n + 1) * length]
                if h % 2:
                    put(h // 2, jnp.where(low, done.pop(h - 1), done.pop(h)), True)
            if g % 2:
                (ka, va), (kb, vb) = fold.pop(g - 1), fold.pop(g)
                put(fq // 128 + g // 2, jnp.where(low, ka, kb), True)
                put((fq + fk) // 128 + g // 2, jnp.where(low, va, vb), False)

    vm = pl.BlockSpec(memory_space=pltpu.VMEM)
    return pl.pallas_call(
        body,
        in_specs=[pl.BlockSpec(memory_space=pltpu.SMEM)] + [vm] * 6 + [ANY] * n_out,
        out_shape=like(length, total),
        scratch_shapes=[pltpu.VMEM((fq, width), BF), pltpu.SemaphoreType.DMA((n_out,))],
        compiler_params=BIG,
        cost_estimate=cost(
            2 * length * fq * width + 12 * heads * length * length * 128,
            2 * fq * width + 8 * length * total,
            heads * length * length,
        ),
        name="attend_back",
    )(out_spots, qkv, *tables, branch, *out_parts)


def ring_rows(wanted, at, value, scratch, own, sib, columns):
    per = value.shape[0] // wanted
    scratch[...] = value
    for i in range(wanted):
        block = narrow(scratch[pl.ds(pl.multiple_of(at[i] * per, 8), per)])
        out, j = (own, i) if i < wanted // 2 else (sib, i - wanted // 2)
        out[j * per : (j + 1) * per, columns] = block


def out_gradient(attended, branches, seats):
    dh, width = attended[0].shape[1], branches[0].shape[1]
    tile = 512

    def body(at, aa, ab, ba, bb, own, sib, scratch):
        a = jnp.concatenate([aa[...], ab[...]])
        b = jnp.concatenate([ba[...], bb[...]])
        for j in range(width // tile):
            cols = slice(j * tile, (j + 1) * tile)
            ring_rows(seats.shape[0], at, mm_tn(a, b[:, cols]), scratch, own, sib, cols)

    vm = pl.BlockSpec(memory_space=pltpu.VMEM)
    return pl.pallas_call(
        body,
        in_specs=[pl.BlockSpec(memory_space=pltpu.SMEM)] + [vm] * 4,
        out_shape=[like(dh // 2, width)] * 2,
        scratch_shapes=[pltpu.VMEM((dh, tile), F32)],
        compiler_params=BIG,
        cost_estimate=cost(4 * attended[0].shape[0] * dh * width, 2 * dh * width),
        name="out_gradient",
    )(seats, *attended, *branches)


def projection_gradient(grads, low, normed, cols, inverses, small, seats, experts):
    length, total = grads[0].shape
    dh = low.shape[0]
    tile = 256
    steps = total // tile

    def body(at, ga, gb, w, norm, ca, cb, ia, ib, sa, sb, own, sib, n1a, n1b, scratch, acc, last):
        i = pl.program_id(0)
        g = jnp.concatenate([ga[...], gb[...]])
        add = mm_nt(g, w[...])

        @pl.when(i == 0)
        def _():
            acc[...] = add

        @pl.when(i > 0)
        def _():
            acc[...] += add

        where = pl.ds(pl.multiple_of(i * tile, tile), tile)
        ring_rows(seats.shape[0], at, mm_tn(norm[...], g), scratch, own, sib, where)

        @pl.when(i == steps - 1)
        def _():
            n1 = acc[...]
            n1a[...], n1b[...] = n1[:length], narrow(n1[length:])
            gain = n1[:length] * (wide(ca[...]) * ia[...]) + n1[length:] * (
                wide(cb[...]) * ib[...]
            )
            last[...] = jnp.zeros_like(last)
            last[: experts + 16] = wide(sa[...]) + wide(sb[...])
            row = jnp.sum(gain, 0, keepdims=True)
            last[experts + 8 : experts + 16] = jnp.broadcast_to(row, (8, dh))
            ring_rows(
                seats.shape[0], at, last[...].T, scratch.at[:, :128], own, sib,
                slice(total, total + 128),
            )

    whole = lambda a: pl.BlockSpec(a.shape, lambda i, at: (0, 0))
    column = lambda a: pl.BlockSpec((a.shape[0], tile), lambda i, at: (0, i))
    shapes = [like(dh // 2, total + 128)] * 2 + [like(length, dh, dtype=F32), like(length, dh)]
    return pl.pallas_call(
        body,
        grid_spec=pltpu.PrefetchScalarGridSpec(
            num_scalar_prefetch=1,
            grid=(steps,),
            in_specs=[column(grads[0]), column(grads[1]), column(low)]
            + [whole(v) for v in (normed, *cols, *inverses, *small)],
            out_specs=[whole(s) for s in shapes],
            scratch_shapes=[
                pltpu.VMEM((dh, tile), F32),
                pltpu.VMEM((2 * length, dh), F32),
                pltpu.VMEM((128, dh), F32),
            ],
        ),
        out_shape=shapes,
        compiler_params=BIG,
        cost_estimate=cost(8 * length * dh * total, 4 * dh * total),
        name="projection_gradient",
    )(seats, *grads, low, normed, *cols, *inverses, *small)


def put_rows(pair, at, widths):
    rows, per = pair[0].shape[0] * 2, pair[0].shape[0] * 2 // at.shape[0]
    n = at.shape[0]
    c = n // 2
    total = sum(widths)
    cuts = [sum(widths[:i]) for i in range(len(widths) + 1)]
    if per % 16:
        out = jnp.zeros((rows, total), F32)
        for i in range(n):
            blk = wide(pair[i // c][i % c * per : (i % c + 1) * per])
            out = lax.dynamic_update_slice_in_dim(out, blk, at[i] * per, 0)
        return [out[:, a:b] for a, b in zip(cuts, cuts[1:])]
    k = len(widths)

    def body(at_ref, own, sib, *refs):
        outs, held, sems = refs[:k], refs[k : 2 * k], refs[2 * k]
        copies = []
        for i in range(n):
            src, j = (own, i) if i < c else (sib, i - c)
            row = pl.multiple_of(at_ref[i] * per, 8)
            for w in range(k):
                held[w][i * per : (i + 1) * per] = wide(
                    src[j * per : (j + 1) * per, cuts[w] : cuts[w + 1]]
                )
                copy = pltpu.make_async_copy(
                    held[w].at[pl.ds(i * per, per)], outs[w].at[pl.ds(row, per)], sems.at[i, w]
                )
                copy.start()
                copies.append(copy)
        for copy in copies:
            copy.wait()

    vm = pl.BlockSpec(memory_space=pltpu.VMEM)
    return pl.pallas_call(
        body,
        in_specs=[pl.BlockSpec(memory_space=pltpu.SMEM), vm, vm],
        out_specs=[ANY] * k,
        out_shape=[like(rows, w, dtype=F32) for w in widths],
        scratch_shapes=[pltpu.VMEM((rows, w), F32) for w in widths]
        + [pltpu.SemaphoreType.DMA((n, k))],
        compiler_params=BIG,
        cost_estimate=cost(rows * total, rows * total * 6),
        name="put_rows",
    )(at, *pair)


def expert_step(me, tiles, cots, cot_blocks, router, gate, up, down, spots, kept, start, total):
    width, ffe = cots.shape[1] - router.shape[0], gate[0].shape[1]
    tail = router.shape[0]
    count = len(tiles)
    two = sum(p.shape[0] for p in tiles[0])
    block = two // 2
    n = count * block
    pieces = [p for t in tiles for p in t]
    parts = [*gate, *up, *down]
    k, m = len(gate), len(pieces)

    def body(spot, rows_at, ca, cb, rt, *refs):
        xs, ws = refs[:m], refs[m : m + 3 * k]
        refs = refs[-15:]
        mix_a, mix_b, row_a, row_b, x_o, hid_o, gpg_o, upg_o, rg_o = refs[:9]
        held, gw, uw, dw, sems, wsems = refs[9:]
        i = pl.program_id(0)
        moves, at, j = [], 0, 0
        for t in tiles:
            group = []
            for p in t:
                dst = held.at[pl.ds(at, p.shape[0])]
                group.append(pltpu.make_async_copy(xs[j], dst, sems.at[j]))
                at, j = at + p.shape[0], j + 1
            moves.append(group)
        loads = []
        for z, whole in enumerate((gw, uw, dw)):
            loads.append(
                [
                    pltpu.make_async_copy(
                        ws[z * k + p],
                        whole.at[
                            pl.ds(pl.multiple_of(rows_at[z * k + p], 16), ws[z * k + p].shape[0])
                        ],
                        wsems.at[z * k + p],
                    )
                    for p in range(k)
                ]
            )

        @pl.when(i == 0)
        def _():
            for copy in [*moves[0], *loads[0], *loads[1], *loads[2]]:
                copy.start()
            for copy in [c for g in moves[1:] for c in g]:
                copy.start()

        for t in range(count):

            @pl.when(i == t)
            def _():
                for copy in moves[t]:
                    copy.wait()

        @pl.when(i == 0)
        def _():
            for copy in [*loads[0], *loads[1], *loads[2]]:
                copy.wait()

        x = held[pl.ds(pl.multiple_of(i * two, two), two)]
        cm = jnp.concatenate([ca[...], cb[...]])
        cot, chosen = wide(cm[:, :width]), cm[:, width:] > 0
        x_o[...] = x
        logits = jnp.where(chosen, mm_nt(x, rt[...]), mask_fill)
        top = jnp.max(logits, -1, keepdims=True)
        raised = jnp.where(chosen, jnp.exp(logits - top), 0.0)
        mine = lax.broadcasted_iota(jnp.int32, raised.shape, 1)
        weight = jnp.sum(jnp.where(mine == spot[0], raised, 0.0), -1, keepdims=True)
        weight = wide(narrow(weight / jnp.sum(raised, -1, keepdims=True)))
        gate_pre, up_pre = mm(x, gw[...]), mm(x, uw[...])
        sg = jax.nn.sigmoid(gate_pre)
        silu = gate_pre * sg
        hidden = narrow(silu * up_pre)
        hid_o[...] = hidden
        result_grad = narrow(weight * cot)
        rg_o[...] = result_grad
        result = wide(narrow(mm(hidden, dw[...])))
        mix = narrow(weight * result)
        mix_a[...], mix_b[...] = mix[:block], mix[block:]
        gate_grad = jnp.sum(result * cot, -1, keepdims=True)
        hidden_grad = mm_nt(result_grad, dw[...])
        gpg = narrow(hidden_grad * up_pre * sg * (1.0 + gate_pre * (1.0 - sg)))
        upg = narrow(hidden_grad * silu)
        gpg_o[...], upg_o[...] = gpg, upg
        row = narrow(mm_nt(gpg, gw[...]) + mm_nt(upg, uw[...]))
        row_a[:, :width], row_b[:, :width] = row[:block], row[block:]
        high = wide(narrow(gate_grad))
        ends = jnp.where(mine == spot[0], high, 0.0)
        ends = narrow(jnp.where(mine == spot[0] + tail // 2, gate_grad - high, ends))
        row_a[:, width:], row_b[:, width:] = ends[:block], ends[block:]

    step = lambda w: pl.BlockSpec((block, w), lambda i, s, r: (i, 0))
    keep = lambda w: pl.BlockSpec((two, w), lambda i, s, r: (start + i, 0))
    widths = [width, ffe, ffe, ffe, width]
    out_shape = [like(n, width), like(n, width), like(n, width + tail), like(n, width + tail)]
    out_shape += [like(total, w) for w in widths]
    given = list(kept or ())
    before = 5 + m + 3 * k
    return pl.pallas_call(
        body,
        grid_spec=pltpu.PrefetchScalarGridSpec(
            num_scalar_prefetch=2,
            grid=(count,),
            in_specs=[
                pl.BlockSpec((block, width + tail), lambda i, s, r: (s[1 + i], 0)),
                pl.BlockSpec((block, width + tail), lambda i, s, r: (s[1 + count + i], 0)),
                pl.BlockSpec(router.shape, lambda i, s, r: (0, 0)),
            ]
            + [ANY] * (m + 3 * k + len(given)),
            out_specs=[step(width), step(width), step(width + tail), step(width + tail)]
            + [keep(w) for w in widths],
            scratch_shapes=[
                pltpu.VMEM((count * two, width), BF),
                pltpu.VMEM((width, ffe), BF),
                pltpu.VMEM((width, ffe), BF),
                pltpu.VMEM((ffe, width), BF),
                pltpu.SemaphoreType.DMA((m,)),
                pltpu.SemaphoreType.DMA((3 * k,)),
            ],
        ),
        out_shape=out_shape,
        input_output_aliases={before + i: 4 + i for i in range(len(given))},
        compiler_params=BIG,
        cost_estimate=cost(
            24 * n * width * ffe, 6 * width * ffe + n * width * 28, 2 * n * ffe
        ),
        name="expert_step",
    )(jnp.stack([me, *cot_blocks]).astype(jnp.int32), spots, cots, cots, router, *pieces, *parts, *given)


class Links:
    def __init__(self):
        self.n = lax.axis_size("dp")
        self.e = lax.axis_size("expert")
        self.chips = self.e // 2
        order = list(range(self.chips))
        if self.n == 2 and self.chips == 8:
            order = [0, 2, 4, 6, 7, 5, 3, 1]
        self.order = order
        where = np.argsort(np.array(order)).astype(np.int32)
        self.x = lax.axis_index("dp")
        self.me = lax.axis_index("expert")
        self.core = self.me % 2
        chip = self.me // 2
        self.place = jnp.sum(
            jnp.where(jnp.arange(self.chips, dtype=jnp.int32) == chip, jnp.asarray(where), 0)
        )

    def at_place(self, r):
        return (self.place + r) % self.chips

    def at(self, r, lane):
        place = self.at_place(r)
        order = jnp.asarray(np.array(self.order, np.int32))
        chip = jnp.sum(jnp.where(jnp.arange(self.chips, dtype=jnp.int32) == place, order, 0))
        return chip * 2 + (self.core ^ lane)

    def sibling(self, v):
        return lax.ppermute(v, "expert", [(i, i ^ 1) for i in range(self.e)])

    def flip(self, v, bit):
        return lax.ppermute(v, "expert", [(i, i ^ bit) for i in range(self.e)])

    def ring(self, v, step):
        c, o = self.chips, self.order
        pairs = [(o[k] * 2 + l, o[(k + step) % c] * 2 + l) for k in range(c) for l in (0, 1)]
        return lax.ppermute(v, "expert", pairs)

    def gather(self, block):
        c = self.chips
        half = block.shape[0] // 2
        got = {0: block}
        up = down = block
        for s in range(1, c // 2):
            up, down = self.ring(up, 1), self.ring(down, -1)
            got[c - s], got[s] = up, down
        far = (self.ring(up[:half], 1), self.ring(down[half:], -1))
        return got, far

    def scatter(self, s, far):
        c = self.chips
        half = far[0].shape[0]
        first = up, down = self.ring(far[0], 1), self.ring(far[1], -1)
        r = c // 2 - 1
        up = jnp.concatenate([add_low(up, s[r][:half]), s[r][half:]])
        down = jnp.concatenate([s[c - r][:half], add_low(down, s[c - r][half:])])
        up, down = self.ring(up, 1), self.ring(down, -1)
        for r in range(c // 2 - 2, 0, -1):
            up, down = self.ring(add_low(up, s[r]), 1), self.ring(add_low(down, s[c - r]), -1)
        return (s[0], up, down), first

    def swap(self, v):
        return lax.ppermute(v, "dp", [(0, 1), (1, 0)])

    def pick(self, v, other, axis):
        size = v.shape[axis] // self.n
        at = (1 - self.x if other else self.x) * size
        return lax.dynamic_slice_in_dim(v, at, size, axis)

    def both(self, own, got, axis):
        return jnp.where(
            self.x == 0,
            jnp.concatenate([own, got], axis),
            jnp.concatenate([got, own], axis),
        )

    def columns(self, v):
        if self.n == 2:
            return jnp.concatenate([self.pick(v, False, 1), self.swap(self.pick(v, True, 1))])
        return lax.all_to_all(v, "dp", split_axis=1, concat_axis=0, tiled=True)

    def columns_back(self, v):
        if self.n == 2:
            t = v.shape[0] // 2
            return self.both(v[:t], wide(self.swap(narrow(v[t:]))), 1)
        return wide(lax.all_to_all(narrow(v), "dp", split_axis=0, concat_axis=1, tiled=True))

    def rows(self, v):
        if self.n == 2:
            return jnp.concatenate([v, self.swap(v)])
        return lax.all_gather(v, "dp", axis=0, tiled=True)

    def sum_back(self, v):
        if self.n == 2:
            t = v.shape[0] // 2
            return v[:t] + wide(self.swap(narrow(v[t:])))
        return wide(lax.psum_scatter(narrow(v), "dp", scatter_dimension=0, tiled=True))

    def whole(self, v, axis):
        if self.n == 2:
            return self.both(v, self.swap(v), axis)
        return lax.all_gather(v, "dp", axis=axis, tiled=True)

    def shard_sum(self, v, axis, after=None):
        if self.n == 2:
            got = self.swap(narrow(self.pick(v, True, axis)))
            return self.pick(v, False, axis) + wide(got if after is None else tie(got, after))
        return wide(lax.psum_scatter(narrow(v), "dp", scatter_dimension=axis, tiled=True))

    def parts(self, w):
        if self.n == 2:
            n = w.shape[0]
            return [w, self.swap(w)], [self.x * n, (1 - self.x) * n]
        return [lax.all_gather(w, "dp", axis=0, tiled=True)], [self.x * 0]

    def parts_by_four(self, w):
        if self.n != 2 or self.e % 4:
            return self.parts(w)
        n = w.shape[0]
        part = n // 4
        q = self.me % 4
        a = self.swap(lax.dynamic_slice_in_dim(w, q * part, part, 0))
        b = self.flip(a, 2)
        c, d = self.flip(a, 1), self.flip(b, 1)
        base = (1 - self.x) * n
        return [w, a, b, c, d], [self.x * n] + [base + (q ^ z) * part for z in (0, 2, 1, 3)]


def wide_sum(v):
    out = wide(v[0])
    for w in v[1:]:
        out = out + wide(w)
    return out


def shards(
    tokens, cotangent, lengths, routes, gain_attn, w_query, key_weight, value_weight,
    w_out, gain_moe, w_router, w_gate, w_up, w_down,
):
    net = Links()
    c, pair = net.chips, net.n == 2
    length, width = tokens.shape
    dh = gain_attn.shape[0]
    heads, kv_heads = w_query.shape[1] // HEAD, key_weight.shape[1] // HEAD
    fq, fk = w_query.shape[1], key_weight.shape[1]
    experts = w_router.shape[1]
    tail = 128
    far, half = c // 2, length // 2

    stream = wide(tokens)
    inv_one = lax.rsqrt(jnp.mean(stream * stream, -1, keepdims=True) + norm_eps)
    if pair:
        cols = (net.pick(tokens, False, 1), net.swap(net.pick(tokens, True, 1)))
        inverses = (inv_one, net.swap(inv_one.reshape(1, length)).reshape(length, 1))
        own, other, normed_cols, w_qkv = project_columns(
            cols, inverses, gain_attn[None], (w_query, key_weight, value_weight)
        )
        arrived = net.swap(other)
        sums = (own, arrived)
    else:
        scaled_cols = wide(net.columns(tokens)) * net.rows(inv_one.reshape(1, length)).reshape(-1, 1)
        normed_cols = narrow(scaled_cols * wide(narrow(gain_attn))[None, :])
        w_qkv = jnp.concatenate([narrow(w_query), narrow(key_weight), narrow(value_weight)], 1)
        arrived = net.sum_back(mm(normed_cols, w_qkv))
        sums = (arrived,)

    small = jnp.concatenate(
        [narrow(w_router).T, narrow(gain_attn)[None], narrow(gain_moe)[None]], 0
    )
    small = net.whole(small, 1)
    gain_one, gain_two = wide(small[experts])[None], wide(small[experts + 1])[None]
    router = jnp.pad(small[:experts], ((0, tail - experts), (0, 0)))
    out_parts, out_spots = net.parts_by_four(narrow(w_out))
    out_spots = jnp.stack(out_spots).astype(jnp.int32)
    hits = routes[:, :, None] == jnp.arange(tail, dtype=jnp.int32)[None, None, :]
    chosen = narrow(jnp.any(hits, 1))
    cot_all = lax.all_gather(
        jnp.concatenate([cotangent, chosen], 1), "expert", axis=0, tiled=True
    )
    gate_parts, gate_spots = net.parts(tie(narrow(w_gate[0]), arrived))
    up_parts, _ = net.parts(tie(narrow(w_up[0]), arrived))
    down_parts, down_spots = net.parts(tie(narrow(w_down[0]), arrived))
    expert_spots = jnp.stack(gate_spots * 2 + down_spots).astype(jnp.int32)

    places, live, allowed = layout(lengths[0], length)
    inner = jnp.arange(128, dtype=jnp.int32) % (HEAD // 2)
    angles = places.astype(F32)[:, None] * (rope_base ** (-inner.astype(F32) * 2.0 / HEAD))[None]
    sign = jnp.where(jnp.arange(128) % HEAD < HEAD // 2, -1.0, 1.0)[None]
    tables = (
        jnp.cos(angles), jnp.sin(angles) * sign, allowed.astype(F32), live.astype(F32)[:, None],
    )
    qkv, attended, mid, normed_two, gates = attend(
        sums, tables, tokens, gain_two, router, chosen, out_parts, out_spots, heads, kv_heads
    )

    got, ends = net.gather(normed_two)
    beside = {r: net.sibling(v) for r, v in got.items()}
    ends_beside = tuple(net.sibling(v) for v in ends)
    near = [0] + [r for s in range(1, far - 1) for r in (s, c - s)]
    kept, start, mixes, backs = None, 0, {}, {}
    for g in (near, [far, far - 1, c - far + 1]):
        tiles = [(*ends, *ends_beside) if r == far else (got[r], beside[r]) for r in g]
        blocks = [net.at(r, l) for l in (0, 1) for r in g]
        out = expert_step(
            net.me, tiles, cot_all, blocks, router, gate_parts, up_parts, down_parts,
            expert_spots, kept, start, net.e * length,
        )
        kept, start = out[4:], start + len(g)
        for store, a, b in ((mixes, out[0], out[1]), (backs, out[2], out[3])):
            s = add_low(a, net.sibling(b))
            for i, r in enumerate(g):
                store[r] = s[i * length : (i + 1) * length]
        if g == near:
            after_near = out[0]
    back, first = net.scatter(backs, (backs[far][:half], backs[far][half:]))
    mix_far = tie(mixes[far], back[1])
    mixed, _ = net.scatter(mixes, (mix_far[:half], mix_far[half:]))
    mixed = narrow(mid + wide_sum(mixed))

    rows_all, hid_all, gpg_all, upg_all, rg_all = kept
    hid_all, gpg_all, upg_all = (tie(v, first[0]) for v in (hid_all, gpg_all, upg_all))
    expert_grads = [mm_tn(hid_all, rg_all), mm_tn(rows_all, gpg_all), mm_tn(rows_all, upg_all)]

    mid_grad, branch, d_small = second_norm_back(
        back, gates, router, mid, gain_two, cotangent, normed_two, experts
    )

    seats = jnp.stack([net.at_place(r) * 2 + (net.core ^ l) for l in (0, 1) for r in range(c)])
    seats = seats.astype(jnp.int32)
    per = dh // net.e
    if not pair:
        slot = jnp.arange(dh, dtype=jnp.int32)
        source = jnp.sum(
            jnp.where(slot[:, None] // per == jnp.arange(net.e)[None, :], seats[None, :], 0), 1
        ) * per + slot % per
        perm = (slot[:, None] == source[None, :]).astype(BF)

    def all_sum(own, sib, widths):
        s = add_low(own, net.sibling(sib))
        s = {r: s[r * per : (r + 1) * per] for r in range(c)}
        cut = per // 2
        total, _ = net.scatter(s, (s[far][:cut], s[far][cut:]))
        got, ends = net.gather(narrow(wide_sum(total)))
        got[far] = jnp.concatenate(ends)
        own = jnp.concatenate([got[r] for r in range(c)])
        return put_rows((own, net.sibling(own)), seats, widths)

    if pair:
        part = tie(net.pick(attended, True, 1), after_near)
        pieces = out_gradient(
            (net.pick(attended, False, 1), net.swap(part)), (branch, net.swap(branch)), seats
        )
    else:
        d = narrow(mm_tn(narrow(mm(net.columns(attended), perm)), net.rows(branch)))
        pieces = d[: dh // 2], d[dh // 2 :]
    [d_out] = all_sum(*pieces, [width])

    grads = attend_back(qkv, tables, branch, out_parts, out_spots, heads, kv_heads)
    if pair:
        d_small = (net.pick(d_small, False, 1), net.swap(net.pick(d_small, True, 1)))
        own, sib, n1, n1_other = projection_gradient(
            (grads, net.swap(grads)), w_qkv, normed_cols, cols, inverses, d_small, seats, experts
        )
        n1g = net.both(n1, wide(net.swap(n1_other)), 1)
    else:
        grads_all = net.rows(grads)
        d_qkv = mm_tn(narrow(mm(normed_cols, perm)), grads_all)
        n1 = mm_nt(grads_all, w_qkv)
        n1g = net.columns_back(n1)
        d_small = net.shard_sum(wide(d_small), 1)
        d_gain = jnp.broadcast_to(jnp.sum(n1 * scaled_cols, 0)[None], (8, dh))
        d_small = jnp.concatenate([d_small[: experts + 8], d_gain], 0)
        d_small = jnp.pad(mm(narrow(d_small), perm).T, ((0, 0), (0, tail - experts - 16)))
        d = narrow(jnp.concatenate([d_qkv, d_small], 1))
        own, sib = d[: dh // 2], d[dh // 2 :]
    d_query, d_key, d_value, d_small = all_sum(own, sib, [fq, fk, fk, tail])
    scaled_one = stream * inv_one
    du = n1g * gain_one
    d_tokens = mid_grad + inv_one * (
        du - scaled_one * jnp.mean(du * scaled_one, -1, keepdims=True)
    )
    d_down, d_gate, d_up = (net.shard_sum(v, 0, grads)[None] for v in expert_grads)
    return (
        mixed,
        d_tokens,
        d_small[:, experts + 8],
        d_query,
        d_key,
        d_value,
        d_out,
        d_small[:, experts],
        d_small[:, :experts],
        d_gate,
        d_up,
        d_down,
    )


def solution(mesh):
    rows = P(("dp", "expert"), None)
    flat, dense, routed = P("dp"), P("dp", None), P("expert", "dp", None)
    return jax.shard_map(
        shards,
        mesh=mesh,
        in_specs=(
            rows, rows, rows, rows, flat, dense, dense, dense, dense, flat, dense,
            routed, routed, routed,
        ),
        out_specs=(
            rows, rows, flat, dense, dense, dense, dense, flat, dense, routed, routed, routed,
        ),
        check_vma=False,
    )
```

```python
import jax
import jax.numpy as jnp
import numpy as np
from jax import lax
from jax.experimental import pallas as pl
from jax.experimental.pallas import tpu as pltpu
from jax.sharding import PartitionSpec as P

HEAD = 64
norm_eps = 1e-06
score_scale = 0.015625
rope_base = 10000.0
mask_fill = -1e30
BF = jnp.bfloat16
F32 = jnp.float32


def narrow(v):
    return v.astype(BF)


def wide(v):
    return v.astype(F32)


def mm(a, b):
    return jnp.dot(a, b, preferred_element_type=F32)


def mm_tn(a, b):
    return lax.dot_general(a, b, (((0,), (0,)), ((), ())), preferred_element_type=F32)


def mm_nt(a, b):
    return lax.dot_general(a, b, (((1,), (1,)), ((), ())), preferred_element_type=F32)


def add_low(a, b):
    return narrow(wide(a) + wide(b))


def layout(lengths, length):
    pieces = lengths.shape[0]
    order = jnp.arange(pieces, dtype=jnp.int32)
    ends = jnp.sum(jnp.where(order[None, :] <= order[:, None], lengths[None, :], 0), 1)
    starts = ends - lengths
    at = jnp.arange(length, dtype=jnp.int32)
    segment = jnp.sum((at[:, None] >= ends[None, :]).astype(jnp.int32), 1)
    owned = segment[:, None] == order[None, :]
    places = at - jnp.sum(jnp.where(owned, starts[None, :], 0), 1)
    live = segment < pieces - 1
    allowed = (
        (segment[:, None] == segment[None, :])
        & (at[None, :] <= at[:, None])
        & (live[None, :] | (at[:, None] == at[None, :]))
    )
    return places, live, allowed


def tie(v, *after):
    return lax.optimization_barrier((v, *after))[0]


def level(a, b, *after):
    return lax.optimization_barrier((a, b, *after))[:2]


ANY = pl.BlockSpec(memory_space=pl.ANY)
BIG = pltpu.CompilerParams(vmem_limit_bytes=56 << 20)


def cost(flops, moved, hard=0):
    return pl.CostEstimate(flops=int(flops), bytes_accessed=int(moved), transcendentals=int(hard))


def like(*shape, dtype=BF):
    return jax.ShapeDtypeStruct(shape, dtype)


def load_parts(parts, spots, base, whole, sems):
    return [
        pltpu.make_async_copy(
            ref, whole.at[pl.ds(pl.multiple_of(spots[base + i], 16), ref.shape[0])], sems.at[i]
        )
        for i, ref in enumerate(parts)
    ]


def column(row):
    n = row.shape[1]
    return jnp.broadcast_to(row, (n, n)).T[:, :1]


def turn(v, cosine, sine):
    lane = lax.broadcasted_iota(jnp.int32, v.shape, 1) % HEAD
    other = jnp.where(lane < HEAD // 2, pltpu.roll(v, 96, 1), pltpu.roll(v, 32, 1))
    return v * cosine + other * sine


def twice(v, odd):
    low = lax.broadcasted_iota(jnp.int32, v.shape, 1) < HEAD
    return jnp.where(low != odd, v, pltpu.roll(v, HEAD, 1))


def softmax_rows(q3, keys, allowed3):
    s = jnp.where(allowed3, mm_nt(q3, keys) * score_scale, mask_fill)
    e = jnp.exp(s - jnp.max(s, -1, keepdims=True))
    return e / jnp.sum(e, -1, keepdims=True)


def project_columns(cols, inverse, gain, weights, kind):
    length, dh = cols.shape
    widths = [w.shape[1] for w in weights]
    tile = 512
    counts = [w // tile for w in widths]
    first = [sum(counts[:i]) for i in range(len(counts))]
    total = sum(widths)

    def body(c, inv, g, wq, wk, wv, out, normed):
        i = pl.program_id(0)

        @pl.when(i == 0)
        def _():
            normed[...] = narrow(wide(c[...]) * column(inv[...]) * wide(narrow(g[...])))

        def go(w):
            out[...] = mm(normed[...], narrow(w[...])).astype(kind)

        for ref, a, n in zip((wq, wk, wv), first, counts):
            pl.when((i >= a) & (i < a + n))(lambda ref=ref: go(ref))

    whole = lambda a: pl.BlockSpec(a.shape, lambda i: (0, 0))
    strip = lambda a, n: pl.BlockSpec((dh, tile), lambda i: (0, jnp.clip(i - a, 0, n - 1)))
    return pl.pallas_call(
        body,
        grid=(sum(counts),),
        in_specs=[whole(v) for v in (cols, inverse, gain)]
        + [strip(a, n) for a, n in zip(first, counts)],
        out_specs=[pl.BlockSpec((length, tile), lambda i: (0, i)), whole(cols)],
        out_shape=[like(length, total, dtype=kind), like(length, dh)],
        compiler_params=BIG,
        cost_estimate=cost(2 * length * dh * total, 4 * dh * total),
        name="project_columns",
    )(cols, inverse, gain, *weights)


def attend(sums, tables, tokens, gain_two, router, chosen, out_parts, spots, base, heads, kv_heads):
    length, width = tokens.shape
    group = heads // kv_heads
    fq, fk = heads * HEAD, kv_heads * HEAD
    total = fq + 2 * fk
    n_sum, n_out = len(sums), len(out_parts)

    def body(spots, *refs):
        parts, refs = refs[:n_sum], refs[n_sum:]
        cosine, sine, allowed, live, tok, gain, rt, pick = refs[:8]
        outs = refs[8 : 8 + n_out]
        qkv_o, att_o, mid_o, norm_o, gate_o, w_out, sems = refs[8 + n_out :]
        copies = load_parts(outs, spots, base, w_out, sems)
        for copy in copies:
            copy.start()
        cos, sin = cosine[...], sine[...]

        def block(j):
            at = slice(j * 128, j * 128 + 128)
            v = wide(parts[0][:, at])
            for p in parts[1:]:
                v = v + wide(p[:, at])
            return at, v

        keys, values, q = [], [], []
        for j in range(fq // 128):
            at, v = block(j)
            v = narrow(turn(v, cos, sin))
            qkv_o[:, at] = v
            q.append(v)
        for j in range(fk // 128):
            at, v = block(fq // 128 + j)
            v = turn(v, cos, sin)
            qkv_o[:, at] = narrow(v)
            keys += [narrow(twice(v, False)), narrow(twice(v, True))]
        for j in range(fk // 128):
            at, v = block((fq + fk) // 128 + j)
            qkv_o[:, at] = narrow(v)
            values += [narrow(twice(v, False)), narrow(twice(v, True))]
        low = lax.broadcasted_iota(jnp.int32, (length, 128), 1) < HEAD
        ok = jnp.concatenate([allowed[...] > 0] * group)
        alive = column(live[...]) > 0
        done = {}
        zero = jnp.zeros((length, 128), BF)
        for g in range(kv_heads):
            hs = range(g * group, (g + 1) * group)
            q3 = jnp.concatenate([jnp.where(low != bool(h % 2), q[h // 2], zero) for h in hs])
            a = narrow(softmax_rows(q3, keys[g], ok))
            ctx = mm(a, values[g])
            for n, h in enumerate(hs):
                done[h] = ctx[n * length : (n + 1) * length]
                if h % 2:
                    both = jnp.where(low, done.pop(h - 1), done.pop(h))
                    att_o[:, h // 2 * 128 : h // 2 * 128 + 128] = narrow(
                        jnp.where(alive, both, 0.0)
                    )
        for copy in copies:
            copy.wait()
        mid = wide(tok[...]) + mm(att_o[...], w_out[...])
        mid_o[...] = mid
        inverse = lax.rsqrt(jnp.mean(mid * mid, -1, keepdims=True) + norm_eps)
        normed = narrow(mid * inverse * gain[...])
        norm_o[...] = normed
        yes = pick[...] > 0
        logits = jnp.where(yes, mm_nt(normed, rt[...]), mask_fill)
        up = jnp.where(yes, jnp.exp(logits - jnp.max(logits, -1, keepdims=True)), 0.0)
        gate_o[...] = up / jnp.sum(up, -1, keepdims=True)

    given = (*sums, *tables, tokens, gain_two, router, chosen)
    whole = [pl.BlockSpec(memory_space=pltpu.VMEM)] * len(given)
    return pl.pallas_call(
        body,
        in_specs=[pl.BlockSpec(memory_space=pltpu.SMEM)] + whole + [ANY] * n_out,
        out_shape=[
            like(length, total),
            like(length, fq),
            like(length, width, dtype=F32),
            like(length, width),
            like(length, router.shape[0], dtype=F32),
        ],
        scratch_shapes=[
            pltpu.VMEM((fq, width), BF),
            pltpu.SemaphoreType.DMA((n_out,)),
        ],
        compiler_params=BIG,
        cost_estimate=cost(
            2 * length * fq * width + 4 * heads * length * length * 128,
            2 * fq * width + 12 * length * total,
            heads * length * length,
        ),
        name="attend",
    )(spots, *given, *out_parts)


def second_norm_back(sums, gates, router, mid, gain_two, cotangent, normed, experts):
    length, width = mid.shape
    tail = router.shape[0]

    def body(a, b, c, gate_r, rt, mid_r, gain, cot, norm, mid_o, out_o):
        ends = wide(a[:, width:]) + wide(b[:, width:]) + wide(c[:, width:])
        grad = ends + pltpu.roll(ends, tail // 2, 1)
        gate = gate_r[...]
        chosen = gate * (grad - jnp.sum(gate * grad, -1, keepdims=True))
        logit = narrow(chosen)
        n2g = wide(a[:, :width]) + wide(b[:, :width]) + wide(c[:, :width]) + mm(logit, rt[...])
        m = mid_r[...]
        inverse = lax.rsqrt(jnp.mean(m * m, -1, keepdims=True) + norm_eps)
        scaled = m * inverse
        du = n2g * gain[...]
        out = wide(cot[...]) + inverse * (
            du - scaled * jnp.mean(du * scaled, -1, keepdims=True)
        )
        mid_o[...] = out
        out_o[:length] = narrow(out)
        out_o[length : length + experts] = narrow(mm_tn(logit, norm[...])[:experts])
        gain_row = jnp.sum(n2g * scaled, 0, keepdims=True)
        out_o[length + experts :] = narrow(jnp.broadcast_to(gain_row, (16, width)))

    return pl.pallas_call(
        body,
        out_shape=[like(length, width, dtype=F32), like(length + experts + 16, width)],
        compiler_params=BIG,
        cost_estimate=cost(6 * length * width * tail, 20 * length * width),
        name="second_norm_back",
    )(*sums, gates, router, mid, gain_two, cotangent, normed)


def attend_back(qkv, tables, branch, out_parts, spots, base, heads, kv_heads):
    length, width = tables[0].shape[0], branch.shape[1]
    group = heads // kv_heads
    fq, fk = heads * HEAD, kv_heads * HEAD
    total = fq + 2 * fk
    n_out = len(out_parts)

    def body(spots, qkv_r, cosine, sine, allowed, live, br, *refs):
        outs = refs[:n_out]
        grads, w_out, sems = refs[n_out:]
        copies = load_parts(outs, spots, base, w_out, sems)
        for copy in copies:
            copy.start()
        cos, sin = cosine[...], -sine[...]
        low = lax.broadcasted_iota(jnp.int32, (length, 128), 1) < HEAD
        ok = jnp.concatenate([allowed[...] > 0] * group)
        zero = jnp.zeros((length, 128), BF)
        q = [qkv_r[:, j * 128 : j * 128 + 128] for j in range(fq // 128)]
        keys, values = [], []
        for store, left in ((keys, fq), (values, fq + fk)):
            for j in range(fk // 128):
                v = wide(qkv_r[:, left + j * 128 : left + j * 128 + 128])
                store += [narrow(twice(v, False)), narrow(twice(v, True))]
        for copy in copies:
            copy.wait()
        cg = narrow(jnp.where(column(live[...]) > 0, mm_nt(br[:length], w_out[...]), 0.0))
        done, fold = {}, {}

        def put(at, v, rotate):
            v = turn(v, cos, sin) if rotate else v
            grads[:, at * 128 : at * 128 + 128] = narrow(v)

        for g in range(kv_heads):
            hs = range(g * group, (g + 1) * group)
            pick = lambda src: jnp.concatenate(
                [jnp.where(low != bool(h % 2), src(h // 2), zero) for h in hs]
            )
            q3 = pick(lambda j: q[j])
            c3 = pick(lambda j: cg[:, j * 128 : j * 128 + 128])
            a = softmax_rows(q3, keys[g], ok)
            ag = mm_nt(c3, values[g])
            sg = narrow(a * (ag - jnp.sum(a * ag, -1, keepdims=True)))
            vg = mm_tn(narrow(a), c3)
            kg = score_scale * mm_tn(sg, q3)
            qg = score_scale * mm(sg, keys[g])
            fold[g] = (kg + pltpu.roll(kg, HEAD, 1), vg + pltpu.roll(vg, HEAD, 1))
            for n, h in enumerate(hs):
                done[h] = qg[n * length : (n + 1) * length]
                if h % 2:
                    put(h // 2, jnp.where(low, done.pop(h - 1), done.pop(h)), True)
            if g % 2:
                (ka, va), (kb, vb) = fold.pop(g - 1), fold.pop(g)
                put(fq // 128 + g // 2, jnp.where(low, ka, kb), True)
                put((fq + fk) // 128 + g // 2, jnp.where(low, va, vb), False)

    vm = pl.BlockSpec(memory_space=pltpu.VMEM)
    return pl.pallas_call(
        body,
        in_specs=[pl.BlockSpec(memory_space=pltpu.SMEM)] + [vm] * 6 + [ANY] * n_out,
        out_shape=like(length, total),
        scratch_shapes=[pltpu.VMEM((fq, width), BF), pltpu.SemaphoreType.DMA((n_out,))],
        compiler_params=BIG,
        cost_estimate=cost(
            2 * length * fq * width + 12 * heads * length * length * 128,
            2 * fq * width + 8 * length * total,
            heads * length * length,
        ),
        name="attend_back",
    )(spots, qkv, *tables, branch, *out_parts)


def ring_columns(v, at, base, n, scratch, out):
    per = v.shape[1] // n
    scratch[...] = wide(v).T
    for i in range(n):
        block = scratch[pl.ds(pl.multiple_of(at[base + i] * per, 8), per)]
        out[i * per : (i + 1) * per] = narrow(block)


def out_gradient(attended, branches, total, spots, base, n):
    length, dh = attended[0].shape
    width = branches[0].shape[1]
    tile = 512

    def body(at, aa, ab, ba, bb, own, sib, scratch, lhs):
        @pl.when(pl.program_id(0) == 0)
        def _():
            ring_columns(jnp.concatenate([aa[...], ab[...]]), at, base, n, scratch, lhs)

        d = narrow(mm(lhs[...], jnp.concatenate([ba[...], bb[...]])))
        own[...], sib[...] = d[: dh // 2], d[dh // 2 :]

    whole = pl.BlockSpec((length, dh), lambda i, at: (0, 0))
    return pl.pallas_call(
        body,
        grid_spec=pltpu.PrefetchScalarGridSpec(
            num_scalar_prefetch=1,
            grid=(width // tile,),
            in_specs=[whole, whole] + [pl.BlockSpec((length, tile), lambda i, at: (0, i))] * 2,
            out_specs=[pl.BlockSpec((dh // 2, tile), lambda i, at: (0, i))] * 2,
            scratch_shapes=[
                pltpu.VMEM((dh, 2 * length), F32), pltpu.VMEM((dh, 2 * length), BF),
            ],
        ),
        out_shape=[like(dh // 2, total)] * 2,
        compiler_params=BIG,
        cost_estimate=cost(4 * length * dh * width, 2 * dh * width),
        name="out_gradient",
    )(spots, *attended, *branches)


def projection_gradient(
    grads, low, normed, cols, inverses, small, begun, skip, spots, base, side, n, experts
):
    length, total = grads[0].shape
    dh = low.shape[0]
    tile = 512
    steps, last = total // tile, experts + 16

    def body(at, ga, gb, w, na, nb, ca, cb, ia, ib, sa, sb, _0, _1, own, sib, n1a, n1b, scratch, lhs, acc, tiny):
        i = pl.program_id(0)

        @pl.when(i == 0)
        def _():
            ring_columns(jnp.concatenate([na[...], nb[...]]), at, base, n, scratch, lhs)
            acc[...] = jnp.zeros_like(acc)

        @pl.when(i < steps)
        def _():
            g = jnp.concatenate([ga[...], gb[...]])
            d = narrow(mm(lhs[...], g))
            own[...], sib[...] = d[: dh // 2], d[dh // 2 :]
            acc[...] += mm_nt(g, w[...])

        @pl.when(i == steps)
        def _():
            n1 = acc[...]
            n1a[...], n1b[...] = n1[:length], narrow(n1[length:])
            gain = n1[:length] * (wide(ca[...]) * column(ia[...])) + n1[length:] * (
                wide(cb[...]) * column(ib[...])
            )
            tiny[...] = jnp.zeros_like(tiny)
            tiny[:last] = wide(sa[...]) + wide(sb[...])
            row = jnp.sum(gain, 0, keepdims=True)
            tiny[experts + 8 : last] = jnp.broadcast_to(row, (8, dh))
            ring_columns(tiny[...], at, base, n, scratch.at[:, :128], lhs.at[:, :128])
            own[:, :128], sib[:, :128] = lhs[: dh // 2, :128], lhs[dh // 2 :, :128]

    whole = lambda a: pl.BlockSpec(a.shape, lambda i, at: (0, 0))
    strip = lambda a: pl.BlockSpec(
        (a.shape[0], tile), lambda i, at: (0, jnp.minimum(i, steps - 1))
    )
    out = pl.BlockSpec((dh // 2, tile), lambda i, at: (0, skip // tile + i))
    shapes = [like(*begun[0].shape)] * 2 + [like(length, dh, dtype=F32), like(length, dh)]
    return pl.pallas_call(
        body,
        grid_spec=pltpu.PrefetchScalarGridSpec(
            num_scalar_prefetch=1,
            grid=(steps + 1,),
            in_specs=[strip(grads[0]), strip(grads[1]), strip(low)]
            + [whole(v) for v in (*normed, *cols, *inverses)]
            + [pl.BlockSpec((last, dh), lambda i, at: (length // last, at[side]))] * 2
            + [ANY, ANY],
            out_specs=[out, out, whole(shapes[2]), whole(shapes[3])],
            scratch_shapes=[
                pltpu.VMEM((dh, 2 * length), F32),
                pltpu.VMEM((dh, 2 * length), BF),
                pltpu.VMEM((2 * length, dh), F32),
                pltpu.VMEM((128, dh), F32),
            ],
        ),
        out_shape=shapes,
        input_output_aliases={12: 0, 13: 1},
        compiler_params=BIG,
        cost_estimate=cost(8 * length * dh * total, 4 * dh * total),
        name="projection_gradient",
    )(spots, *grads, low, *normed, *cols, *inverses, *small, *begun)


def put_rows(pieces, spots, seats, per, widths, rows, kept=None, small=None):
    k = len(widths)
    cuts = [sum(widths[:i]) for i in range(k + 1)]
    given = list(kept or ())
    closing = small is not None
    plain = k - 1 if closing else k
    flat = [(p, i, at) for p, places in enumerate(seats) for i, at in enumerate(places)]
    n, m = len(flat), len(pieces)

    def body(at_ref, *refs):
        src, refs = refs[:m], refs[m:]
        before, refs = refs[: len(given)], refs[len(given) :]
        outs, refs = refs[:plain], refs[plain:]
        if closing:
            router, moe, attn, refs = *refs[:3], refs[3:]
            table, sem, refs = *refs[:2], refs[2:]
            fetch = pltpu.make_async_copy(before[-1], table, sem)
            fetch.start()
        held, sems = refs[:plain], refs[plain]
        copies = []
        for j, (p, i, at) in enumerate(flat):
            row = pl.multiple_of(at_ref[at] * per, 8)
            for w in range(plain):
                held[w][j * per : (j + 1) * per] = wide(
                    src[p][i * per : (i + 1) * per, cuts[w] : cuts[w + 1]]
                )
                copy = pltpu.make_async_copy(
                    held[w].at[pl.ds(j * per, per)], outs[w].at[pl.ds(row, per)], sems.at[j, w]
                )
                copy.start()
                copies.append(copy)
        if closing:
            fetch.wait()
            for p, i, at in flat:
                row = pl.multiple_of(at_ref[at] * per, 8)
                table[pl.ds(row, per)] = wide(src[p][i * per : (i + 1) * per, cuts[plain] :])
            across = table[...].T
            router[...] = across[:small]
            moe[...], attn[...] = across[small], across[small + 8]
        for copy in copies:
            copy.wait()

    vm = pl.BlockSpec(memory_space=pltpu.VMEM)
    out_specs = [ANY] * plain
    out_shape = [like(rows, w, dtype=F32) for w in widths[:plain]]
    scratch = [pltpu.VMEM((n * per, w), F32) for w in widths[:plain]]
    scratch += [pltpu.SemaphoreType.DMA((n, plain))]
    if closing:
        out_specs += [vm] * 3
        out_shape += [like(small, rows, dtype=F32)] + [like(rows, dtype=F32)] * 2
        scratch = [pltpu.VMEM((rows, widths[-1]), F32), pltpu.SemaphoreType.DMA] + scratch
    return pl.pallas_call(
        body,
        in_specs=[pl.BlockSpec(memory_space=pltpu.SMEM)] + [vm] * m + [ANY] * len(given),
        out_specs=out_specs,
        out_shape=out_shape,
        input_output_aliases={1 + m + i: i for i in range(plain if given else 0)},
        scratch_shapes=scratch,
        compiler_params=BIG,
        cost_estimate=cost(n * per * cuts[-1], n * per * cuts[-1] * 6),
        name="put_rows",
    )(spots, *pieces, *given)


def expert_step(spots, base, tiles, cots, router, gate, up, down, starts, kept, start, total, apart):
    width, ffe = cots.shape[1] - router.shape[0], gate[0].shape[1]
    tail = router.shape[0]
    count = len(tiles)
    two = sum(p.shape[0] for p in tiles[0])
    block = two // 2
    n = count * block
    pieces = [p for t in tiles for p in t]
    parts = [*gate, *up, *down]
    sets, m = [len(gate), len(up), len(down)], len(pieces)
    k = sum(sets)

    def body(spot, ca, cb, rt, *refs):
        xs, ws = refs[:m], refs[m : m + k]
        products = refs[-10 - n_out : -10]
        x_o, hid_o, pre_o, rg_o = refs[-10:-6]
        held, gw, uw, dw, sems, wsems = refs[-6:]
        i = pl.program_id(0)
        moves, at, j = [], 0, 0
        for t in tiles:
            group = []
            for p in t:
                dst = held.at[pl.ds(at, p.shape[0])]
                group.append(pltpu.make_async_copy(xs[j], dst, sems.at[j]))
                at, j = at + p.shape[0], j + 1
            moves.append(group)
        loads = []
        first = 0
        for size, whole in zip(sets, (gw, uw, dw)):
            part = slice(first, first + size)
            loads += load_parts(ws[part], spot, starts + first, whole, wsems.at[pl.ds(first, size)])
            first += size

        @pl.when(i == 0)
        def _():
            for copy in [*moves[0], *loads]:
                copy.start()
            for copy in [c for g in moves[1:] for c in g]:
                copy.start()

        for t in range(count):

            @pl.when(i == t)
            def _():
                for copy in moves[t]:
                    copy.wait()

        @pl.when(i == 0)
        def _():
            for copy in loads:
                copy.wait()

        x = held[pl.ds(pl.multiple_of(i * two, two), two)]
        cm = jnp.concatenate([ca[...], cb[...]])
        cot, chosen = cm[:, :width], cm[:, width:] > 0
        x_o[...] = x
        logits = jnp.where(chosen, mm_nt(x, rt[...]), mask_fill)
        top = jnp.max(logits, -1, keepdims=True)
        raised = jnp.where(chosen, jnp.exp(logits - top), 0.0)
        mine = lax.broadcasted_iota(jnp.int32, raised.shape, 1)
        weight = jnp.sum(jnp.where(mine == spot[0], raised, 0.0), -1, keepdims=True)
        weight = narrow(weight / jnp.sum(raised, -1, keepdims=True))
        gate_pre, up_pre = mm(x, gw[...]), mm(x, uw[...])
        sg = jax.nn.sigmoid(gate_pre)
        silu = gate_pre * sg
        hidden = narrow(silu * up_pre)
        hid_o[...] = hidden
        result_grad = weight * cot
        rg_o[...] = result_grad
        result = narrow(mm(hidden, dw[...]))
        mix = weight * result
        gate_grad = jnp.sum(wide(result) * wide(cot), -1, keepdims=True)
        hidden_grad = mm_nt(result_grad, dw[...])
        gpg = narrow(hidden_grad * up_pre * sg * (1.0 + gate_pre * (1.0 - sg)))
        upg = narrow(hidden_grad * silu)
        pre_o[:, :ffe], pre_o[:, ffe:] = gpg, upg
        row = narrow(mm_nt(gpg, gw[...]) + mm_nt(upg, uw[...]))
        high = wide(narrow(gate_grad))
        ends = jnp.where(mine == spot[0], high, 0.0)
        ends = narrow(jnp.where(mine == spot[0] + tail // 2, gate_grad - high, ends))

        def store(mix_a, mix_b, row_a, row_b):
            mix_a[...], mix_b[...] = mix[:block], mix[block:]
            row_a[:, :width], row_b[:, :width] = row[:block], row[block:]
            row_a[:, width:], row_b[:, width:] = ends[:block], ends[block:]

        if apart:
            pl.when(i == 0)(lambda: store(*products[:4]))
            pl.when(i > 0)(lambda: store(*products[4:]))
        else:
            store(*products)

    gap = 1 if apart else 0
    step = lambda w: pl.BlockSpec((block, w), lambda i, s: (jnp.maximum(i - gap, 0), 0))
    once = lambda w: pl.BlockSpec((block, w), lambda i, s: (0, 0))
    four = (width, width, width + tail, width + tail)
    keep = lambda w: pl.BlockSpec((two, w), lambda i, s: (start + i, 0))
    widths = [width, ffe, 2 * ffe, width]
    out_shape = [like(block, w) for w in four] if apart else []
    out_shape += [like(n - gap * block, w) for w in four]
    out_shape += [like(total, w) for w in widths]
    given = list(kept or ())
    before, n_out = 4 + m + k, 8 if apart else 4
    return pl.pallas_call(
        body,
        grid_spec=pltpu.PrefetchScalarGridSpec(
            num_scalar_prefetch=1,
            grid=(count,),
            in_specs=[
                pl.BlockSpec((block, width + tail), lambda i, s: (s[base + i], 0)),
                pl.BlockSpec((block, width + tail), lambda i, s: (s[base + count + i], 0)),
                pl.BlockSpec(router.shape, lambda i, s: (0, 0)),
            ]
            + [ANY] * (m + k + len(given)),
            out_specs=[once(w) for w in (four if apart else ())]
            + [step(w) for w in four]
            + [keep(w) for w in widths],
            scratch_shapes=[
                pltpu.VMEM((count * two, width), BF),
                pltpu.VMEM((width, ffe), BF),
                pltpu.VMEM((width, ffe), BF),
                pltpu.VMEM((ffe, width), BF),
                pltpu.SemaphoreType.DMA((m,)),
                pltpu.SemaphoreType.DMA((k,)),
            ],
        ),
        out_shape=out_shape,
        input_output_aliases={before + i: n_out + i for i in range(len(given))},
        compiler_params=BIG,
        cost_estimate=cost(
            24 * n * width * ffe, 6 * width * ffe + n * width * 28, 2 * n * ffe
        ),
        name="expert_step",
    )(spots, cots, cots, router, *pieces, *parts, *given)


class Links:
    def __init__(self):
        self.n = lax.axis_size("dp")
        self.e = lax.axis_size("expert")
        self.chips = self.e // 2
        order = list(range(self.chips))
        if self.n == 2 and self.chips == 8:
            order = [0, 2, 4, 6, 7, 5, 3, 1]
        self.order = order
        self.x = lax.axis_index("dp")
        self.me = lax.axis_index("expert")

    def table(self, of):
        rows, begins = [], {}
        for x in range(self.n):
            for me in range(self.e):
                lists, row = of(x, me, self.order.index(me // 2)), []
                for name, values in lists.items():
                    begins[name] = len(row)
                    row += values
                rows.append(row)
        at = self.x * self.e + self.me
        whole = jnp.asarray(np.array(rows, np.int32))
        return lax.dynamic_slice_in_dim(whole, at, 1, 0).reshape(-1), begins

    def sibling(self, v):
        return lax.ppermute(v, "expert", [(i, i ^ 1) for i in range(self.e)])

    def flip(self, v, bit):
        return lax.ppermute(v, "expert", [(i, i ^ bit) for i in range(self.e)])

    def ring(self, v, step):
        c, o = self.chips, self.order
        pairs = [(o[k] * 2 + l, o[(k + step) % c] * 2 + l) for k in range(c) for l in (0, 1)]
        return lax.ppermute(v, "expert", pairs)

    def gather(self, block, waits=()):
        c = self.chips
        half = block.shape[0] // 2
        got = {0: block}
        up = down = block
        for s in range(1, c // 2):
            up, down = level(up, down, *(waits[s] if s < len(waits) else ()))
            up, down = self.ring(up, 1), self.ring(down, -1)
            got[c - s], got[s] = up, down
        up, down = level(up, down)
        far = (self.ring(up[:half], 1), self.ring(down[half:], -1))
        return got, far

    def scatter(self, s, far, waits=(), steps=None):
        c = self.chips
        half = far[0].shape[0]
        up, down = self.ring(far[0], 1), self.ring(far[1], -1)
        steps = [] if steps is None else steps
        steps.append((up, down))
        r = c // 2 - 1
        a, b = s(r, None), s(c - r, None)
        up = jnp.concatenate([add_low(up, a[:half]), a[half:]])
        down = jnp.concatenate([b[:half], add_low(down, b[half:])])
        for r in range(c // 2 - 2, -1, -1):
            up, down = level(up, down, *(waits(len(steps)) if waits else ()))
            up, down = self.ring(up, 1), self.ring(down, -1)
            steps.append((up, down))
            if r:
                last = steps[-2]
                up, down = add_low(up, s(r, last)), add_low(down, s(c - r, last))
        return (s(0, up), up, down), steps

    def swap(self, v):
        return lax.ppermute(v, "dp", [(0, 1), (1, 0)])

    def pick(self, v, other, axis):
        size = v.shape[axis] // self.n
        at = (1 - self.x if other else self.x) * size
        return lax.dynamic_slice_in_dim(v, at, size, axis)

    def both(self, own, got, axis):
        return jnp.where(
            self.x == 0,
            jnp.concatenate([own, got], axis),
            jnp.concatenate([got, own], axis),
        )

    def columns(self, v):
        if self.n == 2:
            return jnp.concatenate([self.pick(v, False, 1), self.swap(self.pick(v, True, 1))])
        return lax.all_to_all(v, "dp", split_axis=1, concat_axis=0, tiled=True)

    def columns_back(self, v):
        if self.n == 2:
            t = v.shape[0] // 2
            return self.both(v[:t], wide(self.swap(narrow(v[t:]))), 1)
        return wide(lax.all_to_all(narrow(v), "dp", split_axis=0, concat_axis=1, tiled=True))

    def rows(self, v):
        if self.n == 2:
            return jnp.concatenate([v, self.swap(v)])
        return lax.all_gather(v, "dp", axis=0, tiled=True)

    def sum_back(self, v):
        if self.n == 2:
            t = v.shape[0] // 2
            return v[:t] + wide(self.swap(narrow(v[t:])))
        return wide(lax.psum_scatter(narrow(v), "dp", scatter_dimension=0, tiled=True))

    def whole(self, v, axis):
        if self.n == 2:
            return self.both(v, self.swap(v), axis)
        return lax.all_gather(v, "dp", axis=axis, tiled=True)

    def shard_sum(self, v, axis):
        return wide(lax.psum_scatter(narrow(v), "dp", scatter_dimension=axis, tiled=True))

    def parts(self, w):
        if self.n == 2:
            return [w, self.swap(w)]
        return [lax.all_gather(w, "dp", axis=0, tiled=True)]

    def parts_by_four(self, w, after):
        if self.n != 2:
            return self.parts(narrow(w))
        part = w.shape[0] // 4
        a = self.swap(narrow(lax.dynamic_slice_in_dim(w, self.me % 4 * part, part, 0)))
        w, a = narrow(tie(w, after)), tie(a, after)
        b = self.flip(a, 2)
        return [w, a, b, self.flip(a, 1), self.flip(b, 1)]


def wide_sum(v):
    out = wide(v[0])
    for w in v[1:]:
        out = out + wide(w)
    return out


def shards(
    tokens, cotangent, lengths, routes, gain_attn, w_query, key_weight, value_weight,
    w_out, gain_moe, w_router, w_gate, w_up, w_down,
):
    net = Links()
    c, pair = net.chips, net.n == 2
    length, width = tokens.shape
    dh = gain_attn.shape[0]
    heads, kv_heads = w_query.shape[1] // HEAD, key_weight.shape[1] // HEAD
    fq, fk = w_query.shape[1], key_weight.shape[1]
    experts = w_router.shape[1]
    tail = 128
    far, half = c // 2, length // 2

    if pair:
        away = net.pick(tokens, True, 1)
        stream = wide(tie(tokens, away))
    else:
        stream = wide(tokens)
    inv_one = lax.rsqrt(jnp.mean(stream * stream, -1, keepdims=True) + norm_eps)
    if pair:
        cols = (net.pick(tokens, False, 1), net.swap(away))
        inv_row = inv_one.reshape(1, length)
        inverses = (inv_row, net.swap(inv_row))
        weights = (w_query, key_weight, value_weight)
        other, normed_other = project_columns(cols[1], inverses[1], gain_attn[None], weights, BF)
        arrived = net.swap(other)
        own, normed_own = project_columns(
            tie(cols[0], other), inverses[0], gain_attn[None], weights, F32
        )
        normed_cols = (normed_own, normed_other)
        sums = (own, arrived)
        w_qkv = jnp.concatenate(
            [narrow(tie(w, own)) for w in (w_query, key_weight, value_weight)], 1
        )
    else:
        scaled_cols = wide(net.columns(tokens)) * net.rows(inv_one.reshape(1, length)).reshape(-1, 1)
        normed_cols = narrow(scaled_cols * wide(narrow(gain_attn))[None, :])
        w_qkv = jnp.concatenate([narrow(w_query), narrow(key_weight), narrow(value_weight)], 1)
        arrived = net.sum_back(mm(normed_cols, w_qkv))
        sums, own, other = (arrived,), arrived, arrived

    near = [0] + [r for s in range(1, far - 1) for r in (s, c - s)]
    last = [far, far - 1, c - far + 1]
    ffe = w_down.shape[1]

    def numbers(x, me, place):
        at = lambda r, l: net.order[(place + r) % c] * 2 + (me % 2 ^ l)
        seat = lambda r, l: (place + r) % c * 2 + (me % 2 ^ l)
        y, q, part = 1 - x, me % 4, dh // 4
        return {
            "me": [me],
            "x": [x],
            "near": [at(r, l) for l in (0, 1) for r in near],
            "last": [at(r, l) for l in (0, 1) for r in last],
            "expert": [x * dh, y * dh, y * dh + dh // 2, x * dh, y * dh, x * ffe, y * ffe]
            if pair
            else [0, 0, 0],
            "out": [x * dh] + [y * dh + (q ^ z) * part for z in (0, 2, 1, 3)] if pair else [0],
            "seats": [seat(r, l) for l in (0, 1) for r in range(c)],
        }

    spots, begins = net.table(numbers)
    small = jnp.concatenate(
        [narrow(tie(w_router, inv_one)).T, narrow(gain_attn)[None], narrow(gain_moe)[None]], 0
    )
    small = net.whole(small, 1)
    gain_one, gain_two = wide(small[experts])[None], wide(small[experts + 1])[None]
    router = jnp.pad(small[:experts], ((0, tail - experts), (0, 0)))
    out_parts = net.parts_by_four(tie(w_out, inv_one), other)
    hits = routes[:, :, None] == jnp.arange(tail, dtype=jnp.int32)[None, None, :]
    chosen = narrow(jnp.any(hits, 1))
    cot_all = lax.all_gather(
        jnp.concatenate([tie(cotangent, inv_one), chosen], 1), "expert", axis=0, tiled=True
    )
    if pair:
        low = narrow(tie(w_gate, inv_one)[0])
        gate_parts = [low, net.swap(low[: dh // 2]), net.swap(tie(low[dh // 2 :], out_parts[2]))]
        up_parts, down_parts = (
            net.parts(tie(narrow(tie(w, own)[0]), out_parts[2])) for w in (w_up, w_down)
        )
        hold = (w_qkv, gate_parts[1])
        waits = ((), (), gate_parts[2:], up_parts[1:])
    else:
        gate_parts, up_parts, down_parts = (net.parts(narrow(w[0])) for w in (w_gate, w_up, w_down))
        hold, waits = (w_qkv,), ()

    places, live, allowed = layout(lengths[0], length)
    inner = jnp.arange(128, dtype=jnp.int32) % (HEAD // 2)
    angles = places.astype(F32)[:, None] * (rope_base ** (-inner.astype(F32) * 2.0 / HEAD))[None]
    sign = jnp.where(jnp.arange(128) % HEAD < HEAD // 2, -1.0, 1.0)[None]
    tables = (
        jnp.cos(angles), jnp.sin(angles) * sign, allowed.astype(F32), live.astype(F32)[None],
    )
    qkv, attended, mid, normed_two, gates = attend(
        sums, tables, tie(tokens, *hold), gain_two, router, chosen, out_parts, spots,
        begins["out"], heads, kv_heads,
    )

    got, ends = net.gather(normed_two, waits)
    beside = {r: net.sibling(v) for r, v in got.items()}
    kept, start, made = None, 0, []
    for g, name in ((near, "near"), (last, "last")):
        if made:
            ends = tuple(tie(v, made[0][0]) for v in ends)
            ends_beside = tuple(net.sibling(v) for v in ends)
        tiles = [(*ends, *ends_beside) if r == far else (got[r], beside[r]) for r in g]
        out = expert_step(
            spots, begins[name], tiles, cot_all, router, gate_parts, up_parts, down_parts,
            begins["expert"], kept, start, net.e * length, far in g,
        )
        kept, start = out[-4:], start + len(g)
        made += [out[i : i + 4] for i in range(0, len(out) - 4, 4)]
    after_near = made[0][0]

    def ring_sum(which, after, waits=(), steps=None):
        (a0, b0), (a2, b2), (a1, b1) = (m[which : which + 2] for m in made)
        edge = add_low(a2, net.sibling(tie(b2, *after)))
        b1 = net.sibling(b1)
        done = {}

        def block(r, then):
            group, at = (near, 0) if r in near else (last[1:], 1)
            if at not in done:
                done[at] = add_low(a1, b1) if at else add_low(a0, net.sibling(tie(b0, *then)))
            i = group.index(r)
            return done[at][i * length : (i + 1) * length]

        return net.scatter(block, (edge[:half], edge[half:]), waits, steps)

    rows_all, hid_all, pre_all, rg_all = kept
    ffe = w_gate.shape[2]
    if pair:
        part = net.swap(tie(net.pick(attended, True, 1), after_near))
        halves = lambda v: (net.pick(v, False, 0), narrow(net.pick(v, True, 0)))
        back, steps = ring_sum(2, ())
        d_pre = halves(mm_tn(tie(rows_all, *steps[1]), pre_all))
        back = (tie(back[0], d_pre[1]), *back[1:])
    else:
        back, steps = ring_sum(2, ())

    mid_grad, branch = second_norm_back(
        back, gates, router, mid, gain_two, cotangent, normed_two, experts
    )

    mixed, mix_steps = ring_sum(0, steps[-2])
    mixed = narrow(mid + wide_sum(mixed))

    base = begins["seats"]
    seats = spots[base : base + net.e]
    per = dh // net.e
    if not pair:
        slot = jnp.arange(dh, dtype=jnp.int32)
        source = jnp.sum(
            jnp.where(slot[:, None] // per == jnp.arange(net.e)[None, :], seats[None, :], 0), 1
        ) * per + slot % per
        perm = (slot[:, None] == source[None, :]).astype(BF)

    def all_sum(own, sib, widths, small, ready, last_mix):
        at = slice(far * per, (far + 1) * per)
        edge = add_low(own[at], net.sibling(sib[at]))
        s = []

        def block(r, after):
            if not s:
                s.append(add_low(own, net.sibling(sib)))
            return s[0][r * per : (r + 1) * per]

        cut = per // 2
        total, _ = net.scatter(
            block, (edge[:cut], edge[cut:]), lambda k: last_mix if k == 1 else ()
        )
        up = down = held = narrow(wide_sum(total))
        seat = lambda rs: [[base + l * c + r for r in rs] for l in (0, 1)]
        pieces = []
        for s in range(far):
            if s:
                before = [p[1] for p in pieces[max(s - 2, 0) : s - 1]]
                up, down = level(up, down, *before, *jax.tree.leaves(ready[s : s + 1]))
            rs = [s, c - s] if s else [0]
            pieces.append((held, net.sibling(held), seat(rs)))
            if s < far - 1:
                up, down = net.ring(up, 1), net.ring(down, -1)
                held = jnp.concatenate([down, up])
            else:
                up, down = net.ring(up[:cut], 1), net.ring(down[cut:], -1)
        if per % 16 == 0:
            both = [v for p in pieces for v in p[:2]]
            seats = [v for p in pieces for v in p[2]]
            kept = put_rows(both, spots, seats, per, widths, dh)
            up, down = level(up, down, kept[0], *jax.tree.leaves(ready[far:]))
        held = jnp.concatenate([up, down])
        pieces.append((held, net.sibling(held), seat([far])))
        if per % 16 == 0:
            return put_rows(pieces[-1][:2], spots, seat([far]), per, widths, dh, kept, small)
        out = jnp.zeros((dh, sum(widths)), F32)
        for a, b, seats in pieces:
            for v, ats in zip((a, b), seats):
                for i, at in enumerate(ats):
                    blk = wide(v[i * per : (i + 1) * per])
                    out = lax.dynamic_update_slice_in_dim(out, blk, spots[at] * per, 0)
        cuts = [sum(widths[:i]) for i in range(len(widths) + 1)]
        out = [out[:, a:b] for a, b in zip(cuts, cuts[1:])]
        return [*out[:-1], out[-1][:, :small].T, out[-1][:, small], out[-1][:, small + 8]]

    part_width = width + fq + 2 * fk + tail
    if pair:
        beyond = net.swap(branch)
        begun = out_gradient(
            (net.pick(attended, False, 1), part), (branch, beyond), part_width, spots,
            base, net.e,
        )

    grads = attend_back(
        qkv, tables, tie(branch, *mix_steps[0]), out_parts, spots, begins["out"], heads, kv_heads
    )
    sent = grads
    if pair:
        sent = tie(net.swap(tie(grads, beyond, part, *mix_steps[1])), *mix_steps[2])
        d_down = halves(mm_tn(tie(hid_all, *mix_steps[1]), rg_all))
        sent = tie(sent, d_down[1])
        own, sib, n1, n1_other = projection_gradient(
            (grads, sent), w_qkv, normed_cols, cols, inverses, (branch, beyond), begun, width, spots,
            base, begins["x"], net.e, experts,
        )
        n1_other = net.swap(n1_other)
        n1g = net.both(n1, wide(n1_other), 1)
    else:
        grads_all = net.rows(grads)
        d_out = mm_tn(narrow(mm(net.columns(attended), perm)), net.rows(branch[:length]))
        d_qkv = mm_tn(narrow(mm(normed_cols, perm)), grads_all)
        n1 = mm_nt(grads_all, w_qkv)
        n1g = net.columns_back(n1)
        d_small = net.shard_sum(wide(branch[length:]), 1)
        d_gain = jnp.broadcast_to(jnp.sum(n1 * scaled_cols, 0)[None], (8, dh))
        d_small = jnp.concatenate([d_small[: experts + 8], d_gain], 0)
        d_small = jnp.pad(mm(narrow(d_small), perm).T, ((0, 0), (0, tail - experts - 16)))
        d = narrow(jnp.concatenate([d_out, d_qkv, d_small], 1))
        own, sib = d[: dh // 2], d[dh // 2 :]
    scaled_one = stream * inv_one
    du = n1g * gain_one
    d_tokens = mid_grad + inv_one * (
        du - scaled_one * jnp.mean(du * scaled_one, -1, keepdims=True)
    )
    if pair:
        d_pre, d_down = (v[0] + wide(net.swap(tie(v[1], n1_other))) for v in (d_pre, d_down))
        d_gate, d_up, d_down = d_pre[None, :, :ffe], d_pre[None, :, ffe:], d_down[None]
        last_mix = mix_steps[3]
        ready = ((), (), (d_tokens, mixed), (), (d_gate, d_up, d_down))
    else:
        d_down, d_pre = (
            net.shard_sum(mm_tn(a, b), 0)[None] for a, b in ((hid_all, rg_all), (rows_all, pre_all))
        )
        d_gate, d_up = d_pre[..., :ffe], d_pre[..., ffe:]
        ready, last_mix = (), ()
    d_out, d_query, d_key, d_value, d_router, d_moe, d_attn = all_sum(
        own, sib, [width, fq, fk, fk, tail], experts, ready, last_mix
    )
    return (
        mixed,
        d_tokens,
        d_attn,
        d_query,
        d_key,
        d_value,
        d_out,
        d_moe,
        d_router.T,
        d_gate,
        d_up,
        d_down,
    )


def solution(mesh):
    rows = P(("dp", "expert"), None)
    flat, dense, routed = P("dp"), P("dp", None), P("expert", "dp", None)
    return jax.shard_map(
        shards,
        mesh=mesh,
        in_specs=(
            rows, rows, rows, rows, flat, dense, dense, dense, dense, flat, dense,
            routed, routed, routed,
        ),
        out_specs=(
            rows, rows, flat, dense, dense, dense, dense, flat, dense, routed, routed, routed,
        ),
        check_vma=False,
    )
```

```python
import jax
import jax.numpy as jnp
import numpy as np
from jax import lax
from jax.experimental import pallas as pl
from jax.experimental.pallas import tpu as pltpu
from jax.sharding import PartitionSpec as P

HEAD = 64
norm_eps = 1e-06
score_scale = 0.015625
rope_base = 10000.0
mask_fill = -1e30
BF = jnp.bfloat16
F32 = jnp.float32


def narrow(v):
    return v.astype(BF)


def wide(v):
    return v.astype(F32)


def mm(a, b):
    return jnp.dot(a, b, preferred_element_type=F32)


def mm_tn(a, b):
    return lax.dot_general(a, b, (((0,), (0,)), ((), ())), preferred_element_type=F32)


def mm_nt(a, b):
    return lax.dot_general(a, b, (((1,), (1,)), ((), ())), preferred_element_type=F32)


def add_low(a, b):
    return narrow(wide(a) + wide(b))


def layout(lengths, length):
    pieces = lengths.shape[0]
    order = jnp.arange(pieces, dtype=jnp.int32)
    ends = jnp.sum(jnp.where(order[None, :] <= order[:, None], lengths[None, :], 0), 1)
    starts = ends - lengths
    at = jnp.arange(length, dtype=jnp.int32)
    segment = jnp.sum((at[:, None] >= ends[None, :]).astype(jnp.int32), 1)
    owned = segment[:, None] == order[None, :]
    places = at - jnp.sum(jnp.where(owned, starts[None, :], 0), 1)
    live = segment < pieces - 1
    allowed = (
        (segment[:, None] == segment[None, :])
        & (at[None, :] <= at[:, None])
        & (live[None, :] | (at[:, None] == at[None, :]))
    )
    return places, live, allowed


def tie(v, *after):
    return lax.optimization_barrier((v, *after))[0]


def level(a, b, *after):
    return lax.optimization_barrier((a, b, *after))[:2]


ANY = pl.BlockSpec(memory_space=pl.ANY)
BIG = pltpu.CompilerParams(vmem_limit_bytes=56 << 20)


def cost(flops, moved, hard=0):
    return pl.CostEstimate(flops=int(flops), bytes_accessed=int(moved), transcendentals=int(hard))


def like(*shape, dtype=BF):
    return jax.ShapeDtypeStruct(shape, dtype)


def load_parts(parts, spots, base, whole, sems):
    return [
        pltpu.make_async_copy(
            ref, whole.at[pl.ds(pl.multiple_of(spots[base + i], 16), ref.shape[0])], sems.at[i]
        )
        for i, ref in enumerate(parts)
    ]


def column(row):
    n = row.shape[1]
    return jnp.broadcast_to(row, (n, n)).T[:, :1]


def turn(v, cosine, sine):
    lane = lax.broadcasted_iota(jnp.int32, v.shape, 1) % HEAD
    other = jnp.where(lane < HEAD // 2, pltpu.roll(v, 96, 1), pltpu.roll(v, 32, 1))
    return v * cosine + other * sine


def twice(v, odd):
    low = lax.broadcasted_iota(jnp.int32, v.shape, 1) < HEAD
    return jnp.where(low != odd, v, pltpu.roll(v, HEAD, 1))


def softmax_rows(q3, keys, allowed3):
    s = jnp.where(allowed3, mm_nt(q3, keys) * score_scale, mask_fill)
    e = jnp.exp(s - jnp.max(s, -1, keepdims=True))
    return e / jnp.sum(e, -1, keepdims=True)


def project_columns(cols, inverse, gain, weights, kind):
    length, dh = cols.shape
    widths = [w.shape[1] for w in weights]
    tile = 512
    counts = [w // tile for w in widths]
    first = [sum(counts[:i]) for i in range(len(counts))]
    total = sum(widths)

    def body(c, inv, g, wq, wk, wv, out, normed):
        i = pl.program_id(0)

        @pl.when(i == 0)
        def _():
            normed[...] = narrow(wide(c[...]) * column(inv[...]) * wide(narrow(g[...])))

        def go(w):
            out[...] = mm(normed[...], narrow(w[...])).astype(kind)

        for ref, a, n in zip((wq, wk, wv), first, counts):
            pl.when((i >= a) & (i < a + n))(lambda ref=ref: go(ref))

    whole = lambda a: pl.BlockSpec(a.shape, lambda i: (0, 0))
    strip = lambda a, n: pl.BlockSpec((dh, tile), lambda i: (0, jnp.clip(i - a, 0, n - 1)))
    return pl.pallas_call(
        body,
        grid=(sum(counts),),
        in_specs=[whole(v) for v in (cols, inverse, gain)]
        + [strip(a, n) for a, n in zip(first, counts)],
        out_specs=[pl.BlockSpec((length, tile), lambda i: (0, i)), whole(cols)],
        out_shape=[like(length, total, dtype=kind), like(length, dh)],
        compiler_params=BIG,
        cost_estimate=cost(2 * length * dh * total, 4 * dh * total),
        name="project_columns",
    )(cols, inverse, gain, *weights)


def attend(sums, tables, tokens, gain_two, router, chosen, out_parts, spots, base, heads, kv_heads):
    length, width = tokens.shape
    group = heads // kv_heads
    fq, fk = heads * HEAD, kv_heads * HEAD
    total = fq + 2 * fk
    n_sum, n_out = len(sums), len(out_parts)

    def body(spots, *refs):
        parts, refs = refs[:n_sum], refs[n_sum:]
        cosine, sine, allowed, live, tok, gain, rt, pick = refs[:8]
        outs = refs[8 : 8 + n_out]
        qkv_o, att_o, mid_o, norm_o, gate_o, w_out, sems = refs[8 + n_out :]
        copies = load_parts(outs, spots, base, w_out, sems)
        for copy in copies:
            copy.start()
        cos, sin = cosine[...], sine[...]

        def block(j):
            at = slice(j * 128, j * 128 + 128)
            v = wide(parts[0][:, at])
            for p in parts[1:]:
                v = v + wide(p[:, at])
            return at, v

        keys, values, q = [], [], []
        for j in range(fq // 128):
            at, v = block(j)
            v = narrow(turn(v, cos, sin))
            qkv_o[:, at] = v
            q.append(v)
        for j in range(fk // 128):
            at, v = block(fq // 128 + j)
            v = turn(v, cos, sin)
            qkv_o[:, at] = narrow(v)
            keys += [narrow(twice(v, False)), narrow(twice(v, True))]
        for j in range(fk // 128):
            at, v = block((fq + fk) // 128 + j)
            qkv_o[:, at] = narrow(v)
            values += [narrow(twice(v, False)), narrow(twice(v, True))]
        low = lax.broadcasted_iota(jnp.int32, (length, 128), 1) < HEAD
        ok = jnp.concatenate([allowed[...] > 0] * group)
        alive = column(live[...]) > 0
        done = {}
        zero = jnp.zeros((length, 128), BF)
        for g in range(kv_heads):
            hs = range(g * group, (g + 1) * group)
            q3 = jnp.concatenate([jnp.where(low != bool(h % 2), q[h // 2], zero) for h in hs])
            a = narrow(softmax_rows(q3, keys[g], ok))
            ctx = mm(a, values[g])
            for n, h in enumerate(hs):
                done[h] = ctx[n * length : (n + 1) * length]
                if h % 2:
                    both = jnp.where(low, done.pop(h - 1), done.pop(h))
                    att_o[:, h // 2 * 128 : h // 2 * 128 + 128] = narrow(
                        jnp.where(alive, both, 0.0)
                    )
        for copy in copies:
            copy.wait()
        mid = wide(tok[...]) + mm(att_o[...], w_out[...])
        mid_o[...] = mid
        inverse = lax.rsqrt(jnp.mean(mid * mid, -1, keepdims=True) + norm_eps)
        normed = narrow(mid * inverse * gain[...])
        norm_o[...] = normed
        yes = pick[...] > 0
        logits = jnp.where(yes, mm_nt(normed, rt[...]), mask_fill)
        up = jnp.where(yes, jnp.exp(logits - jnp.max(logits, -1, keepdims=True)), 0.0)
        gate_o[...] = up / jnp.sum(up, -1, keepdims=True)

    given = (*sums, *tables, tokens, gain_two, router, chosen)
    whole = [pl.BlockSpec(memory_space=pltpu.VMEM)] * len(given)
    return pl.pallas_call(
        body,
        in_specs=[pl.BlockSpec(memory_space=pltpu.SMEM)] + whole + [ANY] * n_out,
        out_shape=[
            like(length, total),
            like(length, fq),
            like(length, width, dtype=F32),
            like(length, width),
            like(length, router.shape[0], dtype=F32),
        ],
        scratch_shapes=[
            pltpu.VMEM((fq, width), BF),
            pltpu.SemaphoreType.DMA((n_out,)),
        ],
        compiler_params=BIG,
        cost_estimate=cost(
            2 * length * fq * width + 4 * heads * length * length * 128,
            2 * fq * width + 12 * length * total,
            heads * length * length,
        ),
        name="attend",
    )(spots, *given, *out_parts)


def second_norm_back(sums, gates, router, mid, gain_two, cotangent, normed, experts):
    length, width = mid.shape
    tail = router.shape[0]

    def body(a, b, c, gate_r, rt, mid_r, gain, cot, norm, mid_o, out_o):
        ends = wide(a[:, width:]) + wide(b[:, width:]) + wide(c[:, width:])
        grad = ends + pltpu.roll(ends, tail // 2, 1)
        gate = gate_r[...]
        chosen = gate * (grad - jnp.sum(gate * grad, -1, keepdims=True))
        logit = narrow(chosen)
        n2g = wide(a[:, :width]) + wide(b[:, :width]) + wide(c[:, :width]) + mm(logit, rt[...])
        m = mid_r[...]
        inverse = lax.rsqrt(jnp.mean(m * m, -1, keepdims=True) + norm_eps)
        scaled = m * inverse
        du = n2g * gain[...]
        out = wide(cot[...]) + inverse * (
            du - scaled * jnp.mean(du * scaled, -1, keepdims=True)
        )
        mid_o[...] = out
        out_o[:length] = narrow(out)
        out_o[length : length + experts] = narrow(mm_tn(logit, norm[...])[:experts])
        gain_row = jnp.sum(n2g * scaled, 0, keepdims=True)
        out_o[length + experts :] = narrow(jnp.broadcast_to(gain_row, (16, width)))

    return pl.pallas_call(
        body,
        out_shape=[like(length, width, dtype=F32), like(length + experts + 16, width)],
        compiler_params=BIG,
        cost_estimate=cost(6 * length * width * tail, 20 * length * width),
        name="second_norm_back",
    )(*sums, gates, router, mid, gain_two, cotangent, normed)


def attend_back(qkv, tables, branch, out_parts, spots, base, heads, kv_heads):
    length, width = tables[0].shape[0], branch.shape[1]
    group = heads // kv_heads
    fq, fk = heads * HEAD, kv_heads * HEAD
    total = fq + 2 * fk
    n_out = len(out_parts)

    def body(spots, qkv_r, cosine, sine, allowed, live, br, *refs):
        outs = refs[:n_out]
        grads, w_out, sems = refs[n_out:]
        copies = load_parts(outs, spots, base, w_out, sems)
        for copy in copies:
            copy.start()
        cos, sin = cosine[...], -sine[...]
        low = lax.broadcasted_iota(jnp.int32, (length, 128), 1) < HEAD
        ok = jnp.concatenate([allowed[...] > 0] * group)
        zero = jnp.zeros((length, 128), BF)
        q = [qkv_r[:, j * 128 : j * 128 + 128] for j in range(fq // 128)]
        keys, values = [], []
        for store, left in ((keys, fq), (values, fq + fk)):
            for j in range(fk // 128):
                v = wide(qkv_r[:, left + j * 128 : left + j * 128 + 128])
                store += [narrow(twice(v, False)), narrow(twice(v, True))]
        for copy in copies:
            copy.wait()
        cg = narrow(jnp.where(column(live[...]) > 0, mm_nt(br[:length], w_out[...]), 0.0))
        done, fold = {}, {}

        def put(at, v, rotate):
            v = turn(v, cos, sin) if rotate else v
            grads[:, at * 128 : at * 128 + 128] = narrow(v)

        for g in range(kv_heads):
            hs = range(g * group, (g + 1) * group)
            pick = lambda src: jnp.concatenate(
                [jnp.where(low != bool(h % 2), src(h // 2), zero) for h in hs]
            )
            q3 = pick(lambda j: q[j])
            c3 = pick(lambda j: cg[:, j * 128 : j * 128 + 128])
            a = softmax_rows(q3, keys[g], ok)
            ag = mm_nt(c3, values[g])
            sg = narrow(a * (ag - jnp.sum(a * ag, -1, keepdims=True)))
            vg = mm_tn(narrow(a), c3)
            kg = score_scale * mm_tn(sg, q3)
            qg = score_scale * mm(sg, keys[g])
            fold[g] = (kg + pltpu.roll(kg, HEAD, 1), vg + pltpu.roll(vg, HEAD, 1))
            for n, h in enumerate(hs):
                done[h] = qg[n * length : (n + 1) * length]
                if h % 2:
                    put(h // 2, jnp.where(low, done.pop(h - 1), done.pop(h)), True)
            if g % 2:
                (ka, va), (kb, vb) = fold.pop(g - 1), fold.pop(g)
                put(fq // 128 + g // 2, jnp.where(low, ka, kb), True)
                put((fq + fk) // 128 + g // 2, jnp.where(low, va, vb), False)

    vm = pl.BlockSpec(memory_space=pltpu.VMEM)
    return pl.pallas_call(
        body,
        in_specs=[pl.BlockSpec(memory_space=pltpu.SMEM)] + [vm] * 6 + [ANY] * n_out,
        out_shape=like(length, total),
        scratch_shapes=[pltpu.VMEM((fq, width), BF), pltpu.SemaphoreType.DMA((n_out,))],
        compiler_params=BIG,
        cost_estimate=cost(
            2 * length * fq * width + 12 * heads * length * length * 128,
            2 * fq * width + 8 * length * total,
            heads * length * length,
        ),
        name="attend_back",
    )(spots, qkv, *tables, branch, *out_parts)


def ring_columns(v, at, base, n, scratch, out):
    per = v.shape[1] // n
    scratch[...] = wide(v).T
    for i in range(n):
        block = scratch[pl.ds(pl.multiple_of(at[base + i] * per, 8), per)]
        out[i * per : (i + 1) * per] = narrow(block)


def out_gradient(attended, branches, total, spots, base, n):
    length, dh = attended[0].shape
    width = branches[0].shape[1]
    tile = 512

    def body(at, aa, ab, ba, bb, own, sib, scratch, lhs):
        @pl.when(pl.program_id(0) == 0)
        def _():
            ring_columns(jnp.concatenate([aa[...], ab[...]]), at, base, n, scratch, lhs)

        d = narrow(mm(lhs[...], jnp.concatenate([ba[...], bb[...]])))
        own[...], sib[...] = d[: dh // 2], d[dh // 2 :]

    whole = pl.BlockSpec((length, dh), lambda i, at: (0, 0))
    return pl.pallas_call(
        body,
        grid_spec=pltpu.PrefetchScalarGridSpec(
            num_scalar_prefetch=1,
            grid=(width // tile,),
            in_specs=[whole, whole] + [pl.BlockSpec((length, tile), lambda i, at: (0, i))] * 2,
            out_specs=[pl.BlockSpec((dh // 2, tile), lambda i, at: (0, i))] * 2,
            scratch_shapes=[
                pltpu.VMEM((dh, 2 * length), F32), pltpu.VMEM((dh, 2 * length), BF),
            ],
        ),
        out_shape=[like(dh // 2, total)] * 2,
        compiler_params=BIG,
        cost_estimate=cost(4 * length * dh * width, 2 * dh * width),
        name="out_gradient",
    )(spots, *attended, *branches)


def projection_gradient(
    grads, low, normed, cols, inverses, small, begun, skip, spots, base, side, n, experts
):
    length, total = grads[0].shape
    dh = low.shape[0]
    tile = 512
    steps, last = total // tile, experts + 16

    def body(at, ga, gb, w, na, nb, ca, cb, ia, ib, sa, sb, _0, _1, own, sib, n1a, n1b, scratch, lhs, acc, tiny):
        i = pl.program_id(0)

        @pl.when(i == 0)
        def _():
            ring_columns(jnp.concatenate([na[...], nb[...]]), at, base, n, scratch, lhs)
            acc[...] = jnp.zeros_like(acc)

        @pl.when(i < steps)
        def _():
            g = jnp.concatenate([ga[...], gb[...]])
            d = narrow(mm(lhs[...], g))
            own[...], sib[...] = d[: dh // 2], d[dh // 2 :]
            acc[...] += mm_nt(g, w[...])

        @pl.when(i == steps)
        def _():
            n1 = acc[...]
            n1a[...], n1b[...] = n1[:length], narrow(n1[length:])
            gain = n1[:length] * (wide(ca[...]) * column(ia[...])) + n1[length:] * (
                wide(cb[...]) * column(ib[...])
            )
            tiny[...] = jnp.zeros_like(tiny)
            tiny[:last] = wide(sa[...]) + wide(sb[...])
            row = jnp.sum(gain, 0, keepdims=True)
            tiny[experts + 8 : last] = jnp.broadcast_to(row, (8, dh))
            ring_columns(tiny[...], at, base, n, scratch.at[:, :128], lhs.at[:, :128])
            own[:, :128], sib[:, :128] = lhs[: dh // 2, :128], lhs[dh // 2 :, :128]

    whole = lambda a: pl.BlockSpec(a.shape, lambda i, at: (0, 0))
    strip = lambda a: pl.BlockSpec(
        (a.shape[0], tile), lambda i, at: (0, jnp.minimum(i, steps - 1))
    )
    out = pl.BlockSpec((dh // 2, tile), lambda i, at: (0, skip // tile + i))
    shapes = [like(*begun[0].shape)] * 2 + [like(length, dh, dtype=F32), like(length, dh)]
    return pl.pallas_call(
        body,
        grid_spec=pltpu.PrefetchScalarGridSpec(
            num_scalar_prefetch=1,
            grid=(steps + 1,),
            in_specs=[strip(grads[0]), strip(grads[1]), strip(low)]
            + [whole(v) for v in (*normed, *cols, *inverses)]
            + [pl.BlockSpec((last, dh), lambda i, at: (length // last, at[side]))] * 2
            + [ANY, ANY],
            out_specs=[out, out, whole(shapes[2]), whole(shapes[3])],
            scratch_shapes=[
                pltpu.VMEM((dh, 2 * length), F32),
                pltpu.VMEM((dh, 2 * length), BF),
                pltpu.VMEM((2 * length, dh), F32),
                pltpu.VMEM((128, dh), F32),
            ],
        ),
        out_shape=shapes,
        input_output_aliases={12: 0, 13: 1},
        compiler_params=BIG,
        cost_estimate=cost(8 * length * dh * total, 4 * dh * total),
        name="projection_gradient",
    )(spots, *grads, low, *normed, *cols, *inverses, *small, *begun)


def put_rows(pieces, spots, seats, per, widths, rows, kept=None, small=None):
    k = len(widths)
    cuts = [sum(widths[:i]) for i in range(k + 1)]
    given = list(kept or ())
    closing = small is not None
    plain = k - 1 if closing else k
    flat = [(p, i, at) for p, places in enumerate(seats) for i, at in enumerate(places)]
    n, m = len(flat), len(pieces)

    def body(at_ref, *refs):
        src, refs = refs[:m], refs[m:]
        before, refs = refs[: len(given)], refs[len(given) :]
        outs, refs = refs[:plain], refs[plain:]
        if closing:
            router, moe, attn, refs = *refs[:3], refs[3:]
            table, sem, refs = *refs[:2], refs[2:]
            fetch = pltpu.make_async_copy(before[-1], table, sem)
            fetch.start()
        held, sems = refs[:plain], refs[plain]
        copies = []
        for j, (p, i, at) in enumerate(flat):
            row = pl.multiple_of(at_ref[at] * per, 8)
            for w in range(plain):
                held[w][j * per : (j + 1) * per] = wide(
                    src[p][i * per : (i + 1) * per, cuts[w] : cuts[w + 1]]
                )
                copy = pltpu.make_async_copy(
                    held[w].at[pl.ds(j * per, per)], outs[w].at[pl.ds(row, per)], sems.at[j, w]
                )
                copy.start()
                copies.append(copy)
        if closing:
            fetch.wait()
            for p, i, at in flat:
                row = pl.multiple_of(at_ref[at] * per, 8)
                table[pl.ds(row, per)] = wide(src[p][i * per : (i + 1) * per, cuts[plain] :])
            across = table[...].T
            router[...] = across[:small]
            moe[...], attn[...] = across[small], across[small + 8]
        for copy in copies:
            copy.wait()

    vm = pl.BlockSpec(memory_space=pltpu.VMEM)
    out_specs = [ANY] * plain
    out_shape = [like(rows, w, dtype=F32) for w in widths[:plain]]
    scratch = [pltpu.VMEM((n * per, w), F32) for w in widths[:plain]]
    scratch += [pltpu.SemaphoreType.DMA((n, plain))]
    if closing:
        out_specs += [vm] * 3
        out_shape += [like(small, rows, dtype=F32)] + [like(rows, dtype=F32)] * 2
        scratch = [pltpu.VMEM((rows, widths[-1]), F32), pltpu.SemaphoreType.DMA] + scratch
    return pl.pallas_call(
        body,
        in_specs=[pl.BlockSpec(memory_space=pltpu.SMEM)] + [vm] * m + [ANY] * len(given),
        out_specs=out_specs,
        out_shape=out_shape,
        input_output_aliases={1 + m + i: i for i in range(plain if given else 0)},
        scratch_shapes=scratch,
        compiler_params=BIG,
        cost_estimate=cost(n * per * cuts[-1], n * per * cuts[-1] * 6),
        name="put_rows",
    )(spots, *pieces, *given)


def expert_step(spots, base, tiles, cots, router, gate, up, down, starts, kept, start, total, apart):
    width, ffe = cots.shape[1] - router.shape[0], gate[0].shape[1]
    tail = router.shape[0]
    count = len(tiles)
    two = sum(p.shape[0] for p in tiles[0])
    block = two // 2
    n = count * block
    pieces = [p for t in tiles for p in t]
    parts = [*gate, *up, *down]
    sets, m = [len(gate), len(up), len(down)], len(pieces)
    k = sum(sets)

    def body(spot, ca, cb, rt, *refs):
        xs, ws = refs[:m], refs[m : m + k]
        products = refs[-10 - n_out : -10]
        x_o, hid_o, pre_o, rg_o = refs[-10:-6]
        held, gw, uw, dw, sems, wsems = refs[-6:]
        i = pl.program_id(0)
        moves, at, j = [], 0, 0
        for t in tiles:
            group = []
            for p in t:
                dst = held.at[pl.ds(at, p.shape[0])]
                group.append(pltpu.make_async_copy(xs[j], dst, sems.at[j]))
                at, j = at + p.shape[0], j + 1
            moves.append(group)
        loads = []
        first = 0
        for size, whole in zip(sets, (gw, uw, dw)):
            part = slice(first, first + size)
            loads += load_parts(ws[part], spot, starts + first, whole, wsems.at[pl.ds(first, size)])
            first += size

        @pl.when(i == 0)
        def _():
            for copy in [*moves[0], *loads]:
                copy.start()
            for copy in [c for g in moves[1:] for c in g]:
                copy.start()

        for t in range(count):

            @pl.when(i == t)
            def _():
                for copy in moves[t]:
                    copy.wait()

        @pl.when(i == 0)
        def _():
            for copy in loads:
                copy.wait()

        x = held[pl.ds(pl.multiple_of(i * two, two), two)]
        cm = jnp.concatenate([ca[...], cb[...]])
        cot, chosen = cm[:, :width], cm[:, width:] > 0
        x_o[...] = x
        logits = jnp.where(chosen, mm_nt(x, rt[...]), mask_fill)
        top = jnp.max(logits, -1, keepdims=True)
        raised = jnp.where(chosen, jnp.exp(logits - top), 0.0)
        mine = lax.broadcasted_iota(jnp.int32, raised.shape, 1)
        weight = jnp.sum(jnp.where(mine == spot[0], raised, 0.0), -1, keepdims=True)
        weight = narrow(weight / jnp.sum(raised, -1, keepdims=True))
        gate_pre, up_pre = mm(x, gw[...]), mm(x, uw[...])
        sg = jax.nn.sigmoid(gate_pre)
        silu = gate_pre * sg
        hidden = narrow(silu * up_pre)
        hid_o[...] = hidden
        result_grad = weight * cot
        rg_o[...] = result_grad
        result = narrow(mm(hidden, dw[...]))
        mix = weight * result
        gate_grad = jnp.sum(wide(result) * wide(cot), -1, keepdims=True)
        hidden_grad = mm_nt(result_grad, dw[...])
        gpg = narrow(hidden_grad * up_pre * sg * (1.0 + gate_pre * (1.0 - sg)))
        upg = narrow(hidden_grad * silu)
        pre_o[:, :ffe], pre_o[:, ffe:] = gpg, upg
        row = narrow(mm_nt(gpg, gw[...]) + mm_nt(upg, uw[...]))
        high = wide(narrow(gate_grad))
        ends = jnp.where(mine == spot[0], high, 0.0)
        ends = narrow(jnp.where(mine == spot[0] + tail // 2, gate_grad - high, ends))

        def store(mix_a, mix_b, row_a, row_b):
            mix_a[...], mix_b[...] = mix[:block], mix[block:]
            row_a[:, :width], row_b[:, :width] = row[:block], row[block:]
            row_a[:, width:], row_b[:, width:] = ends[:block], ends[block:]

        if apart:
            pl.when(i == 0)(lambda: store(*products[:4]))
            pl.when(i > 0)(lambda: store(*products[4:]))
        else:
            store(*products)

    gap = 1 if apart else 0
    step = lambda w: pl.BlockSpec((block, w), lambda i, s: (jnp.maximum(i - gap, 0), 0))
    once = lambda w: pl.BlockSpec((block, w), lambda i, s: (0, 0))
    four = (width, width, width + tail, width + tail)
    keep = lambda w: pl.BlockSpec((two, w), lambda i, s: (start + i, 0))
    widths = [width, ffe, 2 * ffe, width]
    out_shape = [like(block, w) for w in four] if apart else []
    out_shape += [like(n - gap * block, w) for w in four]
    out_shape += [like(total, w) for w in widths]
    given = list(kept or ())
    before, n_out = 4 + m + k, 8 if apart else 4
    return pl.pallas_call(
        body,
        grid_spec=pltpu.PrefetchScalarGridSpec(
            num_scalar_prefetch=1,
            grid=(count,),
            in_specs=[
                pl.BlockSpec((block, width + tail), lambda i, s: (s[base + i], 0)),
                pl.BlockSpec((block, width + tail), lambda i, s: (s[base + count + i], 0)),
                pl.BlockSpec(router.shape, lambda i, s: (0, 0)),
            ]
            + [ANY] * (m + k + len(given)),
            out_specs=[once(w) for w in (four if apart else ())]
            + [step(w) for w in four]
            + [keep(w) for w in widths],
            scratch_shapes=[
                pltpu.VMEM((count * two, width), BF),
                pltpu.VMEM((width, ffe), BF),
                pltpu.VMEM((width, ffe), BF),
                pltpu.VMEM((ffe, width), BF),
                pltpu.SemaphoreType.DMA((m,)),
                pltpu.SemaphoreType.DMA((k,)),
            ],
        ),
        out_shape=out_shape,
        input_output_aliases={before + i: n_out + i for i in range(len(given))},
        compiler_params=BIG,
        cost_estimate=cost(
            24 * n * width * ffe, 6 * width * ffe + n * width * 28, 2 * n * ffe
        ),
        name="expert_step",
    )(spots, cots, cots, router, *pieces, *parts, *given)


class Links:
    def __init__(self):
        self.n = lax.axis_size("dp")
        self.e = lax.axis_size("expert")
        self.chips = self.e // 2
        order = list(range(self.chips))
        if self.n == 2 and self.chips == 8:
            order = [0, 2, 4, 6, 7, 5, 3, 1]
        self.order = order
        self.x = lax.axis_index("dp")
        self.me = lax.axis_index("expert")

    def table(self, of):
        rows, begins = [], {}
        for x in range(self.n):
            for me in range(self.e):
                lists, row = of(x, me, self.order.index(me // 2)), []
                for name, values in lists.items():
                    begins[name] = len(row)
                    row += values
                rows.append(row)
        at = self.x * self.e + self.me
        whole = jnp.asarray(np.array(rows, np.int32))
        return lax.dynamic_slice_in_dim(whole, at, 1, 0).reshape(-1), begins

    def sibling(self, v):
        return lax.ppermute(v, "expert", [(i, i ^ 1) for i in range(self.e)])

    def flip(self, v, bit):
        return lax.ppermute(v, "expert", [(i, i ^ bit) for i in range(self.e)])

    def ring(self, v, step):
        c, o = self.chips, self.order
        pairs = [(o[k] * 2 + l, o[(k + step) % c] * 2 + l) for k in range(c) for l in (0, 1)]
        return lax.ppermute(v, "expert", pairs)

    def gather(self, block, waits=()):
        c = self.chips
        half = block.shape[0] // 2
        got = {0: block}
        up = down = block
        for s in range(1, c // 2):
            up, down = level(up, down, *(waits[s] if s < len(waits) else ()))
            up, down = self.ring(up, 1), self.ring(down, -1)
            got[c - s], got[s] = up, down
        up, down = level(up, down)
        far = (self.ring(up[:half], 1), self.ring(down[half:], -1))
        return got, far

    def scatter(self, s, far, waits=(), steps=None):
        c = self.chips
        half = far[0].shape[0]
        up, down = self.ring(far[0], 1), self.ring(far[1], -1)
        steps = [] if steps is None else steps
        steps.append((up, down))
        r = c // 2 - 1
        a, b = s(r, None), s(c - r, None)
        up = jnp.concatenate([add_low(up, a[:half]), a[half:]])
        down = jnp.concatenate([b[:half], add_low(down, b[half:])])
        for r in range(c // 2 - 2, -1, -1):
            up, down = level(up, down, *(waits(len(steps)) if waits else ()))
            up, down = self.ring(up, 1), self.ring(down, -1)
            steps.append((up, down))
            if r:
                last = steps[-2]
                up, down = add_low(up, s(r, last)), add_low(down, s(c - r, last))
        return (s(0, up), up, down), steps

    def swap(self, v):
        return lax.ppermute(v, "dp", [(0, 1), (1, 0)])

    def pick(self, v, other, axis):
        size = v.shape[axis] // self.n
        at = (1 - self.x if other else self.x) * size
        return lax.dynamic_slice_in_dim(v, at, size, axis)

    def both(self, own, got, axis):
        return jnp.where(
            self.x == 0,
            jnp.concatenate([own, got], axis),
            jnp.concatenate([got, own], axis),
        )

    def columns(self, v):
        if self.n == 2:
            return jnp.concatenate([self.pick(v, False, 1), self.swap(self.pick(v, True, 1))])
        return lax.all_to_all(v, "dp", split_axis=1, concat_axis=0, tiled=True)

    def columns_back(self, v):
        if self.n == 2:
            t = v.shape[0] // 2
            return self.both(v[:t], wide(self.swap(narrow(v[t:]))), 1)
        return wide(lax.all_to_all(narrow(v), "dp", split_axis=0, concat_axis=1, tiled=True))

    def rows(self, v):
        if self.n == 2:
            return jnp.concatenate([v, self.swap(v)])
        return lax.all_gather(v, "dp", axis=0, tiled=True)

    def sum_back(self, v):
        if self.n == 2:
            t = v.shape[0] // 2
            return v[:t] + wide(self.swap(narrow(v[t:])))
        return wide(lax.psum_scatter(narrow(v), "dp", scatter_dimension=0, tiled=True))

    def whole(self, v, axis):
        if self.n == 2:
            return self.both(v, self.swap(v), axis)
        return lax.all_gather(v, "dp", axis=axis, tiled=True)

    def shard_sum(self, v, axis):
        return wide(lax.psum_scatter(narrow(v), "dp", scatter_dimension=axis, tiled=True))

    def parts(self, w):
        if self.n == 2:
            return [w, self.swap(w)]
        return [lax.all_gather(w, "dp", axis=0, tiled=True)]

    def parts_by_four(self, w, after):
        if self.n != 2:
            return self.parts(narrow(w))
        part = w.shape[0] // 4
        a = self.swap(narrow(lax.dynamic_slice_in_dim(w, self.me % 4 * part, part, 0)))
        w, a = narrow(tie(w, after)), tie(a, after)
        b = self.flip(a, 2)
        return [w, a, b, self.flip(a, 1), self.flip(b, 1)]


def wide_sum(v):
    out = wide(v[0])
    for w in v[1:]:
        out = out + wide(w)
    return out


def shards(
    tokens, cotangent, lengths, routes, gain_attn, w_query, key_weight, value_weight,
    w_out, gain_moe, w_router, w_gate, w_up, w_down,
):
    net = Links()
    c, pair = net.chips, net.n == 2
    length, width = tokens.shape
    dh = gain_attn.shape[0]
    heads, kv_heads = w_query.shape[1] // HEAD, key_weight.shape[1] // HEAD
    fq, fk = w_query.shape[1], key_weight.shape[1]
    experts = w_router.shape[1]
    tail = 128
    far, half = c // 2, length // 2

    if pair:
        away = net.pick(tokens, True, 1)
        stream = wide(tie(tokens, away))
    else:
        stream = wide(tokens)
    inv_one = lax.rsqrt(jnp.mean(stream * stream, -1, keepdims=True) + norm_eps)
    if pair:
        cols = (net.pick(tokens, False, 1), net.swap(away))
        inv_row = inv_one.reshape(1, length)
        inverses = (inv_row, net.swap(inv_row))
        weights = (w_query, key_weight, value_weight)
        other, normed_other = project_columns(cols[1], inverses[1], gain_attn[None], weights, BF)
        arrived = net.swap(other)
        own, normed_own = project_columns(
            tie(cols[0], other), inverses[0], gain_attn[None], weights, F32
        )
        normed_cols = (normed_own, normed_other)
        sums = (own, arrived)
        w_qkv = jnp.concatenate(
            [narrow(tie(w, own)) for w in (w_query, key_weight, value_weight)], 1
        )
    else:
        scaled_cols = wide(net.columns(tokens)) * net.rows(inv_one.reshape(1, length)).reshape(-1, 1)
        normed_cols = narrow(scaled_cols * wide(narrow(gain_attn))[None, :])
        w_qkv = jnp.concatenate([narrow(w_query), narrow(key_weight), narrow(value_weight)], 1)
        arrived = net.sum_back(mm(normed_cols, w_qkv))
        sums, own, other = (arrived,), arrived, arrived

    near = [0] + [r for s in range(1, far - 1) for r in (s, c - s)]
    last = [far, far - 1, c - far + 1]
    ffe = w_down.shape[1]

    def numbers(x, me, place):
        at = lambda r, l: net.order[(place + r) % c] * 2 + (me % 2 ^ l)
        seat = lambda r, l: (place + r) % c * 2 + (me % 2 ^ l)
        y, q, part = 1 - x, me % 4, dh // 4
        return {
            "me": [me],
            "x": [x],
            "near": [at(r, l) for l in (0, 1) for r in near],
            "last": [at(r, l) for l in (0, 1) for r in last],
            "expert": [x * dh, y * dh, y * dh + dh // 2, x * dh, y * dh, x * ffe, y * ffe]
            if pair
            else [0, 0, 0],
            "out": [x * dh] + [y * dh + (q ^ z) * part for z in (0, 2, 1, 3)] if pair else [0],
            "seats": [seat(r, l) for l in (0, 1) for r in range(c)],
        }

    spots, begins = net.table(numbers)
    small = jnp.concatenate(
        [narrow(tie(w_router, inv_one)).T, narrow(gain_attn)[None], narrow(gain_moe)[None]], 0
    )
    small = net.whole(small, 1)
    gain_one, gain_two = wide(small[experts])[None], wide(small[experts + 1])[None]
    router = jnp.pad(small[:experts], ((0, tail - experts), (0, 0)))
    out_parts = net.parts_by_four(tie(w_out, inv_one), other)
    hits = routes[:, :, None] == jnp.arange(tail, dtype=jnp.int32)[None, None, :]
    chosen = narrow(jnp.any(hits, 1))
    cot_all = lax.all_gather(
        jnp.concatenate([tie(cotangent, inv_one), chosen], 1), "expert", axis=0, tiled=True
    )
    if pair:
        low = narrow(tie(w_gate, inv_one)[0])
        gate_parts = [low, net.swap(low[: dh // 2]), net.swap(tie(low[dh // 2 :], out_parts[2]))]
        up_parts, down_parts = (
            net.parts(tie(narrow(tie(w, own)[0]), out_parts[2])) for w in (w_up, w_down)
        )
        hold = (w_qkv, gate_parts[1])
        waits = ((), (), gate_parts[2:], up_parts[1:])
    else:
        gate_parts, up_parts, down_parts = (net.parts(narrow(w[0])) for w in (w_gate, w_up, w_down))
        hold, waits = (w_qkv,), ()

    places, live, allowed = layout(lengths[0], length)
    inner = jnp.arange(128, dtype=jnp.int32) % (HEAD // 2)
    angles = places.astype(F32)[:, None] * (rope_base ** (-inner.astype(F32) * 2.0 / HEAD))[None]
    sign = jnp.where(jnp.arange(128) % HEAD < HEAD // 2, -1.0, 1.0)[None]
    tables = (
        jnp.cos(angles), jnp.sin(angles) * sign, allowed.astype(F32), live.astype(F32)[None],
    )
    qkv, attended, mid, normed_two, gates = attend(
        sums, tables, tie(tokens, *hold), gain_two, router, chosen, out_parts, spots,
        begins["out"], heads, kv_heads,
    )

    got, ends = net.gather(normed_two, waits)
    beside = {r: net.sibling(v) for r, v in got.items()}
    kept, start, made = None, 0, []
    for g, name in ((near, "near"), (last, "last")):
        if made:
            ends = tuple(tie(v, made[0][0]) for v in ends)
            ends_beside = tuple(net.sibling(v) for v in ends)
        tiles = [(*ends, *ends_beside) if r == far else (got[r], beside[r]) for r in g]
        out = expert_step(
            spots, begins[name], tiles, cot_all, router, gate_parts, up_parts, down_parts,
            begins["expert"], kept, start, net.e * length, far in g,
        )
        kept, start = out[-4:], start + len(g)
        made += [out[i : i + 4] for i in range(0, len(out) - 4, 4)]
    after_near = made[0][0]

    sums = {0: {}, 2: {}}

    def ring_sum(which, after, waits=(), steps=None):
        (a0, b0), (a2, b2), (a1, b1) = (m[which : which + 2] for m in made)
        edge = add_low(a2, net.sibling(tie(b2, *after)))
        b1 = net.sibling(b1)
        done = sums[which]

        def block(r, then):
            group, at = (near, 0) if r in near else (last[1:], 1)
            if at not in done:
                done[at] = add_low(a1, b1) if at else add_low(a0, net.sibling(tie(b0, *then)))
            i = group.index(r)
            return done[at][i * length : (i + 1) * length]

        return net.scatter(block, (edge[:half], edge[half:]), waits, steps)

    rows_all, hid_all, pre_all, rg_all = kept
    ffe = w_gate.shape[2]
    if pair:
        part = net.swap(tie(net.pick(attended, True, 1), after_near))
        halves = lambda v: (net.pick(v, False, 0), narrow(net.pick(v, True, 0)))
        back, steps = ring_sum(2, ())
    else:
        back, steps = ring_sum(2, ())

    mid_grad, branch = second_norm_back(
        back, gates, router, mid, gain_two, cotangent, normed_two, experts
    )

    mixed, mix_steps = ring_sum(0, ())
    mix_parts = mixed

    base = begins["seats"]
    seats = spots[base : base + net.e]
    per = dh // net.e
    if not pair:
        slot = jnp.arange(dh, dtype=jnp.int32)
        source = jnp.sum(
            jnp.where(slot[:, None] // per == jnp.arange(net.e)[None, :], seats[None, :], 0), 1
        ) * per + slot % per
        perm = (slot[:, None] == source[None, :]).astype(BF)

    def all_sum(own, sib, widths, small, ready, last_mix):
        at = slice(far * per, (far + 1) * per)
        edge = add_low(own[at], net.sibling(sib[at]))
        s = []

        def block(r, after):
            if not s:
                s.append(add_low(own, net.sibling(sib)))
            return s[0][r * per : (r + 1) * per]

        cut = per // 2
        total, steps = net.scatter(
            block, (edge[:cut], edge[cut:]), lambda k: last_mix if k == 1 else ()
        )
        ready = ready(steps[0])
        up = down = held = narrow(wide_sum(total))
        seat = lambda rs: [[base + l * c + r for r in rs] for l in (0, 1)]
        pieces, kept = [], ()

        def put(pieces, kept):
            both = [v for p in pieces for v in p[:2]]
            return put_rows(both, spots, [v for p in pieces for v in p[2]], per, widths, dh, kept)

        for s in range(far):
            if s == far - 1 and per % 16 == 0:
                kept = put(pieces, None)
            if s:
                before = [p[1] for p in pieces[max(s - 2, 0) : s - 1]]
                up, down = level(up, down, *before, *jax.tree.leaves(ready[s : s + 1]))
            rs = [s, c - s] if s else [0]
            pieces.append((held, net.sibling(held), seat(rs)))
            if s < far - 1:
                up, down = net.ring(up, 1), net.ring(down, -1)
                held = jnp.concatenate([down, up])
            else:
                up, down = net.ring(up[:cut], 1), net.ring(down[cut:], -1)
        if per % 16 == 0:
            kept = put(pieces[far - 1 :], kept)
            up, down = level(up, down, kept[0], *jax.tree.leaves(ready[far:]))
        held = jnp.concatenate([up, down])
        pieces.append((held, net.sibling(held), seat([far])))
        if per % 16 == 0:
            return put_rows(pieces[-1][:2], spots, seat([far]), per, widths, dh, kept, small)
        out = jnp.zeros((dh, sum(widths)), F32)
        for a, b, seats in pieces:
            for v, ats in zip((a, b), seats):
                for i, at in enumerate(ats):
                    blk = wide(v[i * per : (i + 1) * per])
                    out = lax.dynamic_update_slice_in_dim(out, blk, spots[at] * per, 0)
        cuts = [sum(widths[:i]) for i in range(len(widths) + 1)]
        out = [out[:, a:b] for a, b in zip(cuts, cuts[1:])]
        return [*out[:-1], out[-1][:, :small].T, out[-1][:, small], out[-1][:, small + 8]]

    part_width = width + fq + 2 * fk + tail
    beyond = net.swap(branch) if pair else None

    grads = attend_back(
        qkv, tables, tie(branch, *mix_steps[0]), out_parts, spots, begins["out"], heads, kv_heads
    )
    sent = grads
    if pair:
        sent = tie(net.swap(tie(grads, beyond, part, *mix_steps[1])), *mix_steps[2])
        begun = out_gradient(
            (net.pick(attended, False, 1), part), (branch, tie(beyond, *mix_steps[1])), part_width,
            spots, base, net.e,
        )
        own, sib, n1, n1_other = projection_gradient(
            (grads, sent), w_qkv, normed_cols, cols, inverses, (branch, beyond), begun, width, spots,
            base, begins["x"], net.e, experts,
        )
        n1_other = net.swap(n1_other)
        n1g = net.both(n1, wide(n1_other), 1)
    else:
        grads_all = net.rows(grads)
        d_out = mm_tn(narrow(mm(net.columns(attended), perm)), net.rows(branch[:length]))
        d_qkv = mm_tn(narrow(mm(normed_cols, perm)), grads_all)
        n1 = mm_nt(grads_all, w_qkv)
        n1g = net.columns_back(n1)
        d_small = net.shard_sum(wide(branch[length:]), 1)
        d_gain = jnp.broadcast_to(jnp.sum(n1 * scaled_cols, 0)[None], (8, dh))
        d_small = jnp.concatenate([d_small[: experts + 8], d_gain], 0)
        d_small = jnp.pad(mm(narrow(d_small), perm).T, ((0, 0), (0, tail - experts - 16)))
        d = narrow(jnp.concatenate([d_out, d_qkv, d_small], 1))
        own, sib = d[: dh // 2], d[dh // 2 :]
    scaled_one = stream * inv_one
    du = n1g * gain_one
    d_tokens = mid_grad + inv_one * (
        du - scaled_one * jnp.mean(du * scaled_one, -1, keepdims=True)
    )
    if pair:
        last_mix, grown = mix_steps[3], []

        def ready(arrived):
            d_pre = halves(mm_tn(tie(rows_all, *arrived), pre_all))
            d_down = halves(mm_tn(tie(hid_all, *arrived), rg_all))
            d_down, d_pre = (v[0] + wide(net.swap(tie(v[1], n1_other))) for v in (d_down, d_pre))
            late = (mix_parts[0], *(tie(v, *arrived) for v in mix_parts[1:]))
            grown.extend((d_down, d_pre[:, :ffe], d_pre[:, ffe:], narrow(mid + wide_sum(late))))
            return (), (), (d_tokens,), grown[3:], grown[:3]

    else:
        d_down, d_pre = (
            net.shard_sum(mm_tn(a, b), 0)[None] for a, b in ((hid_all, rg_all), (rows_all, pre_all))
        )
        ready, last_mix, grown = (lambda _: ()), (), ()
    d_out, d_query, d_key, d_value, d_router, d_moe, d_attn = all_sum(
        own, sib, [width, fq, fk, fk, tail], experts, ready, last_mix
    )
    if not pair:
        grown = d_down[0], d_pre[0, :, :ffe], d_pre[0, :, ffe:], narrow(mid + wide_sum(mix_parts))
    d_down, d_gate, d_up = (v[None] for v in grown[:3])
    return (
        grown[3],
        d_tokens,
        d_attn,
        d_query,
        d_key,
        d_value,
        d_out,
        d_moe,
        d_router.T,
        d_gate,
        d_up,
        d_down,
    )


def solution(mesh):
    rows = P(("dp", "expert"), None)
    flat, dense, routed = P("dp"), P("dp", None), P("expert", "dp", None)
    return jax.shard_map(
        shards,
        mesh=mesh,
        in_specs=(
            rows, rows, rows, rows, flat, dense, dense, dense, dense, flat, dense,
            routed, routed, routed,
        ),
        out_specs=(
            rows, rows, flat, dense, dense, dense, dense, flat, dense, routed, routed, routed,
        ),
        check_vma=False,
    )
```

```python
import jax
import jax.numpy as jnp
import numpy as np
from jax import lax
from jax.experimental import pallas as pl
from jax.experimental.pallas import tpu as pltpu
from jax.sharding import PartitionSpec as P

HEAD = 64
norm_eps = 1e-06
score_scale = 0.015625
rope_base = 10000.0
mask_fill = -1e30
BF = jnp.bfloat16
F32 = jnp.float32


def narrow(v):
    return v.astype(BF)


def wide(v):
    return v.astype(F32)


def mm(a, b):
    return jnp.dot(a, b, preferred_element_type=F32)


def mm_tn(a, b):
    return lax.dot_general(a, b, (((0,), (0,)), ((), ())), preferred_element_type=F32)


def mm_nt(a, b):
    return lax.dot_general(a, b, (((1,), (1,)), ((), ())), preferred_element_type=F32)


def add_low(a, b):
    return narrow(wide(a) + wide(b))


def layout(lengths, length):
    pieces = lengths.shape[0]
    order = jnp.arange(pieces, dtype=jnp.int32)
    ends = jnp.sum(jnp.where(order[None, :] <= order[:, None], lengths[None, :], 0), 1)
    starts = ends - lengths
    at = jnp.arange(length, dtype=jnp.int32)
    segment = jnp.sum((at[:, None] >= ends[None, :]).astype(jnp.int32), 1)
    owned = segment[:, None] == order[None, :]
    places = at - jnp.sum(jnp.where(owned, starts[None, :], 0), 1)
    live = segment < pieces - 1
    allowed = (
        (segment[:, None] == segment[None, :])
        & (at[None, :] <= at[:, None])
        & (live[None, :] | (at[:, None] == at[None, :]))
    )
    return places, live, allowed


def tie(v, *after):
    return lax.optimization_barrier((v, *after))[0]


def level(a, b, *after):
    return lax.optimization_barrier((a, b, *after))[:2]


ANY = pl.BlockSpec(memory_space=pl.ANY)
BIG = pltpu.CompilerParams(vmem_limit_bytes=56 << 20)


def cost(flops, moved, hard=0):
    return pl.CostEstimate(flops=int(flops), bytes_accessed=int(moved), transcendentals=int(hard))


def like(*shape, dtype=BF):
    return jax.ShapeDtypeStruct(shape, dtype)


def load_parts(parts, spots, base, whole, sems):
    return [
        pltpu.make_async_copy(
            ref, whole.at[pl.ds(pl.multiple_of(spots[base + i], 16), ref.shape[0])], sems.at[i]
        )
        for i, ref in enumerate(parts)
    ]


def column(row):
    n = row.shape[1]
    return jnp.broadcast_to(row, (n, n)).T[:, :1]


def turn(v, cosine, sine):
    lane = lax.broadcasted_iota(jnp.int32, v.shape, 1) % HEAD
    other = jnp.where(lane < HEAD // 2, pltpu.roll(v, 96, 1), pltpu.roll(v, 32, 1))
    return v * cosine + other * sine


def twice(v, odd):
    low = lax.broadcasted_iota(jnp.int32, v.shape, 1) < HEAD
    return jnp.where(low != odd, v, pltpu.roll(v, HEAD, 1))


def softmax_rows(q3, keys, allowed3):
    s = jnp.where(allowed3, mm_nt(q3, keys) * score_scale, mask_fill)
    e = jnp.exp(s - jnp.max(s, -1, keepdims=True))
    return e / jnp.sum(e, -1, keepdims=True)


def project_columns(cols, inverse, gain, weights, kind):
    length, dh = cols.shape
    widths = [w.shape[1] for w in weights]
    tile = 512
    counts = [w // tile for w in widths]
    first = [sum(counts[:i]) for i in range(len(counts))]
    total = sum(widths)

    def body(c, inv, g, wq, wk, wv, out, normed):
        i = pl.program_id(0)

        @pl.when(i == 0)
        def _():
            normed[...] = narrow(wide(c[...]) * column(inv[...]) * wide(narrow(g[...])))

        def go(w):
            out[...] = mm(normed[...], narrow(w[...])).astype(kind)

        for ref, a, n in zip((wq, wk, wv), first, counts):
            pl.when((i >= a) & (i < a + n))(lambda ref=ref: go(ref))

    whole = lambda a: pl.BlockSpec(a.shape, lambda i: (0, 0))
    strip = lambda a, n: pl.BlockSpec((dh, tile), lambda i: (0, jnp.clip(i - a, 0, n - 1)))
    return pl.pallas_call(
        body,
        grid=(sum(counts),),
        in_specs=[whole(v) for v in (cols, inverse, gain)]
        + [strip(a, n) for a, n in zip(first, counts)],
        out_specs=[pl.BlockSpec((length, tile), lambda i: (0, i)), whole(cols)],
        out_shape=[like(length, total, dtype=kind), like(length, dh)],
        compiler_params=BIG,
        cost_estimate=cost(2 * length * dh * total, 4 * dh * total),
        name="project_columns",
    )(cols, inverse, gain, *weights)


def attend(sums, tables, tokens, gain_two, router, chosen, out_parts, spots, base, heads, kv_heads):
    length, width = tokens.shape
    group = heads // kv_heads
    fq, fk = heads * HEAD, kv_heads * HEAD
    total = fq + 2 * fk
    n_sum, n_out = len(sums), len(out_parts)

    def body(spots, *refs):
        parts, refs = refs[:n_sum], refs[n_sum:]
        cosine, sine, allowed, live, tok, gain, rt, pick = refs[:8]
        outs = refs[8 : 8 + n_out]
        qkv_o, att_o, mid_o, norm_o, gate_o, w_out, sems = refs[8 + n_out :]
        copies = load_parts(outs, spots, base, w_out, sems)
        for copy in copies:
            copy.start()
        cos, sin = cosine[...], sine[...]

        def block(j):
            at = slice(j * 128, j * 128 + 128)
            v = wide(parts[0][:, at])
            for p in parts[1:]:
                v = v + wide(p[:, at])
            return at, v

        keys, values, q = [], [], []
        for j in range(fq // 128):
            at, v = block(j)
            v = narrow(turn(v, cos, sin))
            qkv_o[:, at] = v
            q.append(v)
        for j in range(fk // 128):
            at, v = block(fq // 128 + j)
            v = turn(v, cos, sin)
            qkv_o[:, at] = narrow(v)
            keys += [narrow(twice(v, False)), narrow(twice(v, True))]
        for j in range(fk // 128):
            at, v = block((fq + fk) // 128 + j)
            qkv_o[:, at] = narrow(v)
            values += [narrow(twice(v, False)), narrow(twice(v, True))]
        low = lax.broadcasted_iota(jnp.int32, (length, 128), 1) < HEAD
        ok = jnp.concatenate([allowed[...] > 0] * group)
        alive = column(live[...]) > 0
        done = {}
        zero = jnp.zeros((length, 128), BF)
        for g in range(kv_heads):
            hs = range(g * group, (g + 1) * group)
            q3 = jnp.concatenate([jnp.where(low != bool(h % 2), q[h // 2], zero) for h in hs])
            a = narrow(softmax_rows(q3, keys[g], ok))
            ctx = mm(a, values[g])
            for n, h in enumerate(hs):
                done[h] = ctx[n * length : (n + 1) * length]
                if h % 2:
                    both = jnp.where(low, done.pop(h - 1), done.pop(h))
                    att_o[:, h // 2 * 128 : h // 2 * 128 + 128] = narrow(
                        jnp.where(alive, both, 0.0)
                    )
        for copy in copies:
            copy.wait()
        mid = wide(tok[...]) + mm(att_o[...], w_out[...])
        mid_o[...] = mid
        inverse = lax.rsqrt(jnp.mean(mid * mid, -1, keepdims=True) + norm_eps)
        normed = narrow(mid * inverse * gain[...])
        norm_o[...] = normed
        yes = pick[...] > 0
        logits = jnp.where(yes, mm_nt(normed, rt[...]), mask_fill)
        up = jnp.where(yes, jnp.exp(logits - jnp.max(logits, -1, keepdims=True)), 0.0)
        gate_o[...] = up / jnp.sum(up, -1, keepdims=True)

    given = (*sums, *tables, tokens, gain_two, router, chosen)
    whole = [pl.BlockSpec(memory_space=pltpu.VMEM)] * len(given)
    return pl.pallas_call(
        body,
        in_specs=[pl.BlockSpec(memory_space=pltpu.SMEM)] + whole + [ANY] * n_out,
        out_shape=[
            like(length, total),
            like(length, fq),
            like(length, width, dtype=F32),
            like(length, width),
            like(length, router.shape[0], dtype=F32),
        ],
        scratch_shapes=[
            pltpu.VMEM((fq, width), BF),
            pltpu.SemaphoreType.DMA((n_out,)),
        ],
        compiler_params=BIG,
        cost_estimate=cost(
            2 * length * fq * width + 4 * heads * length * length * 128,
            2 * fq * width + 12 * length * total,
            heads * length * length,
        ),
        name="attend",
    )(spots, *given, *out_parts)


def second_norm_back(sums, gates, router, mid, gain_two, cotangent, normed, experts):
    length, width = mid.shape
    tail = router.shape[0]

    def body(a, b, c, gate_r, rt, mid_r, gain, cot, norm, mid_o, out_o):
        ends = wide(a[:, width:]) + wide(b[:, width:]) + wide(c[:, width:])
        grad = ends + pltpu.roll(ends, tail // 2, 1)
        gate = gate_r[...]
        chosen = gate * (grad - jnp.sum(gate * grad, -1, keepdims=True))
        logit = narrow(chosen)
        n2g = wide(a[:, :width]) + wide(b[:, :width]) + wide(c[:, :width]) + mm(logit, rt[...])
        m = mid_r[...]
        inverse = lax.rsqrt(jnp.mean(m * m, -1, keepdims=True) + norm_eps)
        scaled = m * inverse
        du = n2g * gain[...]
        out = wide(cot[...]) + inverse * (
            du - scaled * jnp.mean(du * scaled, -1, keepdims=True)
        )
        mid_o[...] = out
        out_o[:length] = narrow(out)
        out_o[length : length + experts] = narrow(mm_tn(logit, norm[...])[:experts])
        gain_row = jnp.sum(n2g * scaled, 0, keepdims=True)
        out_o[length + experts :] = narrow(jnp.broadcast_to(gain_row, (16, width)))

    return pl.pallas_call(
        body,
        out_shape=[like(length, width, dtype=F32), like(length + experts + 16, width)],
        compiler_params=BIG,
        cost_estimate=cost(6 * length * width * tail, 20 * length * width),
        name="second_norm_back",
    )(*sums, gates, router, mid, gain_two, cotangent, normed)


def attend_back(qkv, tables, branch, out_parts, spots, base, heads, kv_heads):
    length, width = tables[0].shape[0], branch.shape[1]
    group = heads // kv_heads
    fq, fk = heads * HEAD, kv_heads * HEAD
    total = fq + 2 * fk
    n_out = len(out_parts)

    def body(spots, qkv_r, cosine, sine, allowed, live, br, *refs):
        outs = refs[:n_out]
        grads, w_out, sems = refs[n_out:]
        copies = load_parts(outs, spots, base, w_out, sems)
        for copy in copies:
            copy.start()
        cos, sin = cosine[...], -sine[...]
        low = lax.broadcasted_iota(jnp.int32, (length, 128), 1) < HEAD
        ok = jnp.concatenate([allowed[...] > 0] * group)
        zero = jnp.zeros((length, 128), BF)
        q = [qkv_r[:, j * 128 : j * 128 + 128] for j in range(fq // 128)]
        keys, values = [], []
        for store, left in ((keys, fq), (values, fq + fk)):
            for j in range(fk // 128):
                v = wide(qkv_r[:, left + j * 128 : left + j * 128 + 128])
                store += [narrow(twice(v, False)), narrow(twice(v, True))]
        for copy in copies:
            copy.wait()
        cg = narrow(jnp.where(column(live[...]) > 0, mm_nt(br[:length], w_out[...]), 0.0))
        done, fold = {}, {}

        def put(at, v, rotate):
            v = turn(v, cos, sin) if rotate else v
            grads[:, at * 128 : at * 128 + 128] = narrow(v)

        for g in range(kv_heads):
            hs = range(g * group, (g + 1) * group)
            pick = lambda src: jnp.concatenate(
                [jnp.where(low != bool(h % 2), src(h // 2), zero) for h in hs]
            )
            q3 = pick(lambda j: q[j])
            c3 = pick(lambda j: cg[:, j * 128 : j * 128 + 128])
            a = softmax_rows(q3, keys[g], ok)
            ag = mm_nt(c3, values[g])
            sg = narrow(a * (ag - jnp.sum(a * ag, -1, keepdims=True)))
            vg = mm_tn(narrow(a), c3)
            kg = score_scale * mm_tn(sg, q3)
            qg = score_scale * mm(sg, keys[g])
            fold[g] = (kg + pltpu.roll(kg, HEAD, 1), vg + pltpu.roll(vg, HEAD, 1))
            for n, h in enumerate(hs):
                done[h] = qg[n * length : (n + 1) * length]
                if h % 2:
                    put(h // 2, jnp.where(low, done.pop(h - 1), done.pop(h)), True)
            if g % 2:
                (ka, va), (kb, vb) = fold.pop(g - 1), fold.pop(g)
                put(fq // 128 + g // 2, jnp.where(low, ka, kb), True)
                put((fq + fk) // 128 + g // 2, jnp.where(low, va, vb), False)

    vm = pl.BlockSpec(memory_space=pltpu.VMEM)
    return pl.pallas_call(
        body,
        in_specs=[pl.BlockSpec(memory_space=pltpu.SMEM)] + [vm] * 6 + [ANY] * n_out,
        out_shape=like(length, total),
        scratch_shapes=[pltpu.VMEM((fq, width), BF), pltpu.SemaphoreType.DMA((n_out,))],
        compiler_params=BIG,
        cost_estimate=cost(
            2 * length * fq * width + 12 * heads * length * length * 128,
            2 * fq * width + 8 * length * total,
            heads * length * length,
        ),
        name="attend_back",
    )(spots, qkv, *tables, branch, *out_parts)


def ring_columns(v, at, base, n, scratch, out):
    per = v.shape[1] // n
    scratch[...] = wide(v).T
    for i in range(n):
        block = scratch[pl.ds(pl.multiple_of(at[base + i] * per, 8), per)]
        out[i * per : (i + 1) * per] = narrow(block)


def out_gradient(attended, branches, total, spots, base, n):
    length, dh = attended[0].shape
    width = branches[0].shape[1]
    tile = 512

    def body(at, aa, ab, ba, bb, own, sib, scratch, lhs):
        @pl.when(pl.program_id(0) == 0)
        def _():
            ring_columns(jnp.concatenate([aa[...], ab[...]]), at, base, n, scratch, lhs)

        d = narrow(mm(lhs[...], jnp.concatenate([ba[...], bb[...]])))
        own[...], sib[...] = d[: dh // 2], d[dh // 2 :]

    whole = pl.BlockSpec((length, dh), lambda i, at: (0, 0))
    return pl.pallas_call(
        body,
        grid_spec=pltpu.PrefetchScalarGridSpec(
            num_scalar_prefetch=1,
            grid=(width // tile,),
            in_specs=[whole, whole] + [pl.BlockSpec((length, tile), lambda i, at: (0, i))] * 2,
            out_specs=[pl.BlockSpec((dh // 2, tile), lambda i, at: (0, i))] * 2,
            scratch_shapes=[
                pltpu.VMEM((dh, 2 * length), F32), pltpu.VMEM((dh, 2 * length), BF),
            ],
        ),
        out_shape=[like(dh // 2, total)] * 2,
        compiler_params=BIG,
        cost_estimate=cost(4 * length * dh * width, 2 * dh * width),
        name="out_gradient",
    )(spots, *attended, *branches)


def projection_gradient(
    grads, low, normed, cols, inverses, small, begun, skip, spots, base, side, n, experts
):
    length, total = grads[0].shape
    dh = low.shape[0]
    tile = 512
    steps, last = total // tile, experts + 16

    def body(at, ga, gb, w, na, nb, ca, cb, ia, ib, sa, sb, _0, _1, own, sib, n1a, n1b, scratch, lhs, acc, tiny):
        i = pl.program_id(0)

        @pl.when(i == 0)
        def _():
            ring_columns(jnp.concatenate([na[...], nb[...]]), at, base, n, scratch, lhs)
            acc[...] = jnp.zeros_like(acc)

        @pl.when(i < steps)
        def _():
            g = jnp.concatenate([ga[...], gb[...]])
            d = narrow(mm(lhs[...], g))
            own[...], sib[...] = d[: dh // 2], d[dh // 2 :]
            acc[...] += mm_nt(g, w[...])

        @pl.when(i == steps)
        def _():
            n1 = acc[...]
            n1a[...], n1b[...] = n1[:length], narrow(n1[length:])
            gain = n1[:length] * (wide(ca[...]) * column(ia[...])) + n1[length:] * (
                wide(cb[...]) * column(ib[...])
            )
            tiny[...] = jnp.zeros_like(tiny)
            tiny[:last] = wide(sa[...]) + wide(sb[...])
            row = jnp.sum(gain, 0, keepdims=True)
            tiny[experts + 8 : last] = jnp.broadcast_to(row, (8, dh))
            ring_columns(tiny[...], at, base, n, scratch.at[:, :128], lhs.at[:, :128])
            own[:, :128], sib[:, :128] = lhs[: dh // 2, :128], lhs[dh // 2 :, :128]

    whole = lambda a: pl.BlockSpec(a.shape, lambda i, at: (0, 0))
    strip = lambda a: pl.BlockSpec(
        (a.shape[0], tile), lambda i, at: (0, jnp.minimum(i, steps - 1))
    )
    out = pl.BlockSpec((dh // 2, tile), lambda i, at: (0, skip // tile + i))
    shapes = [like(*begun[0].shape)] * 2 + [like(length, dh, dtype=F32), like(length, dh)]
    return pl.pallas_call(
        body,
        grid_spec=pltpu.PrefetchScalarGridSpec(
            num_scalar_prefetch=1,
            grid=(steps + 1,),
            in_specs=[strip(grads[0]), strip(grads[1]), strip(low)]
            + [whole(v) for v in (*normed, *cols, *inverses)]
            + [pl.BlockSpec((last, dh), lambda i, at: (length // last, at[side]))] * 2
            + [ANY, ANY],
            out_specs=[out, out, whole(shapes[2]), whole(shapes[3])],
            scratch_shapes=[
                pltpu.VMEM((dh, 2 * length), F32),
                pltpu.VMEM((dh, 2 * length), BF),
                pltpu.VMEM((2 * length, dh), F32),
                pltpu.VMEM((128, dh), F32),
            ],
        ),
        out_shape=shapes,
        input_output_aliases={12: 0, 13: 1},
        compiler_params=BIG,
        cost_estimate=cost(8 * length * dh * total, 4 * dh * total),
        name="projection_gradient",
    )(spots, *grads, low, *normed, *cols, *inverses, *small, *begun)


def put_rows(pieces, spots, seats, per, widths, rows, kept=None, small=None):
    k = len(widths)
    cuts = [sum(widths[:i]) for i in range(k + 1)]
    given = list(kept or ())
    closing = small is not None
    plain = k - 1 if closing else k
    flat = [(p, i, at) for p, places in enumerate(seats) for i, at in enumerate(places)]
    n, m = len(flat), len(pieces)

    def body(at_ref, *refs):
        src, refs = refs[:m], refs[m:]
        before, refs = refs[: len(given)], refs[len(given) :]
        outs, refs = refs[:plain], refs[plain:]
        if closing:
            router, moe, attn, refs = *refs[:3], refs[3:]
            table, sem, refs = *refs[:2], refs[2:]
            fetch = pltpu.make_async_copy(before[-1], table, sem)
            fetch.start()
        held, sems = refs[:plain], refs[plain]
        copies = []
        for j, (p, i, at) in enumerate(flat):
            row = pl.multiple_of(at_ref[at] * per, 8)
            for w in range(plain):
                held[w][j * per : (j + 1) * per] = wide(
                    src[p][i * per : (i + 1) * per, cuts[w] : cuts[w + 1]]
                )
                copy = pltpu.make_async_copy(
                    held[w].at[pl.ds(j * per, per)], outs[w].at[pl.ds(row, per)], sems.at[j, w]
                )
                copy.start()
                copies.append(copy)
        if closing:
            fetch.wait()
            for p, i, at in flat:
                row = pl.multiple_of(at_ref[at] * per, 8)
                table[pl.ds(row, per)] = wide(src[p][i * per : (i + 1) * per, cuts[plain] :])
            across = table[...].T
            router[...] = across[:small]
            moe[...], attn[...] = across[small], across[small + 8]
        for copy in copies:
            copy.wait()

    vm = pl.BlockSpec(memory_space=pltpu.VMEM)
    out_specs = [ANY] * plain
    out_shape = [like(rows, w, dtype=F32) for w in widths[:plain]]
    scratch = [pltpu.VMEM((n * per, w), F32) for w in widths[:plain]]
    scratch += [pltpu.SemaphoreType.DMA((n, plain))]
    if closing:
        out_specs += [vm] * 3
        out_shape += [like(small, rows, dtype=F32)] + [like(rows, dtype=F32)] * 2
        scratch = [pltpu.VMEM((rows, widths[-1]), F32), pltpu.SemaphoreType.DMA] + scratch
    return pl.pallas_call(
        body,
        in_specs=[pl.BlockSpec(memory_space=pltpu.SMEM)] + [vm] * m + [ANY] * len(given),
        out_specs=out_specs,
        out_shape=out_shape,
        input_output_aliases={1 + m + i: i for i in range(plain if given else 0)},
        scratch_shapes=scratch,
        compiler_params=BIG,
        cost_estimate=cost(n * per * cuts[-1], n * per * cuts[-1] * 6),
        name="put_rows",
    )(spots, *pieces, *given)


def expert_step(spots, base, tiles, cots, router, gate, up, down, starts, kept, start, total, apart):
    width, ffe = cots.shape[1] - router.shape[0], gate[0].shape[1]
    tail = router.shape[0]
    count = len(tiles)
    two = sum(p.shape[0] for p in tiles[0])
    block = two // 2
    n = count * block
    pieces = [p for t in tiles for p in t]
    parts = [*gate, *up, *down]
    sets, m = [len(gate), len(up), len(down)], len(pieces)
    k = sum(sets)

    def body(spot, ca, cb, rt, *refs):
        xs, ws = refs[:m], refs[m : m + k]
        products = refs[-10 - n_out : -10]
        x_o, hid_o, pre_o, rg_o = refs[-10:-6]
        held, gw, uw, dw, sems, wsems = refs[-6:]
        i = pl.program_id(0)
        moves, at, j = [], 0, 0
        for t in tiles:
            group = []
            for p in t:
                dst = held.at[pl.ds(at, p.shape[0])]
                group.append(pltpu.make_async_copy(xs[j], dst, sems.at[j]))
                at, j = at + p.shape[0], j + 1
            moves.append(group)
        loads = []
        first = 0
        for size, whole in zip(sets, (gw, uw, dw)):
            part = slice(first, first + size)
            loads += load_parts(ws[part], spot, starts + first, whole, wsems.at[pl.ds(first, size)])
            first += size

        @pl.when(i == 0)
        def _():
            for copy in [*moves[0], *loads]:
                copy.start()
            for copy in [c for g in moves[1:] for c in g]:
                copy.start()

        for t in range(count):

            @pl.when(i == t)
            def _():
                for copy in moves[t]:
                    copy.wait()

        @pl.when(i == 0)
        def _():
            for copy in loads[: sets[0] + sets[1]]:
                copy.wait()

        x = held[pl.ds(pl.multiple_of(i * two, two), two)]
        cm = jnp.concatenate([ca[...], cb[...]])
        cot, chosen = cm[:, :width], cm[:, width:] > 0
        x_o[...] = x
        logits = jnp.where(chosen, mm_nt(x, rt[...]), mask_fill)
        top = jnp.max(logits, -1, keepdims=True)
        raised = jnp.where(chosen, jnp.exp(logits - top), 0.0)
        mine = lax.broadcasted_iota(jnp.int32, raised.shape, 1)
        weight = jnp.sum(jnp.where(mine == spot[0], raised, 0.0), -1, keepdims=True)
        weight = narrow(weight / jnp.sum(raised, -1, keepdims=True))
        gate_pre, up_pre = mm(x, gw[...]), mm(x, uw[...])
        sg = jax.nn.sigmoid(gate_pre)
        silu = gate_pre * sg
        hidden = narrow(silu * up_pre)
        hid_o[...] = hidden
        result_grad = weight * cot

        @pl.when(i == 0)
        def _():
            for copy in loads[sets[0] + sets[1] :]:
                copy.wait()

        rg_o[...] = result_grad
        result = narrow(mm(hidden, dw[...]))
        mix = weight * result
        gate_grad = jnp.sum(wide(result) * wide(cot), -1, keepdims=True)
        hidden_grad = mm_nt(result_grad, dw[...])
        gpg = narrow(hidden_grad * up_pre * sg * (1.0 + gate_pre * (1.0 - sg)))
        upg = narrow(hidden_grad * silu)
        pre_o[:, :ffe], pre_o[:, ffe:] = gpg, upg
        row = narrow(mm_nt(gpg, gw[...]) + mm_nt(upg, uw[...]))
        high = wide(narrow(gate_grad))
        ends = jnp.where(mine == spot[0], high, 0.0)
        ends = narrow(jnp.where(mine == spot[0] + tail // 2, gate_grad - high, ends))

        def store(mix_a, mix_b, row_a, row_b):
            mix_a[...], mix_b[...] = mix[:block], mix[block:]
            row_a[:, :width], row_b[:, :width] = row[:block], row[block:]
            row_a[:, width:], row_b[:, width:] = ends[:block], ends[block:]

        if apart:
            pl.when(i == 0)(lambda: store(*products[:4]))
            pl.when(i > 0)(lambda: store(*products[4:]))
        else:
            store(*products)

    gap = 1 if apart else 0
    step = lambda w: pl.BlockSpec((block, w), lambda i, s: (jnp.maximum(i - gap, 0), 0))
    once = lambda w: pl.BlockSpec((block, w), lambda i, s: (0, 0))
    four = (width, width, width + tail, width + tail)
    keep = lambda w: pl.BlockSpec((two, w), lambda i, s: (start + i, 0))
    widths = [width, ffe, 2 * ffe, width]
    out_shape = [like(block, w) for w in four] if apart else []
    out_shape += [like(n - gap * block, w) for w in four]
    out_shape += [like(total, w) for w in widths]
    given = list(kept or ())
    before, n_out = 4 + m + k, 8 if apart else 4
    return pl.pallas_call(
        body,
        grid_spec=pltpu.PrefetchScalarGridSpec(
            num_scalar_prefetch=1,
            grid=(count,),
            in_specs=[
                pl.BlockSpec((block, width + tail), lambda i, s: (s[base + i], 0)),
                pl.BlockSpec((block, width + tail), lambda i, s: (s[base + count + i], 0)),
                pl.BlockSpec(router.shape, lambda i, s: (0, 0)),
            ]
            + [ANY] * (m + k + len(given)),
            out_specs=[once(w) for w in (four if apart else ())]
            + [step(w) for w in four]
            + [keep(w) for w in widths],
            scratch_shapes=[
                pltpu.VMEM((count * two, width), BF),
                pltpu.VMEM((width, ffe), BF),
                pltpu.VMEM((width, ffe), BF),
                pltpu.VMEM((ffe, width), BF),
                pltpu.SemaphoreType.DMA((m,)),
                pltpu.SemaphoreType.DMA((k,)),
            ],
        ),
        out_shape=out_shape,
        input_output_aliases={before + i: n_out + i for i in range(len(given))},
        compiler_params=BIG,
        cost_estimate=cost(
            24 * n * width * ffe, 6 * width * ffe + n * width * 28, 2 * n * ffe
        ),
        name="expert_step",
    )(spots, cots, cots, router, *pieces, *parts, *given)


class Links:
    def __init__(self):
        self.n = lax.axis_size("dp")
        self.e = lax.axis_size("expert")
        self.chips = self.e // 2
        order = list(range(self.chips))
        if self.n == 2 and self.chips == 8:
            order = [0, 2, 4, 6, 7, 5, 3, 1]
        self.order = order
        self.x = lax.axis_index("dp")
        self.me = lax.axis_index("expert")

    def table(self, of):
        rows, begins = [], {}
        for x in range(self.n):
            for me in range(self.e):
                lists, row = of(x, me, self.order.index(me // 2)), []
                for name, values in lists.items():
                    begins[name] = len(row)
                    row += values
                rows.append(row)
        at = self.x * self.e + self.me
        whole = jnp.asarray(np.array(rows, np.int32))
        return lax.dynamic_slice_in_dim(whole, at, 1, 0).reshape(-1), begins

    def sibling(self, v):
        return lax.ppermute(v, "expert", [(i, i ^ 1) for i in range(self.e)])

    def flip(self, v, bit):
        return lax.ppermute(v, "expert", [(i, i ^ bit) for i in range(self.e)])

    def ring(self, v, step):
        c, o = self.chips, self.order
        pairs = [(o[k] * 2 + l, o[(k + step) % c] * 2 + l) for k in range(c) for l in (0, 1)]
        return lax.ppermute(v, "expert", pairs)

    def gather(self, block, waits=()):
        c = self.chips
        half = block.shape[0] // 2
        got = {0: block}
        up = down = block
        for s in range(1, c // 2):
            up, down = level(up, down, *(waits[s] if s < len(waits) else ()))
            up, down = self.ring(up, 1), self.ring(down, -1)
            got[c - s], got[s] = up, down
        up, down = level(up, down)
        far = (self.ring(up[:half], 1), self.ring(down[half:], -1))
        return got, far

    def scatter(self, s, far, waits=(), steps=None):
        c = self.chips
        half = far[0].shape[0]
        up, down = self.ring(far[0], 1), self.ring(far[1], -1)
        steps = [] if steps is None else steps
        steps.append((up, down))
        r = c // 2 - 1
        a, b = s(r, None), s(c - r, None)
        up = jnp.concatenate([add_low(up, a[:half]), a[half:]])
        down = jnp.concatenate([b[:half], add_low(down, b[half:])])
        for r in range(c // 2 - 2, -1, -1):
            up, down = level(up, down, *(waits(len(steps)) if waits else ()))
            up, down = self.ring(up, 1), self.ring(down, -1)
            steps.append((up, down))
            if r:
                last = steps[-2]
                up, down = add_low(up, s(r, last)), add_low(down, s(c - r, last))
        return (s(0, up), up, down), steps

    def swap(self, v):
        return lax.ppermute(v, "dp", [(0, 1), (1, 0)])

    def pick(self, v, other, axis):
        size = v.shape[axis] // self.n
        at = (1 - self.x if other else self.x) * size
        return lax.dynamic_slice_in_dim(v, at, size, axis)

    def both(self, own, got, axis):
        return jnp.where(
            self.x == 0,
            jnp.concatenate([own, got], axis),
            jnp.concatenate([got, own], axis),
        )

    def columns(self, v):
        if self.n == 2:
            return jnp.concatenate([self.pick(v, False, 1), self.swap(self.pick(v, True, 1))])
        return lax.all_to_all(v, "dp", split_axis=1, concat_axis=0, tiled=True)

    def columns_back(self, v):
        if self.n == 2:
            t = v.shape[0] // 2
            return self.both(v[:t], wide(self.swap(narrow(v[t:]))), 1)
        return wide(lax.all_to_all(narrow(v), "dp", split_axis=0, concat_axis=1, tiled=True))

    def rows(self, v):
        if self.n == 2:
            return jnp.concatenate([v, self.swap(v)])
        return lax.all_gather(v, "dp", axis=0, tiled=True)

    def sum_back(self, v):
        if self.n == 2:
            t = v.shape[0] // 2
            return v[:t] + wide(self.swap(narrow(v[t:])))
        return wide(lax.psum_scatter(narrow(v), "dp", scatter_dimension=0, tiled=True))

    def whole(self, v, axis):
        if self.n == 2:
            return self.both(v, self.swap(v), axis)
        return lax.all_gather(v, "dp", axis=axis, tiled=True)

    def shard_sum(self, v, axis):
        return wide(lax.psum_scatter(narrow(v), "dp", scatter_dimension=axis, tiled=True))

    def parts(self, w):
        if self.n == 2:
            return [w, self.swap(w)]
        return [lax.all_gather(w, "dp", axis=0, tiled=True)]

    def parts_by_four(self, w, after):
        if self.n != 2:
            return self.parts(narrow(w))
        part = w.shape[0] // 4
        a = self.swap(narrow(lax.dynamic_slice_in_dim(w, self.me % 4 * part, part, 0)))
        w, a = narrow(tie(w, after)), tie(a, after)
        b = self.flip(a, 2)
        return [w, a, b, self.flip(a, 1), self.flip(b, 1)]


def wide_sum(v):
    out = wide(v[0])
    for w in v[1:]:
        out = out + wide(w)
    return out


def shards(
    tokens, cotangent, lengths, routes, gain_attn, w_query, key_weight, value_weight,
    w_out, gain_moe, w_router, w_gate, w_up, w_down,
):
    net = Links()
    c, pair = net.chips, net.n == 2
    length, width = tokens.shape
    dh = gain_attn.shape[0]
    heads, kv_heads = w_query.shape[1] // HEAD, key_weight.shape[1] // HEAD
    fq, fk = w_query.shape[1], key_weight.shape[1]
    experts = w_router.shape[1]
    tail = 128
    far, half = c // 2, length // 2

    if pair:
        away = net.pick(tokens, True, 1)
        stream = wide(tie(tokens, away))
    else:
        stream = wide(tokens)
    inv_one = lax.rsqrt(jnp.mean(stream * stream, -1, keepdims=True) + norm_eps)
    if pair:
        cols = (net.pick(tokens, False, 1), net.swap(away))
        inv_row = inv_one.reshape(1, length)
        inverses = (inv_row, net.swap(inv_row))
        weights = (w_query, key_weight, value_weight)
        other, normed_other = project_columns(cols[1], inverses[1], gain_attn[None], weights, BF)
        arrived = net.swap(other)
        own, normed_own = project_columns(
            tie(cols[0], other), inverses[0], gain_attn[None], weights, F32
        )
        normed_cols = (normed_own, normed_other)
        sums = (own, arrived)
        w_qkv = jnp.concatenate(
            [narrow(tie(w, own)) for w in (w_query, key_weight, value_weight)], 1
        )
    else:
        scaled_cols = wide(net.columns(tokens)) * net.rows(inv_one.reshape(1, length)).reshape(-1, 1)
        normed_cols = narrow(scaled_cols * wide(narrow(gain_attn))[None, :])
        w_qkv = jnp.concatenate([narrow(w_query), narrow(key_weight), narrow(value_weight)], 1)
        arrived = net.sum_back(mm(normed_cols, w_qkv))
        sums, own, other = (arrived,), arrived, arrived

    near = [0] + [r for s in range(1, far - 1) for r in (s, c - s)]
    last = [far, far - 1, c - far + 1]
    ffe = w_down.shape[1]

    def numbers(x, me, place):
        at = lambda r, l: net.order[(place + r) % c] * 2 + (me % 2 ^ l)
        seat = lambda r, l: (place + r) % c * 2 + (me % 2 ^ l)
        y, q, part = 1 - x, me % 4, dh // 4
        return {
            "me": [me],
            "x": [x],
            "near": [at(r, l) for l in (0, 1) for r in near],
            "last": [at(r, l) for l in (0, 1) for r in last],
            "expert": [x * dh, y * dh, y * dh + dh // 2, x * dh, y * dh, x * ffe, y * ffe]
            if pair
            else [0, 0, 0],
            "out": [x * dh] + [y * dh + (q ^ z) * part for z in (0, 2, 1, 3)] if pair else [0],
            "seats": [seat(r, l) for l in (0, 1) for r in range(c)],
        }

    spots, begins = net.table(numbers)
    small = jnp.concatenate(
        [narrow(tie(w_router, inv_one)).T, narrow(gain_attn)[None], narrow(gain_moe)[None]], 0
    )
    small = net.whole(small, 1)
    gain_one, gain_two = wide(small[experts])[None], wide(small[experts + 1])[None]
    router = jnp.pad(small[:experts], ((0, tail - experts), (0, 0)))
    out_parts = net.parts_by_four(tie(w_out, inv_one), other)
    hits = routes[:, :, None] == jnp.arange(tail, dtype=jnp.int32)[None, None, :]
    chosen = narrow(jnp.any(hits, 1))
    cot_all = lax.all_gather(
        jnp.concatenate([tie(cotangent, inv_one), chosen], 1), "expert", axis=0, tiled=True
    )
    if pair:
        low = narrow(tie(w_gate, inv_one)[0])
        gate_parts = [low, net.swap(low[: dh // 2]), net.swap(tie(low[dh // 2 :], out_parts[2]))]
        up_parts, down_parts = (
            net.parts(tie(narrow(tie(w, own)[0]), out_parts[2])) for w in (w_up, w_down)
        )
        hold = (w_qkv, gate_parts[1])
        waits = ((), (), gate_parts[2:], up_parts[1:])
    else:
        gate_parts, up_parts, down_parts = (net.parts(narrow(w[0])) for w in (w_gate, w_up, w_down))
        hold, waits = (w_qkv,), ()

    places, live, allowed = layout(lengths[0], length)
    inner = jnp.arange(128, dtype=jnp.int32) % (HEAD // 2)
    angles = places.astype(F32)[:, None] * (rope_base ** (-inner.astype(F32) * 2.0 / HEAD))[None]
    sign = jnp.where(jnp.arange(128) % HEAD < HEAD // 2, -1.0, 1.0)[None]
    tables = (
        jnp.cos(angles), jnp.sin(angles) * sign, allowed.astype(F32), live.astype(F32)[None],
    )
    qkv, attended, mid, normed_two, gates = attend(
        sums, tables, tie(tokens, *hold), gain_two, router, chosen, out_parts, spots,
        begins["out"], heads, kv_heads,
    )

    got, ends = net.gather(normed_two, waits)
    beside = {r: net.sibling(v) for r, v in got.items()}
    kept, start, made = None, 0, []
    for g, name in ((near, "near"), (last, "last")):
        if made:
            ends = tuple(tie(v, made[0][0]) for v in ends)
            ends_beside = tuple(net.sibling(v) for v in ends)
        tiles = [(*ends, *ends_beside) if r == far else (got[r], beside[r]) for r in g]
        out = expert_step(
            spots, begins[name], tiles, cot_all, router, gate_parts, up_parts, down_parts,
            begins["expert"], kept, start, net.e * length, far in g,
        )
        kept, start = out[-4:], start + len(g)
        made += [out[i : i + 4] for i in range(0, len(out) - 4, 4)]
    after_near = made[0][0]

    sums = {0: {}, 2: {}}

    def ring_sum(which, after, waits=(), steps=None):
        (a0, b0), (a2, b2), (a1, b1) = (m[which : which + 2] for m in made)
        edge = add_low(a2, net.sibling(tie(b2, *after)))
        b1 = net.sibling(b1)
        done = sums[which]

        def block(r, then):
            group, at = (near, 0) if r in near else (last[1:], 1)
            if at not in done:
                done[at] = add_low(a1, b1) if at else add_low(a0, net.sibling(tie(b0, *then)))
            i = group.index(r)
            return done[at][i * length : (i + 1) * length]

        return net.scatter(block, (edge[:half], edge[half:]), waits, steps)

    rows_all, hid_all, pre_all, rg_all = kept
    ffe = w_gate.shape[2]
    if pair:
        part = net.swap(tie(net.pick(attended, True, 1), after_near))
        halves = lambda v: (net.pick(v, False, 0), narrow(net.pick(v, True, 0)))
        back, steps = ring_sum(2, ())
    else:
        back, steps = ring_sum(2, ())

    mid_grad, branch = second_norm_back(
        back, gates, router, mid, gain_two, cotangent, normed_two, experts
    )

    mixed, mix_steps = ring_sum(0, ())
    mix_parts = mixed

    base = begins["seats"]
    seats = spots[base : base + net.e]
    per = dh // net.e
    if not pair:
        slot = jnp.arange(dh, dtype=jnp.int32)
        source = jnp.sum(
            jnp.where(slot[:, None] // per == jnp.arange(net.e)[None, :], seats[None, :], 0), 1
        ) * per + slot % per
        perm = (slot[:, None] == source[None, :]).astype(BF)

    def all_sum(own, sib, widths, small, ready, last_mix):
        at = slice(far * per, (far + 1) * per)
        edge = add_low(own[at], net.sibling(sib[at]))
        s = []

        def block(r, after):
            if not s:
                s.append(add_low(own, net.sibling(sib)))
            return s[0][r * per : (r + 1) * per]

        cut = per // 2
        total, steps = net.scatter(
            block, (edge[:cut], edge[cut:]), lambda k: last_mix if k == 1 else ()
        )
        ready = ready(steps[0])
        up = down = held = narrow(wide_sum(total))
        seat = lambda rs: [[base + l * c + r for r in rs] for l in (0, 1)]
        pieces, kept = [], ()

        def put(pieces, kept):
            both = [v for p in pieces for v in p[:2]]
            return put_rows(both, spots, [v for p in pieces for v in p[2]], per, widths, dh, kept)

        for s in range(far):
            if s == far - 1 and per % 16 == 0:
                kept = put(pieces, None)
            if s:
                before = [p[1] for p in pieces[max(s - 2, 0) : s - 1]]
                up, down = level(up, down, *before, *jax.tree.leaves(ready[s : s + 1]))
            rs = [s, c - s] if s else [0]
            pieces.append((held, net.sibling(held), seat(rs)))
            if s < far - 1:
                up, down = net.ring(up, 1), net.ring(down, -1)
                held = jnp.concatenate([down, up])
            else:
                up, down = net.ring(up[:cut], 1), net.ring(down[cut:], -1)
        if per % 16 == 0:
            kept = put(pieces[far - 1 :], kept)
            up, down = level(up, down, kept[0], *jax.tree.leaves(ready[far:]))
        held = jnp.concatenate([up, down])
        pieces.append((held, net.sibling(held), seat([far])))
        if per % 16 == 0:
            return put_rows(pieces[-1][:2], spots, seat([far]), per, widths, dh, kept, small)
        out = jnp.zeros((dh, sum(widths)), F32)
        for a, b, seats in pieces:
            for v, ats in zip((a, b), seats):
                for i, at in enumerate(ats):
                    blk = wide(v[i * per : (i + 1) * per])
                    out = lax.dynamic_update_slice_in_dim(out, blk, spots[at] * per, 0)
        cuts = [sum(widths[:i]) for i in range(len(widths) + 1)]
        out = [out[:, a:b] for a, b in zip(cuts, cuts[1:])]
        return [*out[:-1], out[-1][:, :small].T, out[-1][:, small], out[-1][:, small + 8]]

    part_width = width + fq + 2 * fk + tail
    beyond = net.swap(branch) if pair else None

    grads = attend_back(
        qkv, tables, tie(branch, *mix_steps[0]), out_parts, spots, begins["out"], heads, kv_heads
    )
    sent = grads
    if pair:
        sent = tie(net.swap(tie(grads, beyond, part, *mix_steps[1])), *mix_steps[2])
        begun = out_gradient(
            (net.pick(attended, False, 1), part), (branch, tie(beyond, *mix_steps[1])), part_width,
            spots, base, net.e,
        )
        own, sib, n1, n1_other = projection_gradient(
            (grads, sent), w_qkv, normed_cols, cols, inverses, (branch, beyond), begun, width, spots,
            base, begins["x"], net.e, experts,
        )
        n1_other = net.swap(n1_other)
        n1g = net.both(n1, wide(n1_other), 1)
    else:
        grads_all = net.rows(grads)
        d_out = mm_tn(narrow(mm(net.columns(attended), perm)), net.rows(branch[:length]))
        d_qkv = mm_tn(narrow(mm(normed_cols, perm)), grads_all)
        n1 = mm_nt(grads_all, w_qkv)
        n1g = net.columns_back(n1)
        d_small = net.shard_sum(wide(branch[length:]), 1)
        d_gain = jnp.broadcast_to(jnp.sum(n1 * scaled_cols, 0)[None], (8, dh))
        d_small = jnp.concatenate([d_small[: experts + 8], d_gain], 0)
        d_small = jnp.pad(mm(narrow(d_small), perm).T, ((0, 0), (0, tail - experts - 16)))
        d = narrow(jnp.concatenate([d_out, d_qkv, d_small], 1))
        own, sib = d[: dh // 2], d[dh // 2 :]
    scaled_one = stream * inv_one
    du = n1g * gain_one
    d_tokens = mid_grad + inv_one * (
        du - scaled_one * jnp.mean(du * scaled_one, -1, keepdims=True)
    )
    if pair:
        last_mix, grown = mix_steps[3], []

        def ready(arrived):
            d_pre = halves(mm_tn(tie(rows_all, *arrived), pre_all))
            d_down = halves(mm_tn(tie(hid_all, *arrived), rg_all))
            got = [net.swap(tie(v[1], n1_other)) for v in (d_down, d_pre)]
            gate, up = (d_pre[0][:, a] + wide(got[1][:, a]) for a in (slice(ffe), slice(ffe, None)))
            late = (mix_parts[0], *(tie(v, *arrived) for v in mix_parts[1:]))
            grown.extend((d_down[0] + wide(got[0]), gate, up, narrow(mid + wide_sum(late))))
            return (), (), (d_tokens,), grown[3:], grown[:3]

    else:
        d_down, d_pre = (
            net.shard_sum(mm_tn(a, b), 0)[None] for a, b in ((hid_all, rg_all), (rows_all, pre_all))
        )
        ready, last_mix, grown = (lambda _: ()), (), ()
    d_out, d_query, d_key, d_value, d_router, d_moe, d_attn = all_sum(
        own, sib, [width, fq, fk, fk, tail], experts, ready, last_mix
    )
    if not pair:
        grown = d_down[0], d_pre[0, :, :ffe], d_pre[0, :, ffe:], narrow(mid + wide_sum(mix_parts))
    d_down, d_gate, d_up = (v[None] for v in grown[:3])
    return (
        grown[3],
        d_tokens,
        d_attn,
        d_query,
        d_key,
        d_value,
        d_out,
        d_moe,
        d_router.T,
        d_gate,
        d_up,
        d_down,
    )


def solution(mesh):
    rows = P(("dp", "expert"), None)
    flat, dense, routed = P("dp"), P("dp", None), P("expert", "dp", None)
    return jax.shard_map(
        shards,
        mesh=mesh,
        in_specs=(
            rows, rows, rows, rows, flat, dense, dense, dense, dense, flat, dense,
            routed, routed, routed,
        ),
        out_specs=(
            rows, rows, flat, dense, dense, dense, dense, flat, dense, routed, routed, routed,
        ),
        check_vma=False,
    )
```

```python
import jax
import jax.numpy as jnp
import numpy as np
from jax import lax
from jax.experimental import pallas as pl
from jax.experimental.pallas import tpu as pltpu
from jax.sharding import PartitionSpec as P

HEAD = 64
norm_eps = 1e-06
score_scale = 0.015625
rope_base = 10000.0
mask_fill = -1e30
BF = jnp.bfloat16
F32 = jnp.float32


def narrow(v):
    return v.astype(BF)


def wide(v):
    return v.astype(F32)


def mm(a, b):
    return jnp.dot(a, b, preferred_element_type=F32)


def mm_tn(a, b):
    return lax.dot_general(a, b, (((0,), (0,)), ((), ())), preferred_element_type=F32)


def mm_nt(a, b):
    return lax.dot_general(a, b, (((1,), (1,)), ((), ())), preferred_element_type=F32)


def add_low(a, b):
    return narrow(wide(a) + wide(b))


def layout(lengths, length):
    pieces = lengths.shape[0]
    order = jnp.arange(pieces, dtype=jnp.int32)
    ends = jnp.sum(jnp.where(order[None, :] <= order[:, None], lengths[None, :], 0), 1)
    starts = ends - lengths
    at = jnp.arange(length, dtype=jnp.int32)
    segment = jnp.sum((at[:, None] >= ends[None, :]).astype(jnp.int32), 1)
    owned = segment[:, None] == order[None, :]
    places = at - jnp.sum(jnp.where(owned, starts[None, :], 0), 1)
    live = segment < pieces - 1
    allowed = (
        (segment[:, None] == segment[None, :])
        & (at[None, :] <= at[:, None])
        & (live[None, :] | (at[:, None] == at[None, :]))
    )
    return places, live, allowed


def tie(v, *after):
    return lax.optimization_barrier((v, *after))[0]


def level(a, b, *after):
    return lax.optimization_barrier((a, b, *after))[:2]


ANY = pl.BlockSpec(memory_space=pl.ANY)
BIG = pltpu.CompilerParams(vmem_limit_bytes=56 << 20)


def cost(flops, moved, hard=0):
    return pl.CostEstimate(flops=int(flops), bytes_accessed=int(moved), transcendentals=int(hard))


def like(*shape, dtype=BF):
    return jax.ShapeDtypeStruct(shape, dtype)


def load_parts(parts, spots, base, whole, sems):
    return [
        pltpu.make_async_copy(
            ref, whole.at[pl.ds(pl.multiple_of(spots[base + i], 16), ref.shape[0])], sems.at[i]
        )
        for i, ref in enumerate(parts)
    ]


def column(row):
    n = row.shape[1]
    return jnp.broadcast_to(row, (n, n)).T[:, :1]


def turn(v, cosine, sine):
    lane = lax.broadcasted_iota(jnp.int32, v.shape, 1) % HEAD
    other = jnp.where(lane < HEAD // 2, pltpu.roll(v, 96, 1), pltpu.roll(v, 32, 1))
    return v * cosine + other * sine


def twice(v, odd):
    low = lax.broadcasted_iota(jnp.int32, v.shape, 1) < HEAD
    return jnp.where(low != odd, v, pltpu.roll(v, HEAD, 1))


def softmax_rows(q3, keys, allowed3):
    s = jnp.where(allowed3, mm_nt(q3, keys) * score_scale, mask_fill)
    e = jnp.exp(s - jnp.max(s, -1, keepdims=True))
    return e / jnp.sum(e, -1, keepdims=True)


def project_columns(cols, inverse, gain, weights, kind):
    length, dh = cols.shape
    widths = [w.shape[1] for w in weights]
    tile = 512
    counts = [w // tile for w in widths]
    first = [sum(counts[:i]) for i in range(len(counts))]
    total = sum(widths)

    def body(c, inv, g, wq, wk, wv, out, normed):
        i = pl.program_id(0)

        @pl.when(i == 0)
        def _():
            normed[...] = narrow(wide(c[...]) * column(inv[...]) * wide(narrow(g[...])))

        def go(w):
            out[...] = mm(normed[...], narrow(w[...])).astype(kind)

        for ref, a, n in zip((wq, wk, wv), first, counts):
            pl.when((i >= a) & (i < a + n))(lambda ref=ref: go(ref))

    whole = lambda a: pl.BlockSpec(a.shape, lambda i: (0, 0))
    strip = lambda a, n: pl.BlockSpec((dh, tile), lambda i: (0, jnp.clip(i - a, 0, n - 1)))
    return pl.pallas_call(
        body,
        grid=(sum(counts),),
        in_specs=[whole(v) for v in (cols, inverse, gain)]
        + [strip(a, n) for a, n in zip(first, counts)],
        out_specs=[pl.BlockSpec((length, tile), lambda i: (0, i)), whole(cols)],
        out_shape=[like(length, total, dtype=kind), like(length, dh)],
        compiler_params=BIG,
        cost_estimate=cost(2 * length * dh * total, 4 * dh * total),
        name="project_columns",
    )(cols, inverse, gain, *weights)


def attend(sums, tables, tokens, gain_two, router, chosen, out_parts, spots, base, heads, kv_heads):
    length, width = tokens.shape
    group = heads // kv_heads
    fq, fk = heads * HEAD, kv_heads * HEAD
    total = fq + 2 * fk
    n_sum, n_out = len(sums), len(out_parts)

    def body(spots, *refs):
        parts, refs = refs[:n_sum], refs[n_sum:]
        cosine, sine, allowed, live, tok, gain, rt, pick = refs[:8]
        outs = refs[8 : 8 + n_out]
        qkv_o, att_o, mid_o, norm_o, gate_o, w_out, sems = refs[8 + n_out :]
        copies = load_parts(outs, spots, base, w_out, sems)
        for copy in copies:
            copy.start()
        cos, sin = cosine[...], sine[...]

        def block(j):
            at = slice(j * 128, j * 128 + 128)
            v = wide(parts[0][:, at])
            for p in parts[1:]:
                v = v + wide(p[:, at])
            return at, v

        keys, values, q = [], [], []
        for j in range(fq // 128):
            at, v = block(j)
            v = narrow(turn(v, cos, sin))
            qkv_o[:, at] = v
            q.append(v)
        for j in range(fk // 128):
            at, v = block(fq // 128 + j)
            v = turn(v, cos, sin)
            qkv_o[:, at] = narrow(v)
            keys += [narrow(twice(v, False)), narrow(twice(v, True))]
        for j in range(fk // 128):
            at, v = block((fq + fk) // 128 + j)
            qkv_o[:, at] = narrow(v)
            values += [narrow(twice(v, False)), narrow(twice(v, True))]
        low = lax.broadcasted_iota(jnp.int32, (length, 128), 1) < HEAD
        ok = jnp.concatenate([allowed[...] > 0] * group)
        alive = column(live[...]) > 0
        done = {}
        zero = jnp.zeros((length, 128), BF)
        for g in range(kv_heads):
            hs = range(g * group, (g + 1) * group)
            q3 = jnp.concatenate([jnp.where(low != bool(h % 2), q[h // 2], zero) for h in hs])
            a = narrow(softmax_rows(q3, keys[g], ok))
            ctx = mm(a, values[g])
            for n, h in enumerate(hs):
                done[h] = ctx[n * length : (n + 1) * length]
                if h % 2:
                    both = jnp.where(low, done.pop(h - 1), done.pop(h))
                    att_o[:, h // 2 * 128 : h // 2 * 128 + 128] = narrow(
                        jnp.where(alive, both, 0.0)
                    )
        for copy in copies:
            copy.wait()
        mid = wide(tok[...]) + mm(att_o[...], w_out[...])
        mid_o[...] = mid
        inverse = lax.rsqrt(jnp.mean(mid * mid, -1, keepdims=True) + norm_eps)
        normed = narrow(mid * inverse * gain[...])
        norm_o[...] = normed
        yes = pick[...] > 0
        logits = jnp.where(yes, mm_nt(normed, rt[...]), mask_fill)
        up = jnp.where(yes, jnp.exp(logits - jnp.max(logits, -1, keepdims=True)), 0.0)
        gate_o[...] = up / jnp.sum(up, -1, keepdims=True)

    given = (*sums, *tables, tokens, gain_two, router, chosen)
    whole = [pl.BlockSpec(memory_space=pltpu.VMEM)] * len(given)
    return pl.pallas_call(
        body,
        in_specs=[pl.BlockSpec(memory_space=pltpu.SMEM)] + whole + [ANY] * n_out,
        out_shape=[
            like(length, total),
            like(length, fq),
            like(length, width, dtype=F32),
            like(length, width),
            like(length, router.shape[0], dtype=F32),
        ],
        scratch_shapes=[
            pltpu.VMEM((fq, width), BF),
            pltpu.SemaphoreType.DMA((n_out,)),
        ],
        compiler_params=BIG,
        cost_estimate=cost(
            2 * length * fq * width + 4 * heads * length * length * 128,
            2 * fq * width + 12 * length * total,
            heads * length * length,
        ),
        name="attend",
    )(spots, *given, *out_parts)


def second_norm_back(sums, gates, router, mid, gain_two, cotangent, normed, experts):
    length, width = mid.shape
    tail = router.shape[0]

    def body(a, b, c, gate_r, rt, mid_r, gain, cot, norm, mid_o, out_o):
        ends = wide(a[:, width:]) + wide(b[:, width:]) + wide(c[:, width:])
        grad = ends + pltpu.roll(ends, tail // 2, 1)
        gate = gate_r[...]
        chosen = gate * (grad - jnp.sum(gate * grad, -1, keepdims=True))
        logit = narrow(chosen)
        n2g = wide(a[:, :width]) + wide(b[:, :width]) + wide(c[:, :width]) + mm(logit, rt[...])
        m = mid_r[...]
        inverse = lax.rsqrt(jnp.mean(m * m, -1, keepdims=True) + norm_eps)
        scaled = m * inverse
        du = n2g * gain[...]
        out = wide(cot[...]) + inverse * (
            du - scaled * jnp.mean(du * scaled, -1, keepdims=True)
        )
        mid_o[...] = out
        out_o[:length] = narrow(out)
        out_o[length : length + experts] = narrow(mm_tn(logit, norm[...])[:experts])
        gain_row = jnp.sum(n2g * scaled, 0, keepdims=True)
        out_o[length + experts :] = narrow(jnp.broadcast_to(gain_row, (16, width)))

    return pl.pallas_call(
        body,
        out_shape=[like(length, width, dtype=F32), like(length + experts + 16, width)],
        compiler_params=BIG,
        cost_estimate=cost(6 * length * width * tail, 20 * length * width),
        name="second_norm_back",
    )(*sums, gates, router, mid, gain_two, cotangent, normed)


def attend_back(qkv, tables, branch, out_parts, spots, base, heads, kv_heads):
    length, width = tables[0].shape[0], branch.shape[1]
    group = heads // kv_heads
    fq, fk = heads * HEAD, kv_heads * HEAD
    total = fq + 2 * fk
    n_out = len(out_parts)

    def body(spots, qkv_r, cosine, sine, allowed, live, br, *refs):
        outs = refs[:n_out]
        grads, w_out, sems = refs[n_out:]
        copies = load_parts(outs, spots, base, w_out, sems)
        for copy in copies:
            copy.start()
        cos, sin = cosine[...], -sine[...]
        low = lax.broadcasted_iota(jnp.int32, (length, 128), 1) < HEAD
        ok = jnp.concatenate([allowed[...] > 0] * group)
        zero = jnp.zeros((length, 128), BF)
        q = [qkv_r[:, j * 128 : j * 128 + 128] for j in range(fq // 128)]
        keys, values = [], []
        for store, left in ((keys, fq), (values, fq + fk)):
            for j in range(fk // 128):
                v = wide(qkv_r[:, left + j * 128 : left + j * 128 + 128])
                store += [narrow(twice(v, False)), narrow(twice(v, True))]
        for copy in copies:
            copy.wait()
        cg = narrow(jnp.where(column(live[...]) > 0, mm_nt(br[:length], w_out[...]), 0.0))
        done, fold = {}, {}

        def put(at, v, rotate):
            v = turn(v, cos, sin) if rotate else v
            grads[:, at * 128 : at * 128 + 128] = narrow(v)

        for g in range(kv_heads):
            hs = range(g * group, (g + 1) * group)
            pick = lambda src: jnp.concatenate(
                [jnp.where(low != bool(h % 2), src(h // 2), zero) for h in hs]
            )
            q3 = pick(lambda j: q[j])
            c3 = pick(lambda j: cg[:, j * 128 : j * 128 + 128])
            a = softmax_rows(q3, keys[g], ok)
            ag = mm_nt(c3, values[g])
            sg = narrow(a * (ag - jnp.sum(a * ag, -1, keepdims=True)))
            vg = mm_tn(narrow(a), c3)
            kg = score_scale * mm_tn(sg, q3)
            qg = score_scale * mm(sg, keys[g])
            fold[g] = (kg + pltpu.roll(kg, HEAD, 1), vg + pltpu.roll(vg, HEAD, 1))
            for n, h in enumerate(hs):
                done[h] = qg[n * length : (n + 1) * length]
                if h % 2:
                    put(h // 2, jnp.where(low, done.pop(h - 1), done.pop(h)), True)
            if g % 2:
                (ka, va), (kb, vb) = fold.pop(g - 1), fold.pop(g)
                put(fq // 128 + g // 2, jnp.where(low, ka, kb), True)
                put((fq + fk) // 128 + g // 2, jnp.where(low, va, vb), False)

    vm = pl.BlockSpec(memory_space=pltpu.VMEM)
    return pl.pallas_call(
        body,
        in_specs=[pl.BlockSpec(memory_space=pltpu.SMEM)] + [vm] * 6 + [ANY] * n_out,
        out_shape=like(length, total),
        scratch_shapes=[pltpu.VMEM((fq, width), BF), pltpu.SemaphoreType.DMA((n_out,))],
        compiler_params=BIG,
        cost_estimate=cost(
            2 * length * fq * width + 12 * heads * length * length * 128,
            2 * fq * width + 8 * length * total,
            heads * length * length,
        ),
        name="attend_back",
    )(spots, qkv, *tables, branch, *out_parts)


def ring_columns(v, at, base, n, scratch, out):
    per = v.shape[1] // n
    scratch[...] = wide(v).T
    for i in range(n):
        block = scratch[pl.ds(pl.multiple_of(at[base + i] * per, 8), per)]
        out[i * per : (i + 1) * per] = narrow(block)


def out_gradient(attended, branches, total, spots, base, n):
    length, dh = attended[0].shape
    width = branches[0].shape[1]
    tile = 512

    def body(at, aa, ab, ba, bb, own, sib, scratch, lhs):
        @pl.when(pl.program_id(0) == 0)
        def _():
            ring_columns(jnp.concatenate([aa[...], ab[...]]), at, base, n, scratch, lhs)

        d = narrow(mm(lhs[...], jnp.concatenate([ba[...], bb[...]])))
        own[...], sib[...] = d[: dh // 2], d[dh // 2 :]

    whole = pl.BlockSpec((length, dh), lambda i, at: (0, 0))
    return pl.pallas_call(
        body,
        grid_spec=pltpu.PrefetchScalarGridSpec(
            num_scalar_prefetch=1,
            grid=(width // tile,),
            in_specs=[whole, whole] + [pl.BlockSpec((length, tile), lambda i, at: (0, i))] * 2,
            out_specs=[pl.BlockSpec((dh // 2, tile), lambda i, at: (0, i))] * 2,
            scratch_shapes=[
                pltpu.VMEM((dh, 2 * length), F32), pltpu.VMEM((dh, 2 * length), BF),
            ],
        ),
        out_shape=[like(dh // 2, total)] * 2,
        compiler_params=BIG,
        cost_estimate=cost(4 * length * dh * width, 2 * dh * width),
        name="out_gradient",
    )(spots, *attended, *branches)


def projection_gradient(
    grads, low, normed, cols, inverses, small, begun, skip, spots, base, side, n, experts
):
    length, total = grads[0].shape
    dh = low.shape[0]
    tile = 512
    steps, last = total // tile, experts + 16

    def body(at, ga, gb, w, na, nb, ca, cb, ia, ib, sa, sb, _0, _1, own, sib, n1a, n1b, scratch, lhs, acc, tiny):
        i = pl.program_id(0)

        @pl.when(i == 0)
        def _():
            ring_columns(jnp.concatenate([na[...], nb[...]]), at, base, n, scratch, lhs)
            acc[...] = jnp.zeros_like(acc)

        @pl.when(i < steps)
        def _():
            g = jnp.concatenate([ga[...], gb[...]])
            d = narrow(mm(lhs[...], g))
            own[...], sib[...] = d[: dh // 2], d[dh // 2 :]
            acc[...] += mm_nt(g, w[...])

        @pl.when(i == steps)
        def _():
            n1 = acc[...]
            n1a[...], n1b[...] = n1[:length], narrow(n1[length:])
            gain = n1[:length] * (wide(ca[...]) * column(ia[...])) + n1[length:] * (
                wide(cb[...]) * column(ib[...])
            )
            tiny[...] = jnp.zeros_like(tiny)
            tiny[:last] = wide(sa[...]) + wide(sb[...])
            row = jnp.sum(gain, 0, keepdims=True)
            tiny[experts + 8 : last] = jnp.broadcast_to(row, (8, dh))
            ring_columns(tiny[...], at, base, n, scratch.at[:, :128], lhs.at[:, :128])
            own[:, :128], sib[:, :128] = lhs[: dh // 2, :128], lhs[dh // 2 :, :128]

    whole = lambda a: pl.BlockSpec(a.shape, lambda i, at: (0, 0))
    strip = lambda a: pl.BlockSpec(
        (a.shape[0], tile), lambda i, at: (0, jnp.minimum(i, steps - 1))
    )
    out = pl.BlockSpec((dh // 2, tile), lambda i, at: (0, skip // tile + i))
    shapes = [like(*begun[0].shape)] * 2 + [like(length, dh, dtype=F32), like(length, dh)]
    return pl.pallas_call(
        body,
        grid_spec=pltpu.PrefetchScalarGridSpec(
            num_scalar_prefetch=1,
            grid=(steps + 1,),
            in_specs=[strip(grads[0]), strip(grads[1]), strip(low)]
            + [whole(v) for v in (*normed, *cols, *inverses)]
            + [pl.BlockSpec((last, dh), lambda i, at: (length // last, at[side]))] * 2
            + [ANY, ANY],
            out_specs=[out, out, whole(shapes[2]), whole(shapes[3])],
            scratch_shapes=[
                pltpu.VMEM((dh, 2 * length), F32),
                pltpu.VMEM((dh, 2 * length), BF),
                pltpu.VMEM((2 * length, dh), F32),
                pltpu.VMEM((128, dh), F32),
            ],
        ),
        out_shape=shapes,
        input_output_aliases={12: 0, 13: 1},
        compiler_params=BIG,
        cost_estimate=cost(8 * length * dh * total, 4 * dh * total),
        name="projection_gradient",
    )(spots, *grads, low, *normed, *cols, *inverses, *small, *begun)


def put_rows(pieces, spots, seats, per, widths, rows, kept=None, small=None):
    k = len(widths)
    cuts = [sum(widths[:i]) for i in range(k + 1)]
    given = list(kept or ())
    closing = small is not None
    plain = k - 1 if closing else k
    flat = [(p, i, at) for p, places in enumerate(seats) for i, at in enumerate(places)]
    n, m = len(flat), len(pieces)

    def body(at_ref, *refs):
        src, refs = refs[:m], refs[m:]
        before, refs = refs[: len(given)], refs[len(given) :]
        outs, refs = refs[:plain], refs[plain:]
        if closing:
            router, moe, attn, refs = *refs[:3], refs[3:]
            table, sem, refs = *refs[:2], refs[2:]
            fetch = pltpu.make_async_copy(before[-1], table, sem)
            fetch.start()
        held, sems = refs[:plain], refs[plain]
        copies = []
        for j, (p, i, at) in enumerate(flat):
            row = pl.multiple_of(at_ref[at] * per, 8)
            for w in range(plain):
                held[w][j * per : (j + 1) * per] = wide(
                    src[p][i * per : (i + 1) * per, cuts[w] : cuts[w + 1]]
                )
                copy = pltpu.make_async_copy(
                    held[w].at[pl.ds(j * per, per)], outs[w].at[pl.ds(row, per)], sems.at[j, w]
                )
                copy.start()
                copies.append(copy)
        if closing:
            fetch.wait()
            for p, i, at in flat:
                row = pl.multiple_of(at_ref[at] * per, 8)
                table[pl.ds(row, per)] = wide(src[p][i * per : (i + 1) * per, cuts[plain] :])
            across = table[...].T
            router[...] = across[:small]
            moe[...], attn[...] = across[small], across[small + 8]
        for copy in copies:
            copy.wait()

    vm = pl.BlockSpec(memory_space=pltpu.VMEM)
    out_specs = [ANY] * plain
    out_shape = [like(rows, w, dtype=F32) for w in widths[:plain]]
    scratch = [pltpu.VMEM((n * per, w), F32) for w in widths[:plain]]
    scratch += [pltpu.SemaphoreType.DMA((n, plain))]
    if closing:
        out_specs += [vm] * 3
        out_shape += [like(small, rows, dtype=F32)] + [like(rows, dtype=F32)] * 2
        scratch = [pltpu.VMEM((rows, widths[-1]), F32), pltpu.SemaphoreType.DMA] + scratch
    return pl.pallas_call(
        body,
        in_specs=[pl.BlockSpec(memory_space=pltpu.SMEM)] + [vm] * m + [ANY] * len(given),
        out_specs=out_specs,
        out_shape=out_shape,
        input_output_aliases={1 + m + i: i for i in range(plain if given else 0)},
        scratch_shapes=scratch,
        compiler_params=BIG,
        cost_estimate=cost(n * per * cuts[-1], n * per * cuts[-1] * 6),
        name="put_rows",
    )(spots, *pieces, *given)


def expert_step(spots, base, tiles, cots, router, gate, up, down, starts, kept, start, total, apart):
    width, ffe = cots.shape[1] - router.shape[0], gate[0].shape[1]
    tail = router.shape[0]
    count = len(tiles)
    two = sum(p.shape[0] for p in tiles[0])
    block = two // 2
    n = count * block
    pieces = [p for t in tiles for p in t]
    parts = [*gate, *up, *down]
    sets, m = [len(gate), len(up), len(down)], len(pieces)
    k = sum(sets)

    def body(spot, ca, cb, rt, *refs):
        xs, ws = refs[:m], refs[m : m + k]
        products = refs[-10 - n_out : -10]
        x_o, hid_o, pre_o, rg_o = refs[-10:-6]
        held, gw, uw, dw, sems, wsems = refs[-6:]
        i = pl.program_id(0)
        moves, at, j = [], 0, 0
        for t in tiles:
            group = []
            for p in t:
                dst = held.at[pl.ds(at, p.shape[0])]
                group.append(pltpu.make_async_copy(xs[j], dst, sems.at[j]))
                at, j = at + p.shape[0], j + 1
            moves.append(group)
        loads = []
        first = 0
        for size, whole in zip(sets, (gw, uw, dw)):
            part = slice(first, first + size)
            loads += load_parts(ws[part], spot, starts + first, whole, wsems.at[pl.ds(first, size)])
            first += size

        @pl.when(i == 0)
        def _():
            for copy in [*moves[0], *loads]:
                copy.start()
            for copy in [c for g in moves[1:] for c in g]:
                copy.start()

        for t in range(count):

            @pl.when(i == t)
            def _():
                for copy in moves[t]:
                    copy.wait()

        @pl.when(i == 0)
        def _():
            for copy in loads[: sets[0] + sets[1]]:
                copy.wait()

        x = held[pl.ds(pl.multiple_of(i * two, two), two)]
        cm = jnp.concatenate([ca[...], cb[...]])
        cot, chosen = cm[:, :width], cm[:, width:] > 0
        x_o[...] = x
        logits = jnp.where(chosen, mm_nt(x, rt[...]), mask_fill)
        top = jnp.max(logits, -1, keepdims=True)
        raised = jnp.where(chosen, jnp.exp(logits - top), 0.0)
        mine = lax.broadcasted_iota(jnp.int32, raised.shape, 1)
        weight = jnp.sum(jnp.where(mine == spot[0], raised, 0.0), -1, keepdims=True)
        weight = narrow(weight / jnp.sum(raised, -1, keepdims=True))
        gate_pre, up_pre = mm(x, gw[...]), mm(x, uw[...])
        sg = jax.nn.sigmoid(gate_pre)
        silu = gate_pre * sg
        hidden = narrow(silu * up_pre)
        hid_o[...] = hidden
        result_grad = weight * cot

        @pl.when(i == 0)
        def _():
            for copy in loads[sets[0] + sets[1] :]:
                copy.wait()

        rg_o[...] = result_grad
        result = narrow(mm(hidden, dw[...]))
        mix = weight * result
        gate_grad = jnp.sum(wide(result) * wide(cot), -1, keepdims=True)
        hidden_grad = mm_nt(result_grad, dw[...])
        gpg = narrow(hidden_grad * up_pre * sg * (1.0 + gate_pre * (1.0 - sg)))
        upg = narrow(hidden_grad * silu)
        pre_o[:, :ffe], pre_o[:, ffe:] = gpg, upg
        row = narrow(mm_nt(gpg, gw[...]) + mm_nt(upg, uw[...]))
        high = wide(narrow(gate_grad))
        ends = jnp.where(mine == spot[0], high, 0.0)
        ends = narrow(jnp.where(mine == spot[0] + tail // 2, gate_grad - high, ends))

        def store(mix_a, mix_b, row_a, row_b):
            mix_a[...], mix_b[...] = mix[:block], mix[block:]
            row_a[:, :width], row_b[:, :width] = row[:block], row[block:]
            row_a[:, width:], row_b[:, width:] = ends[:block], ends[block:]

        if apart:
            pl.when(i == 0)(lambda: store(*products[:4]))
            pl.when(i > 0)(lambda: store(*products[4:]))
        else:
            store(*products)

    gap = 1 if apart else 0
    step = lambda w: pl.BlockSpec((block, w), lambda i, s: (jnp.maximum(i - gap, 0), 0))
    once = lambda w: pl.BlockSpec((block, w), lambda i, s: (0, 0))
    four = (width, width, width + tail, width + tail)
    keep = lambda w: pl.BlockSpec((two, w), lambda i, s: (start + i, 0))
    widths = [width, ffe, 2 * ffe, width]
    out_shape = [like(block, w) for w in four] if apart else []
    out_shape += [like(n - gap * block, w) for w in four]
    out_shape += [like(total, w) for w in widths]
    given = list(kept or ())
    before, n_out = 4 + m + k, 8 if apart else 4
    return pl.pallas_call(
        body,
        grid_spec=pltpu.PrefetchScalarGridSpec(
            num_scalar_prefetch=1,
            grid=(count,),
            in_specs=[
                pl.BlockSpec((block, width + tail), lambda i, s: (s[base + i], 0)),
                pl.BlockSpec((block, width + tail), lambda i, s: (s[base + count + i], 0)),
                pl.BlockSpec(router.shape, lambda i, s: (0, 0)),
            ]
            + [ANY] * (m + k + len(given)),
            out_specs=[once(w) for w in (four if apart else ())]
            + [step(w) for w in four]
            + [keep(w) for w in widths],
            scratch_shapes=[
                pltpu.VMEM((count * two, width), BF),
                pltpu.VMEM((width, ffe), BF),
                pltpu.VMEM((width, ffe), BF),
                pltpu.VMEM((ffe, width), BF),
                pltpu.SemaphoreType.DMA((m,)),
                pltpu.SemaphoreType.DMA((k,)),
            ],
        ),
        out_shape=out_shape,
        input_output_aliases={before + i: n_out + i for i in range(len(given))},
        compiler_params=BIG,
        cost_estimate=cost(
            24 * n * width * ffe, 6 * width * ffe + n * width * 28, 2 * n * ffe
        ),
        name="expert_step",
    )(spots, cots, cots, router, *pieces, *parts, *given)


class Links:
    def __init__(self):
        self.n = lax.axis_size("dp")
        self.e = lax.axis_size("expert")
        self.chips = self.e // 2
        order = list(range(self.chips))
        if self.n == 2 and self.chips == 8:
            order = [0, 2, 4, 6, 7, 5, 3, 1]
        self.order = order
        self.x = lax.axis_index("dp")
        self.me = lax.axis_index("expert")

    def table(self, of):
        rows, begins = [], {}
        for x in range(self.n):
            for me in range(self.e):
                lists, row = of(x, me, self.order.index(me // 2)), []
                for name, values in lists.items():
                    begins[name] = len(row)
                    row += values
                rows.append(row)
        at = self.x * self.e + self.me
        whole = jnp.asarray(np.array(rows, np.int32))
        return lax.dynamic_slice_in_dim(whole, at, 1, 0).reshape(-1), begins

    def sibling(self, v):
        return lax.ppermute(v, "expert", [(i, i ^ 1) for i in range(self.e)])

    def flip(self, v, bit):
        return lax.ppermute(v, "expert", [(i, i ^ bit) for i in range(self.e)])

    def ring(self, v, step):
        c, o = self.chips, self.order
        pairs = [(o[k] * 2 + l, o[(k + step) % c] * 2 + l) for k in range(c) for l in (0, 1)]
        return lax.ppermute(v, "expert", pairs)

    def gather(self, block, waits=()):
        c = self.chips
        half = block.shape[0] // 2
        got = {0: block}
        up = down = block
        for s in range(1, c // 2):
            up, down = level(up, down, *(waits[s] if s < len(waits) else ()))
            up, down = self.ring(up, 1), self.ring(down, -1)
            got[c - s], got[s] = up, down
        up, down = level(up, down)
        far = (self.ring(up[:half], 1), self.ring(down[half:], -1))
        return got, far

    def scatter(self, s, far, waits=(), steps=None):
        c = self.chips
        half = far[0].shape[0]
        up, down = self.ring(far[0], 1), self.ring(far[1], -1)
        steps = [] if steps is None else steps
        steps.append((up, down))
        r = c // 2 - 1
        a, b = s(r, None), s(c - r, None)
        up = jnp.concatenate([add_low(up, a[:half]), a[half:]])
        down = jnp.concatenate([b[:half], add_low(down, b[half:])])
        for r in range(c // 2 - 2, -1, -1):
            up, down = level(up, down, *(waits(len(steps)) if waits else ()))
            up, down = self.ring(up, 1), self.ring(down, -1)
            steps.append((up, down))
            if r:
                last = steps[-2]
                up, down = add_low(up, s(r, last)), add_low(down, s(c - r, last))
        return (s(0, up), up, down), steps

    def swap(self, v):
        return lax.ppermute(v, "dp", [(0, 1), (1, 0)])

    def pick(self, v, other, axis):
        size = v.shape[axis] // self.n
        at = (1 - self.x if other else self.x) * size
        return lax.dynamic_slice_in_dim(v, at, size, axis)

    def both(self, own, got, axis):
        return jnp.where(
            self.x == 0,
            jnp.concatenate([own, got], axis),
            jnp.concatenate([got, own], axis),
        )

    def columns(self, v):
        if self.n == 2:
            return jnp.concatenate([self.pick(v, False, 1), self.swap(self.pick(v, True, 1))])
        return lax.all_to_all(v, "dp", split_axis=1, concat_axis=0, tiled=True)

    def columns_back(self, v):
        if self.n == 2:
            t = v.shape[0] // 2
            return self.both(v[:t], wide(self.swap(narrow(v[t:]))), 1)
        return wide(lax.all_to_all(narrow(v), "dp", split_axis=0, concat_axis=1, tiled=True))

    def rows(self, v):
        if self.n == 2:
            return jnp.concatenate([v, self.swap(v)])
        return lax.all_gather(v, "dp", axis=0, tiled=True)

    def sum_back(self, v):
        if self.n == 2:
            t = v.shape[0] // 2
            return v[:t] + wide(self.swap(narrow(v[t:])))
        return wide(lax.psum_scatter(narrow(v), "dp", scatter_dimension=0, tiled=True))

    def whole(self, v, axis):
        if self.n == 2:
            return self.both(v, self.swap(v), axis)
        return lax.all_gather(v, "dp", axis=axis, tiled=True)

    def shard_sum(self, v, axis):
        return wide(lax.psum_scatter(narrow(v), "dp", scatter_dimension=axis, tiled=True))

    def parts(self, w):
        if self.n == 2:
            return [w, self.swap(w)]
        return [lax.all_gather(w, "dp", axis=0, tiled=True)]

    def parts_by_four(self, w, after):
        if self.n != 2:
            return self.parts(narrow(w))
        part = w.shape[0] // 4
        a = self.swap(narrow(lax.dynamic_slice_in_dim(w, self.me % 4 * part, part, 0)))
        w, a = narrow(tie(w, after)), tie(a, after)
        b = self.flip(a, 2)
        return [w, a, b, self.flip(a, 1), self.flip(b, 1)]


def wide_sum(v):
    out = wide(v[0])
    for w in v[1:]:
        out = out + wide(w)
    return out


def shards(
    tokens, cotangent, lengths, routes, gain_attn, w_query, key_weight, value_weight,
    w_out, gain_moe, w_router, w_gate, w_up, w_down,
):
    net = Links()
    c, pair = net.chips, net.n == 2
    length, width = tokens.shape
    dh = gain_attn.shape[0]
    heads, kv_heads = w_query.shape[1] // HEAD, key_weight.shape[1] // HEAD
    fq, fk = w_query.shape[1], key_weight.shape[1]
    experts = w_router.shape[1]
    tail = 128
    far, half = c // 2, length // 2

    if pair:
        away = net.pick(tokens, True, 1)
        stream = wide(tie(tokens, away))
    else:
        stream = wide(tokens)
    inv_one = lax.rsqrt(jnp.mean(stream * stream, -1, keepdims=True) + norm_eps)
    if pair:
        cols = (net.pick(tokens, False, 1), net.swap(away))
        inv_row = inv_one.reshape(1, length)
        inverses = (inv_row, net.swap(inv_row))
        weights = (w_query, key_weight, value_weight)
        other, normed_other = project_columns(cols[1], inverses[1], gain_attn[None], weights, BF)
        arrived = net.swap(other)
        own, normed_own = project_columns(
            tie(cols[0], other), inverses[0], gain_attn[None], weights, F32
        )
        normed_cols = (normed_own, normed_other)
        sums = (own, arrived)
        w_qkv = jnp.concatenate(
            [narrow(tie(w, own)) for w in (w_query, key_weight, value_weight)], 1
        )
    else:
        scaled_cols = wide(net.columns(tokens)) * net.rows(inv_one.reshape(1, length)).reshape(-1, 1)
        normed_cols = narrow(scaled_cols * wide(narrow(gain_attn))[None, :])
        w_qkv = jnp.concatenate([narrow(w_query), narrow(key_weight), narrow(value_weight)], 1)
        arrived = net.sum_back(mm(normed_cols, w_qkv))
        sums, own, other = (arrived,), arrived, arrived

    near = [0] + [r for s in range(1, far - 1) for r in (s, c - s)]
    last = [far, far - 1, c - far + 1]
    ffe = w_down.shape[1]

    def numbers(x, me, place):
        at = lambda r, l: net.order[(place + r) % c] * 2 + (me % 2 ^ l)
        seat = lambda r, l: (place + r) % c * 2 + (me % 2 ^ l)
        y, q, part = 1 - x, me % 4, dh // 4
        return {
            "me": [me],
            "x": [x],
            "near": [at(r, l) for l in (0, 1) for r in near],
            "last": [at(r, l) for l in (0, 1) for r in last],
            "expert": [x * dh, y * dh, y * dh + dh // 2, x * dh, y * dh, x * ffe, y * ffe]
            if pair
            else [0, 0, 0],
            "out": [x * dh] + [y * dh + (q ^ z) * part for z in (0, 2, 1, 3)] if pair else [0],
            "seats": [seat(r, l) for l in (0, 1) for r in range(c)],
        }

    spots, begins = net.table(numbers)
    small = jnp.concatenate(
        [narrow(tie(w_router, inv_one)).T, narrow(gain_attn)[None], narrow(gain_moe)[None]], 0
    )
    small = net.whole(small, 1)
    gain_one, gain_two = wide(small[experts])[None], wide(small[experts + 1])[None]
    router = jnp.pad(small[:experts], ((0, tail - experts), (0, 0)))
    out_parts = net.parts_by_four(tie(w_out, inv_one), other)
    hits = routes[:, :, None] == jnp.arange(tail, dtype=jnp.int32)[None, None, :]
    chosen = narrow(jnp.any(hits, 1))
    cot_all = lax.all_gather(
        jnp.concatenate([tie(cotangent, inv_one), chosen], 1), "expert", axis=0, tiled=True
    )
    if pair:
        low = narrow(tie(w_gate, inv_one)[0])
        gate_parts = [low, net.swap(low[: dh // 2]), net.swap(tie(low[dh // 2 :], out_parts[2]))]
        up_parts, down_parts = (
            net.parts(tie(narrow(tie(w, own)[0]), out_parts[2])) for w in (w_up, w_down)
        )
        hold = (w_qkv, gate_parts[1])
        waits = ((), (), gate_parts[2:], up_parts[1:])
    else:
        gate_parts, up_parts, down_parts = (net.parts(narrow(w[0])) for w in (w_gate, w_up, w_down))
        hold, waits = (w_qkv,), ()

    places, live, allowed = layout(lengths[0], length)
    inner = jnp.arange(128, dtype=jnp.int32) % (HEAD // 2)
    angles = places.astype(F32)[:, None] * (rope_base ** (-inner.astype(F32) * 2.0 / HEAD))[None]
    sign = jnp.where(jnp.arange(128) % HEAD < HEAD // 2, -1.0, 1.0)[None]
    tables = (
        jnp.cos(angles), jnp.sin(angles) * sign, allowed.astype(F32), live.astype(F32)[None],
    )
    qkv, attended, mid, normed_two, gates = attend(
        sums, tables, tie(tokens, *hold), gain_two, router, chosen, out_parts, spots,
        begins["out"], heads, kv_heads,
    )

    got, ends = net.gather(normed_two, waits)
    beside = {r: net.sibling(v) for r, v in got.items()}
    kept, start, made = None, 0, []
    for g, name in ((near, "near"), (last, "last")):
        if made:
            ends = tuple(tie(v, made[0][0]) for v in ends)
            ends_beside = tuple(net.sibling(v) for v in ends)
        tiles = [(*ends, *ends_beside) if r == far else (got[r], beside[r]) for r in g]
        out = expert_step(
            spots, begins[name], tiles, cot_all, router, gate_parts, up_parts, down_parts,
            begins["expert"], kept, start, net.e * length, far in g,
        )
        kept, start = out[-4:], start + len(g)
        made += [out[i : i + 4] for i in range(0, len(out) - 4, 4)]
    after_near = made[0][0]

    sums = {0: {}, 2: {}}

    def ring_sum(which, after, waits=(), steps=None):
        (a0, b0), (a2, b2), (a1, b1) = (m[which : which + 2] for m in made)
        edge = add_low(a2, net.sibling(tie(b2, *after)))
        b1 = net.sibling(b1)
        done = sums[which]

        def block(r, then):
            group, at = (near, 0) if r in near else (last[1:], 1)
            if at not in done:
                done[at] = add_low(a1, b1) if at else add_low(a0, net.sibling(tie(b0, *then)))
            i = group.index(r)
            return done[at][i * length : (i + 1) * length]

        return net.scatter(block, (edge[:half], edge[half:]), waits, steps)

    rows_all, hid_all, pre_all, rg_all = kept
    ffe = w_gate.shape[2]
    if pair:
        part = net.swap(tie(net.pick(attended, True, 1), after_near))
        halves = lambda v: (net.pick(v, False, 0), narrow(net.pick(v, True, 0)))
        back, steps = ring_sum(2, ())
    else:
        back, steps = ring_sum(2, ())

    mid_grad, branch = second_norm_back(
        back, gates, router, mid, gain_two, cotangent, normed_two, experts
    )

    mixed, mix_steps = ring_sum(0, ())
    mix_parts = mixed

    base = begins["seats"]
    seats = spots[base : base + net.e]
    per = dh // net.e
    if not pair:
        slot = jnp.arange(dh, dtype=jnp.int32)
        source = jnp.sum(
            jnp.where(slot[:, None] // per == jnp.arange(net.e)[None, :], seats[None, :], 0), 1
        ) * per + slot % per
        perm = (slot[:, None] == source[None, :]).astype(BF)

    def all_sum(own, sib, widths, small, ready, last_mix):
        at = slice(far * per, (far + 1) * per)
        edge = add_low(own[at], net.sibling(sib[at]))
        s = []

        def block(r, after):
            if not s:
                s.append(add_low(own, net.sibling(sib)))
            return s[0][r * per : (r + 1) * per]

        cut = per // 2
        total, steps = net.scatter(
            block, (edge[:cut], edge[cut:]), lambda k: last_mix if k == 1 else ()
        )
        ready = ready(steps[0])
        up = down = held = narrow(wide_sum(total))
        seat = lambda rs: [[base + l * c + r for r in rs] for l in (0, 1)]
        pieces, kept = [], ()

        def put(pieces, kept):
            both = [v for p in pieces for v in p[:2]]
            return put_rows(both, spots, [v for p in pieces for v in p[2]], per, widths, dh, kept)

        for s in range(far):
            if s:
                before = [p[1] for p in pieces[max(s - 2, 0) : s - 1]]
                up, down = level(up, down, *before, *jax.tree.leaves(ready[s : s + 1]))
            rs = [s, c - s] if s else [0]
            pieces.append((held, net.sibling(held), seat(rs)))
            if s < far - 1:
                up, down = net.ring(up, 1), net.ring(down, -1)
                held = jnp.concatenate([down, up])
            else:
                up, down = net.ring(up[:cut], 1), net.ring(down[cut:], -1)
        if per % 16 == 0:
            kept = put(pieces, None)
            up, down = level(up, down, kept[0], *jax.tree.leaves(ready[far:]))
        held = jnp.concatenate([up, down])
        pieces.append((held, net.sibling(held), seat([far])))
        if per % 16 == 0:
            return put_rows(pieces[-1][:2], spots, seat([far]), per, widths, dh, kept, small)
        out = jnp.zeros((dh, sum(widths)), F32)
        for a, b, seats in pieces:
            for v, ats in zip((a, b), seats):
                for i, at in enumerate(ats):
                    blk = wide(v[i * per : (i + 1) * per])
                    out = lax.dynamic_update_slice_in_dim(out, blk, spots[at] * per, 0)
        cuts = [sum(widths[:i]) for i in range(len(widths) + 1)]
        out = [out[:, a:b] for a, b in zip(cuts, cuts[1:])]
        return [*out[:-1], out[-1][:, :small].T, out[-1][:, small], out[-1][:, small + 8]]

    part_width = width + fq + 2 * fk + tail
    beyond = net.swap(branch) if pair else None

    grads = attend_back(
        qkv, tables, tie(branch, *mix_steps[0]), out_parts, spots, begins["out"], heads, kv_heads
    )
    sent = grads
    if pair:
        sent = tie(net.swap(tie(grads, beyond, part, *mix_steps[1])), *mix_steps[2])
        begun = out_gradient(
            (net.pick(attended, False, 1), part), (branch, tie(beyond, *mix_steps[1])), part_width,
            spots, base, net.e,
        )
        own, sib, n1, n1_other = projection_gradient(
            (grads, sent), w_qkv, normed_cols, cols, inverses, (branch, beyond), begun, width, spots,
            base, begins["x"], net.e, experts,
        )
        n1_other = net.swap(n1_other)
        n1g = net.both(n1, wide(n1_other), 1)
    else:
        grads_all = net.rows(grads)
        d_out = mm_tn(narrow(mm(net.columns(attended), perm)), net.rows(branch[:length]))
        d_qkv = mm_tn(narrow(mm(normed_cols, perm)), grads_all)
        n1 = mm_nt(grads_all, w_qkv)
        n1g = net.columns_back(n1)
        d_small = net.shard_sum(wide(branch[length:]), 1)
        d_gain = jnp.broadcast_to(jnp.sum(n1 * scaled_cols, 0)[None], (8, dh))
        d_small = jnp.concatenate([d_small[: experts + 8], d_gain], 0)
        d_small = jnp.pad(mm(narrow(d_small), perm).T, ((0, 0), (0, tail - experts - 16)))
        d = narrow(jnp.concatenate([d_out, d_qkv, d_small], 1))
        own, sib = d[: dh // 2], d[dh // 2 :]
    scaled_one = stream * inv_one
    du = n1g * gain_one
    d_tokens = mid_grad + inv_one * (
        du - scaled_one * jnp.mean(du * scaled_one, -1, keepdims=True)
    )
    if pair:
        last_mix, grown = mix_steps[3], []

        def ready(arrived):
            d_pre = halves(mm_tn(tie(rows_all, *arrived), pre_all))
            d_down = halves(mm_tn(tie(hid_all, *arrived), rg_all))
            got = [net.swap(tie(v[1], n1_other)) for v in (d_down, d_pre)]
            gate, up = (d_pre[0][:, a] + wide(got[1][:, a]) for a in (slice(ffe), slice(ffe, None)))
            late = (mix_parts[0], *(tie(v, *arrived) for v in mix_parts[1:]))
            grown.extend((d_down[0] + wide(got[0]), gate, up, narrow(mid + wide_sum(late))))
            return (), (), (d_tokens,), grown[3:], grown[:3]

    else:
        d_down, d_pre = (
            net.shard_sum(mm_tn(a, b), 0)[None] for a, b in ((hid_all, rg_all), (rows_all, pre_all))
        )
        ready, last_mix, grown = (lambda _: ()), (), ()
    d_out, d_query, d_key, d_value, d_router, d_moe, d_attn = all_sum(
        own, sib, [width, fq, fk, fk, tail], experts, ready, last_mix
    )
    if not pair:
        grown = d_down[0], d_pre[0, :, :ffe], d_pre[0, :, ffe:], narrow(mid + wide_sum(mix_parts))
    d_down, d_gate, d_up = (v[None] for v in grown[:3])
    return (
        grown[3],
        d_tokens,
        d_attn,
        d_query,
        d_key,
        d_value,
        d_out,
        d_moe,
        d_router.T,
        d_gate,
        d_up,
        d_down,
    )


def solution(mesh):
    rows = P(("dp", "expert"), None)
    flat, dense, routed = P("dp"), P("dp", None), P("expert", "dp", None)
    return jax.shard_map(
        shards,
        mesh=mesh,
        in_specs=(
            rows, rows, rows, rows, flat, dense, dense, dense, dense, flat, dense,
            routed, routed, routed,
        ),
        out_specs=(
            rows, rows, flat, dense, dense, dense, dense, flat, dense, routed, routed, routed,
        ),
        check_vma=False,
    )
```
